128 devices in a mesh: gx: 16 (over x, y), gy: 8 (over z, core).
Axes of the slice: x: 4, y: 4, z: 4, core: 2. Of those that a mesh axis runs over, the one named last changes fastest.
Arguments:
- features: bfloat16 [512, 256, 256], P('gx', 'gy'), may hold values from -6 to 6
- occupied: int32 [512, 256], P('gx', 'gy'), may hold values 0 or 1
- conv_weight: bfloat16 [9, 256, 256], replicated, may hold values from -0.125 to 0.125
- norm_gain: float32 [256], replicated, may hold values from 0.1 to 1.9
- w_qkv: bfloat16 [256, 768], replicated, may hold values from -1 to 1
- w_proj: bfloat16 [256, 256], replicated, may hold values from -0.375 to 0.375
- tile_dest: int32 [128, 8], P('gx', 'gy'), may hold values from 0 to 127, as said below
- cotangent: bfloat16 [512, 256, 256], P('gx', 'gy'), may hold values from -6 to 6
Outputs:
- block_output: bfloat16 [512, 256, 256], P('gx', 'gy')
- d_features: bfloat16 [512, 256, 256], P('gx', 'gy')
- w_qkv_grad: float32 [256, 768], replicated
The draws below stay inside these ranges and needn't reach their ends.
Inputs may be any that keep to these rules, and one draw needn't show every extreme that they name: Each column of tile_dest is a permutation of 0 to 127; an entry divided by 8 names the block along gx whose patches receive the tile. Every block sends at most 1 of its tiles to each block of its column (itself included), the counts to different blocks differ by at most one, and 1 is reached in every column.
All inputs are finite; a program needn't handle non-finite values. No bound on the sum of `occupied` on one device may be relied on, other than what follows from the above.
Results may differ from the reference program's by a relative error of at most 0.03.
The reference program's roundings to bfloat16 on the way count: a program that leaves them out, or rounds other values in their place, can miss the bound.
Values may be sent and summed in bfloat16 or wider, within the bound.
No kernel may reach another device: no remote copies, remote signals or barrier semaphores. Data moves between devices by JAX's collectives and lax.ppermute only.
A program may use at most 192 MiB of HBM per device.

```python
import math
import jax
import jax.numpy as jnp
from jax import lax

C = 256
HEADS = 16
PATCH = 1024
TILE = 128
HX = 32
HY = 32
TILES_DEV = 8
NX = 512
NY = 256
N_GX = 16
N_GY = 8


def draw_tile_dest(key, part):
    key = jax.random.fold_in(key, 5)
    group_size = N_GX
    per_device = TILES_DEV

    def one_column(column_key):
        keys_list = jax.random.split(column_key, 4)
        relabel = jax.random.permutation(keys_list[0], group_size).astype(jnp.int32)
        inverse = jnp.argsort(relabel).astype(jnp.int32)
        offset_order = jax.random.permutation(keys_list[1], group_size).astype(jnp.int32)
        offset_rank = jnp.argsort(offset_order).astype(jnp.int32)
        base_load = per_device // group_size
        extra_load = per_device % group_size
        load_counts = base_load + (offset_rank < extra_load).astype(jnp.int32)
        load_ends = jnp.cumsum(load_counts)
        tile_ids = jnp.arange(per_device, dtype=jnp.int32)
        offsets = jnp.sum((load_ends[None, :] <= tile_ids[:, None]).astype(jnp.int32), axis=1)
        source = jnp.arange(group_size, dtype=jnp.int32)
        destination = inverse[(relabel[source][:, None] + offsets[None, :]) % group_size]
        slot_order = jax.vmap(lambda sub_key: jax.random.permutation(sub_key, per_device).astype(jnp.int32))(jax.random.split(keys_list[2], group_size))
        slot_index = slot_order[destination, tile_ids[None, :]]
        slot_value = destination * per_device + slot_index
        shuffle = jax.vmap(lambda sub_key: jax.random.permutation(sub_key, per_device).astype(jnp.int32))(jax.random.split(keys_list[3], group_size))
        placed = jnp.zeros((group_size, per_device), jnp.int32).at[source[:, None], shuffle].set(slot_value)
        return placed.reshape(group_size * per_device)
    columns = jax.vmap(one_column)(jax.random.split(key, N_GY))
    return columns.T.astype(jnp.int32)


def draw_w_qkv(key, part):
    key = jax.random.fold_in(key, 9)
    keys_list = jax.random.split(key, 1)
    matrix = jax.random.normal(keys_list[0], (C, 3 * C), jnp.float32) / math.sqrt(C)
    matrix = jnp.clip(matrix, -1.0, 1.0)
    return matrix.astype(jnp.bfloat16)


def place_ends(values, own_key, least, top_value):
    shape = values.shape
    place = [jax.random.randint(jax.random.fold_in(own_key, axis), (), 0, shape[axis]) for axis in range(len(shape))]
    values = values.at[tuple(place)].set(least)
    longest = shape.index(max(shape))
    place[longest] = (place[longest] + 1) % shape[longest]
    return values.at[tuple(place)].set(top_value)


def shard_levels(key, shape, pieces, smallest, largest):
    def one(position, shards_of):
        heights = jax.random.uniform(jax.random.fold_in(jax.random.fold_in(key, 6), position), (shards_of,), jnp.float32, smallest / len(pieces), largest / len(pieces))
        return jnp.repeat(jnp.exp(heights), shape[position] // shards_of).reshape((-1,) + (1,) * (len(shape) - position - 1))

    gain = one(*pieces[0])
    for cut in pieces[1:]:
        gain = gain * one(*cut)
    return gain


def scatter_about(own_key, dims, scale, most, cuts=(), held_as=jnp.bfloat16):
    factor_of = shard_levels(own_key, dims, cuts, -0.22, 0.18) if cuts else 1.0
    values = jax.random.normal(own_key, dims, jnp.float32) * scale * factor_of
    return jnp.minimum(jnp.maximum(values, -most), most).astype(held_as)


def setup_inputs(seed: int = 0) -> dict:
    arg_keys = jax.random.split(jax.random.key(seed), 9)
    features = scatter_about(arg_keys[0], (NX, NY, C), 1.0, 6.0, ((0, 16), (1, 8)))
    occupied = place_ends((jax.random.randint(arg_keys[1], (NX, NY), 0, 4) < 3).astype(jnp.int32), jax.random.fold_in(arg_keys[1], 1), 0, 1)
    conv_weight = scatter_about(arg_keys[2], (9, C, C), (9 * C) ** -0.5, 0.125)
    norm_gain = jnp.clip(1.0 + 0.18 * jax.random.normal(arg_keys[3], (C,), jnp.float32), 0.1, 1.9)
    w_qkv = draw_w_qkv(jax.random.fold_in(arg_keys[8], 71), 0)
    w_proj = scatter_about(arg_keys[5], (C, C), C ** -0.5, 0.375)
    tile_dest = draw_tile_dest(jax.random.fold_in(arg_keys[8], 71), 0)
    cotangent = scatter_about(arg_keys[7], (NX, NY, C), 1.0, 6.0, ((0, 16), (1, 8)))
    return dict(features=features, occupied=occupied, conv_weight=conv_weight, norm_gain=norm_gain, w_qkv=w_qkv, w_proj=w_proj, tile_dest=tile_dest, cotangent=cotangent)


norm_eps = 1e-05
mask_fill = 1000000000.0

def tap_sum(padded, weight, flip):
    size_x = padded.shape[0] - 2
    size_y = padded.shape[1] - 2
    feat_width = padded.shape[2]
    summed = jnp.zeros((size_x * size_y, feat_width), jnp.float32)
    for row_tap in range(3):
        for col_tap in range(3):
            if flip:
                piece = padded[2 - row_tap:2 - row_tap + size_x, 2 - col_tap:2 - col_tap + size_y]
                kernel = weight[row_tap * 3 + col_tap].T
            else:
                piece = padded[row_tap:row_tap + size_x, col_tap:col_tap + size_y]
                kernel = weight[row_tap * 3 + col_tap]
            summed = summed + jnp.dot(piece.reshape(-1, feat_width), kernel, preferred_element_type=jnp.float32)
    return summed.reshape(size_x, size_y, feat_width)

def patch_full(h_patch, g_patch, key_live, w_qkv, w_proj):
    row_count, feat_width = h_patch.shape
    head_dim = feat_width // HEADS
    score_scale = 1.0 / math.sqrt(head_dim)
    qkv = jnp.dot(h_patch, w_qkv, preferred_element_type=jnp.float32).astype(jnp.bfloat16)
    query_heads = qkv[:, :feat_width].reshape(row_count, HEADS, head_dim).astype(jnp.float32)
    key_heads = qkv[:, feat_width:2 * feat_width].reshape(row_count, HEADS, head_dim).astype(jnp.float32)
    value_heads = qkv[:, 2 * feat_width:].reshape(row_count, HEADS, head_dim).astype(jnp.float32)
    key_bias = (key_live - 1.0) * mask_fill
    block_rows = min(512, row_count)
    q_blocks = query_heads.reshape(row_count // block_rows, block_rows, HEADS, head_dim)
    g_blocks = g_patch.reshape(row_count // block_rows, block_rows, feat_width)

    def one_block(operands):
        q_block, grad_block = operands
        scores = jnp.einsum('qhd,khd->hqk', q_block, key_heads) * score_scale + key_bias[None, None, :]
        row_top = lax.optimization_barrier(jnp.max(scores, axis=-1, keepdims=True))
        powers = jnp.exp(scores - row_top)
        probs_full = powers / lax.optimization_barrier(jnp.sum(powers, axis=-1, keepdims=True))
        probs_low = probs_full.astype(jnp.bfloat16).astype(jnp.float32)
        mixed_heads = jnp.einsum('hqk,khd->qhd', probs_low, value_heads).astype(jnp.bfloat16)
        attended = jnp.dot(mixed_heads.reshape(block_rows, feat_width), w_proj, preferred_element_type=jnp.float32).astype(jnp.bfloat16)
        d_mixed = jnp.dot(grad_block, w_proj.T, preferred_element_type=jnp.float32).astype(jnp.bfloat16)
        d_mixed = d_mixed.reshape(block_rows, HEADS, head_dim).astype(jnp.float32)
        d_probs = jnp.einsum('qhd,khd->hqk', d_mixed, value_heads)
        d_values = jnp.einsum('hqk,qhd->khd', probs_low, d_mixed)
        d_scores = probs_full * (d_probs - lax.optimization_barrier(jnp.sum(d_probs * probs_full, axis=-1, keepdims=True))) * score_scale
        d_scores = d_scores.astype(jnp.bfloat16).astype(jnp.float32)
        d_query = jnp.einsum('hqk,khd->qhd', d_scores, key_heads).astype(jnp.bfloat16)
        d_keys = jnp.einsum('hqk,qhd->khd', d_scores, q_block)
        return (attended, d_query, d_keys, d_values)
    attended, d_query, d_keys, d_values = lax.map(one_block, (q_blocks, g_blocks))
    d_qkv = jnp.concatenate([d_query.reshape(row_count, feat_width), lax.optimization_barrier(jnp.sum(d_keys, axis=0)).astype(jnp.bfloat16).reshape(row_count, feat_width), lax.optimization_barrier(jnp.sum(d_values, axis=0)).astype(jnp.bfloat16).reshape(row_count, feat_width)], axis=1)
    d_hidden = jnp.dot(d_qkv, w_qkv.T, preferred_element_type=jnp.float32).astype(jnp.bfloat16)
    w_part = jnp.dot(h_patch.T, d_qkv, preferred_element_type=jnp.float32)
    return (attended.reshape(row_count, feat_width), d_hidden, w_part)

def to_tiles(array):
    trailing = array.shape[2:]
    blocks = array.reshape((N_GX, HX, N_GY, HY) + trailing)
    blocks = jnp.moveaxis(blocks, 2, 0)
    return blocks.reshape((N_GY, N_GX * TILES_DEV, TILE) + trailing)

def from_tiles(tiles):
    trailing = tiles.shape[3:]
    blocks = tiles.reshape((N_GY, N_GX, HX, HY) + trailing)
    blocks = jnp.moveaxis(blocks, 0, 2)
    return blocks.reshape((N_GX * HX, N_GY * HY) + trailing)

def serialize(tiles, tile_order):
    return jax.vmap(lambda column, places: jnp.zeros_like(column).at[places].set(column))(tiles, tile_order)

def unserialize(serial, tile_order):
    return jax.vmap(lambda column, places: column[places])(serial, tile_order)

def reference(features, occupied, conv_weight, norm_gain, w_qkv, w_proj, tile_dest, cotangent):
    alive = occupied > 0
    occupancy_f = alive[..., None].astype(jnp.float32)
    masked = jnp.where(alive[..., None], features, jnp.zeros_like(features))
    padded = jnp.pad(masked, ((1, 1), (1, 1), (0, 0)))
    conv_out = tap_sum(padded, conv_weight, False) * occupancy_f
    residual = features.astype(jnp.float32) + conv_out
    centre = lax.optimization_barrier(jnp.mean(residual, axis=-1, keepdims=True))
    deviation = residual - centre
    variance = lax.optimization_barrier(jnp.mean(deviation * deviation, axis=-1, keepdims=True))
    inv_std = lax.rsqrt(variance + norm_eps)
    normal = deviation * inv_std
    hidden = (normal * norm_gain).astype(jnp.bfloat16)
    tile_order = tile_dest.T.astype(jnp.int32)
    serial_hidden = serialize(to_tiles(hidden), tile_order)
    serial_cot = serialize(to_tiles(cotangent), tile_order)
    serial_live = serialize(to_tiles(occupied), tile_order)
    feat_width = features.shape[2]
    h_patches = serial_hidden.reshape(-1, PATCH, feat_width)
    g_patches = serial_cot.reshape(-1, PATCH, feat_width)
    l_patches = serial_live.reshape(-1, PATCH).astype(jnp.float32)

    def one_patch(operands):
        return patch_full(operands[0], operands[1], operands[2], w_qkv, w_proj)
    attended, d_hidden, w_parts = lax.map(one_patch, (h_patches, g_patches, l_patches))
    w_qkv_grad = lax.optimization_barrier(jnp.sum(w_parts, axis=0)) / math.sqrt(NX * NY)
    tile_shape = (N_GY, N_GX * TILES_DEV, TILE, feat_width)
    attended = from_tiles(unserialize(attended.reshape(tile_shape), tile_order))
    d_hidden = from_tiles(unserialize(d_hidden.reshape(tile_shape), tile_order))
    block_output = (residual + attended.astype(jnp.float32)).astype(jnp.bfloat16)
    scaled = d_hidden.astype(jnp.float32) * norm_gain
    d_residual = cotangent.astype(jnp.float32) + inv_std * (scaled - lax.optimization_barrier(jnp.mean(scaled, axis=-1, keepdims=True)) - normal * lax.optimization_barrier(jnp.mean(scaled * normal, axis=-1, keepdims=True)))
    grad_masked = jnp.where(alive[..., None], d_residual, 0.0).astype(jnp.bfloat16)
    grad_padded = jnp.pad(grad_masked, ((1, 1), (1, 1), (0, 0)))
    d_features = (d_residual + occupancy_f * tap_sum(grad_padded, conv_weight, True)).astype(jnp.bfloat16)
    return (block_output, d_features, w_qkv_grad)
```

```python
import math

import jax
import jax.numpy as jnp
from jax import lax
from jax.experimental import pallas as pl
from jax.experimental.pallas import tpu as pltpu
from jax.sharding import PartitionSpec as P

C = 256
HEADS = 16
HEAD = 16
PATCH = 1024
TILE = 128
TILES = 8
PEERS = 16
META = 16
KEYS = 832
W_CHUNKS = 96

norm_eps = 1e-05
mask_fill = 1000000000.0
LOG2E = 1.4426950408889634
BOUND2 = (4.0 * 40.0) ** 2

bf16 = jnp.bfloat16
f32 = jnp.float32
VMEM_LIMIT = 56 * 2**20


def nn(a, b):
    return lax.dot_general(a, b, (((1,), (0,)), ((), ())), preferred_element_type=f32)


def nt(a, b):
    return lax.dot_general(a, b, (((1,), (1,)), ((), ())), preferred_element_type=f32)


def tn(a, b):
    return lax.dot_general(a, b, (((0,), (0,)), ((), ())), preferred_element_type=f32)


def call(body, out_shape, scratch=(), smem=0, vmem=0, name=None, cost=None):
    return pl.pallas_call(
        body,
        out_shape=out_shape,
        in_specs=[pl.BlockSpec(memory_space=pltpu.SMEM)] * smem
        + [pl.BlockSpec(memory_space=pltpu.VMEM)] * vmem,
        scratch_shapes=list(scratch),
        name=name,
        cost_estimate=cost,
        compiler_params=pltpu.CompilerParams(vmem_limit_bytes=VMEM_LIMIT),
    )


def struct(shape, dtype):
    return jax.ShapeDtypeStruct(shape, dtype)


def pack_kernel(dest, cot, occ, send):
    rows = lax.broadcasted_iota(jnp.int32, (META, C), 0)
    for peer in range(PEERS):
        send[peer, TILE:, :] = jnp.full((META, C), -1.0, f32).astype(bf16)
    live = occ[...].astype(f32)
    for tile in range(TILES):
        target = dest[tile]
        peer = target >> 3
        slot = (target & 7).astype(f32)
        send[peer, :TILE, :] = cot[tile * TILE : (tile + 1) * TILE, :]
        line = jnp.concatenate([live[tile : tile + 1], jnp.zeros((1, C - TILE), f32)], axis=1)
        send[peer, TILE:, :] = jnp.where(rows == 0, line, slot).astype(bf16)


def shifted_rows(block, top, bottom, left, right, shifts):
    whole = jnp.concatenate([top[...], block[...], bottom[...]], axis=0).astype(f32)
    total = whole.shape[0]
    lines = total // 32
    col = lax.broadcasted_iota(jnp.int32, (total, C), 0) & 31
    left_wide = jnp.broadcast_to(left[...].astype(f32), (lines, 32, C)).reshape(total, C)
    right_wide = jnp.broadcast_to(right[...].astype(f32), (lines, 32, C)).reshape(total, C)
    shifts[0] = jnp.where(col == 0, left_wide, pltpu.roll(whole, 1, 0)).astype(bf16)
    shifts[1] = whole.astype(bf16)
    shifts[2] = jnp.where(col == 31, right_wide, pltpu.roll(whole, total - 1, 0)).astype(bf16)


def occupancy_columns(occ):
    live = occ[...].astype(f32)
    square = jnp.concatenate([live, jnp.zeros((TILE - TILES, TILE), f32)], axis=0)
    return square.T


def forward_kernel(dest, feat, masked, top, bottom, left, right, occ, weight, gain, resid, send, shifts):
    shifted_rows(masked, top, bottom, left, right, shifts)
    columns = occupancy_columns(occ)
    conv = None
    for a in range(3):
        for b in range(3):
            term = nn(shifts[b, a * 32 : a * 32 + PATCH, :], weight[a * 3 + b])
            conv = term if conv is None else conv + term
    for tile in range(TILES):
        rows = slice(tile * TILE, (tile + 1) * TILE)
        residual = feat[rows, :].astype(f32) + conv[rows] * columns[:, tile : tile + 1]
        resid[rows, :] = residual
        centre = jnp.mean(residual, axis=-1, keepdims=True)
        deviation = residual - centre
        variance = jnp.mean(deviation * deviation, axis=-1, keepdims=True)
        normal = deviation * lax.rsqrt(variance + norm_eps)
        send[dest[tile] >> 3] = (normal * gain[...]).astype(bf16)


def fast_heads(q_t, khl, k_t, v_aug, v_t, live_rows, dm_t, o_t, dq_t, dk_t, dv_t):
    rows = lax.broadcasted_iota(jnp.int32, (HEAD, PATCH), 0)

    def one_head(h, carry):
        at = pl.ds(pl.multiple_of(h * HEAD, HEAD), HEAD)
        query = q_t[at, :]
        powers = jnp.exp2(nn(khl[h], jnp.concatenate([query, query], axis=0)))
        low = powers.astype(bf16)
        mixed = nn(jnp.concatenate([v_t[at, :], live_rows[...]], axis=0), low)
        inverse = 1.0 / mixed[HEAD : HEAD + 1]
        mixed = mixed[:HEAD] * inverse
        o_t[at, :] = mixed.astype(bf16)
        d_mixed = dm_t[at, :].astype(f32)
        inner = jnp.sum(d_mixed * mixed, axis=0, keepdims=True) * inverse
        high = inner.astype(bf16).astype(f32)
        extra = jnp.where(rows == 0, -high, jnp.where(rows == 1, high - inner, 0.0)).astype(bf16)
        scaled = (d_mixed * inverse).astype(bf16)
        centred = nn(v_aug[h], jnp.concatenate([scaled, extra], axis=0))
        d_scores = (powers * centred).astype(bf16)
        dq_t[at, :] = (nn(k_t[at, :], d_scores) * 0.25).astype(bf16)
        dv_t[at, :] = nt(scaled, low).astype(bf16)
        dk_t[at, :] = (nt(query, d_scores) * 0.25).astype(bf16)
        return carry

    lax.fori_loop(0, HEADS, one_head, 0)


def plain_heads(q_t, kf_t, vf_t, dm_t, bias, o_t, dqkv_t):
    block = 256

    def one_head(h, carry):
        start = pl.multiple_of(h * HEAD, HEAD)
        at = pl.ds(start, HEAD)
        key, value = kf_t[at, :], vf_t[at, :]

        def one_block(c, sums):
            d_keys, d_values = sums
            cols = pl.ds(pl.multiple_of(c * block, block), block)
            query, d_mixed = q_t[at, cols], dm_t[at, cols]
            scores = tn(key, query) * 0.25 + bias
            powers = jnp.exp(scores - jnp.max(scores, axis=0, keepdims=True))
            probs = powers / jnp.sum(powers, axis=0, keepdims=True)
            low = probs.astype(bf16)
            o_t[at, cols] = nn(value, low).astype(bf16)
            d_probs = tn(value, d_mixed)
            inner = jnp.sum(d_probs * probs, axis=0, keepdims=True)
            d_scores = (probs * (d_probs - inner) * 0.25).astype(bf16)
            dqkv_t[at, cols] = nn(key, d_scores).astype(bf16)
            return (d_keys + nt(query, d_scores), d_values + nt(d_mixed, low))

        zero = jnp.zeros((HEAD, PATCH), f32)
        d_keys, d_values = lax.fori_loop(0, PATCH // block, one_block, (zero, zero))
        dqkv_t[pl.ds(start + C, HEAD), :] = d_keys.astype(bf16)
        dqkv_t[pl.ds(start + 2 * C, HEAD), :] = d_values.astype(bf16)
        return carry

    lax.fori_loop(0, HEADS, one_head, 0)


def attention_kernel(
    src, h_recv, g_recv, w_qkv, w_qkv_t, w_proj, att_send, dh_send, w_send,
    hidden, cot, q_t, kf_t, vf_t, khl, k_t, v_aug, v_t, live_rows, dm_t, o_t, dqkv_t, dkv_t, perm, fits,
):
    lives = []
    for tile in range(TILES):
        rows = slice(tile * TILE, (tile + 1) * TILE)
        hidden[rows, :] = h_recv[src[tile]]
        cot[rows, :] = g_recv[src[tile], :TILE, :]
        lives.append(g_recv[src[tile], TILE:, :].astype(f32)[0:1, :TILE])
    live = jnp.concatenate(lives, axis=0)
    lane_a = lax.broadcasted_iota(jnp.int32, (TILE, TILE), 0)
    lane_b = lax.broadcasted_iota(jnp.int32, (TILE, TILE), 1)
    counts = nn(live.astype(bf16), (lane_a <= lane_b).astype(f32).astype(bf16))
    totals = jnp.broadcast_to(counts[:, TILE - 1 :], (TILES, TILE))
    line_a = lax.broadcasted_iota(jnp.int32, (TILES, TILES), 0)
    line_b = lax.broadcasted_iota(jnp.int32, (TILES, TILES), 1)
    before = nn((line_b < line_a).astype(f32).astype(bf16), totals.astype(bf16))
    place = jnp.where(live > 0.5, counts + before - 1.0, -1.0)
    place_row = jnp.concatenate([place[t : t + 1] for t in range(TILES)], axis=1)
    live_count = jnp.sum(live)
    key_index = lax.broadcasted_iota(jnp.int32, (KEYS, PATCH), 0).astype(f32)
    perm[...] = (key_index == place_row).astype(f32).astype(bf16)

    dm_t[...] = nt(w_proj[...], cot[...]).astype(bf16)
    q_t[...] = nt(w_qkv_t[:C, :], hidden[...]).astype(bf16)
    keys_in = nn(perm[...], hidden[...]).astype(bf16)
    k_t[...] = nt(w_qkv_t[C : 2 * C, :], keys_in).astype(bf16)
    v_t[...] = nt(w_qkv_t[2 * C :, :], keys_in).astype(bf16)
    q_square = jnp.square(q_t[...].astype(f32)).reshape(HEADS, HEAD, PATCH)
    k_square = jnp.square(k_t[...].astype(f32)).reshape(HEADS, HEAD, KEYS)
    q_top = jnp.max(jnp.sum(q_square, axis=1))
    k_top = jnp.max(jnp.sum(k_square, axis=1))
    fits_here = (live_count >= 1.0) & (live_count <= float(KEYS)) & (q_top * k_top <= BOUND2)
    fits[0] = fits_here.astype(jnp.int32)

    @pl.when(fits[0] == 1)
    def _():
        keys = nn(keys_in, w_qkv[:, C : 2 * C]).astype(bf16).astype(f32) * (0.25 * LOG2E)
        values = nn(keys_in, w_qkv[:, 2 * C :]).astype(bf16)
        keys_high = keys.astype(bf16)
        keys_low = (keys - keys_high.astype(f32)).astype(bf16)
        lane = lax.broadcasted_iota(jnp.int32, (KEYS, HEAD), 1)
        ones = (lane < 2).astype(f32).astype(bf16)
        for h in range(HEADS):
            at = slice(h * HEAD, (h + 1) * HEAD)
            khl[h] = jnp.concatenate([keys_high[:, at], keys_low[:, at]], axis=1)
            v_aug[h] = jnp.concatenate([values[:, at], ones], axis=1)
        row = lax.broadcasted_iota(jnp.int32, (HEAD, KEYS), 0)
        col = lax.broadcasted_iota(jnp.int32, (HEAD, KEYS), 1).astype(f32)
        live_rows[...] = ((row == 0) & (col < live_count)).astype(f32).astype(bf16)
        fast_heads(
            q_t, khl, k_t, v_aug, v_t, live_rows, dm_t, o_t,
            dqkv_t.at[pl.ds(0, C)], dkv_t.at[pl.ds(0, C)], dkv_t.at[pl.ds(C, C)],
        )
        dqkv_t[C:, :] = nn(dkv_t[...], perm[...]).astype(bf16)

    @pl.when(fits[0] == 0)
    def _():
        kf_t[...] = nt(w_qkv_t[C : 2 * C, :], hidden[...]).astype(bf16)
        vf_t[...] = nt(w_qkv_t[2 * C :, :], hidden[...]).astype(bf16)
        square = jnp.concatenate([live, jnp.zeros((TILE - TILES, TILE), f32)], axis=0).T
        column = jnp.concatenate([square[:, t : t + 1] for t in range(TILES)], axis=0)
        plain_heads(q_t, kf_t, vf_t, dm_t, (column - 1.0) * mask_fill, o_t, dqkv_t)

    attended = tn(o_t[...], w_proj[...]).astype(bf16)
    d_hidden = tn(dqkv_t[...], w_qkv_t[...]).astype(bf16)
    for tile in range(TILES):
        rows = slice(tile * TILE, (tile + 1) * TILE)
        att_send[src[tile]] = attended[rows]
        dh_send[src[tile]] = d_hidden[rows]
    w_part = nt(hidden[...].T, dqkv_t[...]).astype(bf16)
    for i in range(W_CHUNKS):
        r, c = (i // 6) * 16, (i % 6) * TILE
        w_send[i] = w_part[r : r + 16, c : c + TILE]
    w_send[W_CHUNKS:] = jnp.zeros((TILE - W_CHUNKS, 16, TILE), f32).astype(bf16)


def residual_grad_kernel(dest, back, resid, cot, occ, gain, d_resid, masked):
    columns = occupancy_columns(occ)
    for tile in range(TILES):
        rows = slice(tile * TILE, (tile + 1) * TILE)
        residual = resid[rows, :]
        centre = jnp.mean(residual, axis=-1, keepdims=True)
        deviation = residual - centre
        variance = jnp.mean(deviation * deviation, axis=-1, keepdims=True)
        inv_std = lax.rsqrt(variance + norm_eps)
        normal = deviation * inv_std
        scaled = back[dest[tile] >> 3].astype(f32) * gain[...]
        grad = cot[rows, :].astype(f32) + inv_std * (
            scaled
            - jnp.mean(scaled, axis=-1, keepdims=True)
            - normal * jnp.mean(scaled * normal, axis=-1, keepdims=True)
        )
        d_resid[rows, :] = grad
        masked[rows, :] = jnp.where(columns[:, tile : tile + 1] > 0.0, grad, 0.0).astype(bf16)


def conv_grad_kernel(d_resid, masked, top, bottom, left, right, occ, weight, out, shifts):
    shifted_rows(masked, top, bottom, left, right, shifts)
    columns = occupancy_columns(occ)
    conv = None
    for a in range(3):
        for b in range(3):
            term = nt(shifts[2 - b, (2 - a) * 32 : (2 - a) * 32 + PATCH, :], weight[a * 3 + b])
            conv = term if conv is None else conv + term
    for tile in range(TILES):
        rows = slice(tile * TILE, (tile + 1) * TILE)
        out[rows, :] = (d_resid[rows, :] + conv[rows] * columns[:, tile : tile + 1]).astype(bf16)


def output_kernel(dest, back, resid, out):
    for tile in range(TILES):
        rows = slice(tile * TILE, (tile + 1) * TILE)
        out[rows, :] = (resid[rows, :] + back[dest[tile] >> 3].astype(f32)).astype(bf16)


def exchange(low_edge, high_edge, axis):
    count = lax.axis_size(axis)
    forward = [(i, i + 1) for i in range(count - 1)]
    backward = [(target, source) for source, target in forward]
    return lax.ppermute(high_edge, axis, forward), lax.ppermute(low_edge, axis, backward)


def halo(block):
    grid = block.reshape(32, 32, C)
    top, bottom = exchange(grid[:1], grid[31:], "gx")
    low = jnp.concatenate([top[:, :1], grid[:, :1], bottom[:, :1]], axis=0)
    high = jnp.concatenate([top[:, 31:], grid[:, 31:], bottom[:, 31:]], axis=0)
    left, right = exchange(low, high, "gy")
    return top.reshape(32, C), bottom.reshape(32, C), left, right


def swap(array, axis="gx"):
    return lax.all_to_all(array, axis, split_axis=0, concat_axis=0, tiled=True)


def attention(src, h_recv, g_recv, w_qkv, w_proj):
    scratch = [
        pltpu.VMEM((PATCH, C), bf16), pltpu.VMEM((PATCH, C), bf16),
        pltpu.VMEM((C, PATCH), bf16), pltpu.VMEM((C, PATCH), bf16), pltpu.VMEM((C, PATCH), bf16),
        pltpu.VMEM((HEADS, KEYS, 32), bf16), pltpu.VMEM((C, KEYS), bf16),
        pltpu.VMEM((HEADS, KEYS, 32), bf16), pltpu.VMEM((C, KEYS), bf16),
        pltpu.VMEM((HEAD, KEYS), bf16),
        pltpu.VMEM((C, PATCH), bf16), pltpu.VMEM((C, PATCH), bf16),
        pltpu.VMEM((3 * C, PATCH), bf16), pltpu.VMEM((2 * C, KEYS), bf16),
        pltpu.VMEM((KEYS, PATCH), bf16), pltpu.SMEM((1,), jnp.int32),
    ]
    buckets = struct((PEERS, TILE, C), bf16)
    return call(
        attention_kernel,
        [buckets, buckets, struct((TILE, 16, TILE), bf16)],
        scratch, smem=1, vmem=5, name="attention",
        cost=pl.CostEstimate(flops=40 * 10**9, bytes_accessed=8 * 10**6, transcendentals=16 * 10**6),
    )(src, h_recv, g_recv, w_qkv, w_qkv.T, w_proj)


def local(features, occupied, conv_weight, norm_gain, w_qkv, w_proj, tile_dest, cotangent):
    size_x, size_y, feat_width = features.shape
    cells = size_x * size_y
    dest = tile_dest.reshape(TILES)
    occ = occupied.reshape(TILES, TILE)
    gain = norm_gain.reshape(1, C)
    feat = features.reshape(cells, C)
    cot = cotangent.reshape(cells, C)
    rows_f32 = struct((cells, C), f32)
    rows_bf16 = struct((cells, C), bf16)
    buckets = struct((PEERS, TILE, C), bf16)
    shifts = pltpu.VMEM((3, cells + 64, C), bf16)

    g_send = call(pack_kernel, struct((PEERS, TILE + META, C), bf16), smem=1, vmem=2, name="pack")(dest, cot, occ)
    g_recv = swap(g_send)
    masked = jnp.where((occupied > 0)[..., None], features, jnp.zeros_like(features)).reshape(cells, C)
    edges = halo(masked)
    resid, h_send = call(
        forward_kernel, [rows_f32, buckets], [shifts], smem=1, vmem=9, name="forward"
    )(dest, feat, masked, *edges, occ, conv_weight, gain)
    h_recv = swap(h_send)

    slots = g_recv[:, TILE + 1, 0].astype(f32)
    order = jnp.arange(TILES, dtype=f32)
    peers = jnp.arange(PEERS, dtype=jnp.int32)
    src = jnp.sum(jnp.where(slots[None, :] == order[:, None], peers[None, :], 0), axis=1)

    att_send, dh_send, w_send = attention(src, h_recv, g_recv, w_qkv, w_proj)
    dh_back = swap(dh_send)
    w_terms = swap(w_send, ("gx", "gy"))
    w_sum = jnp.sum(w_terms.astype(f32), axis=0) / math.sqrt(131072)
    att_back = swap(att_send)

    d_resid, grad_masked = call(
        residual_grad_kernel, [rows_f32, rows_bf16], smem=1, vmem=5, name="residual_grad"
    )(dest, dh_back, resid, cot, occ, gain)
    grad_edges = halo(grad_masked)
    d_features = call(
        conv_grad_kernel, rows_bf16, [shifts], vmem=8, name="conv_grad"
    )(d_resid, grad_masked, *grad_edges, occ, conv_weight)
    block_output = call(output_kernel, rows_bf16, smem=1, vmem=2, name="output")(dest, att_back, resid)

    w_all = swap(jnp.broadcast_to(w_sum[None], (TILE, 16, TILE)), ("gx", "gy"))
    w_grad = w_all[:W_CHUNKS].reshape(16, 6, 16, TILE).transpose(0, 2, 1, 3).reshape(C, 3 * C)
    shape = (size_x, size_y, feat_width)
    return (block_output.reshape(shape), d_features.reshape(shape), w_grad)


def solution(mesh):
    in_specs = (
        P("gx", "gy", None),
        P("gx", "gy"),
        P(),
        P(),
        P(),
        P(),
        P("gx", "gy"),
        P("gx", "gy", None),
    )
    out_specs = (P("gx", "gy", None), P("gx", "gy", None), P())
    return jax.shard_map(local, mesh=mesh, in_specs=in_specs, out_specs=out_specs, check_vma=False)
```

```python
import functools
import math

import jax
import jax.numpy as jnp
from jax import lax
from jax.experimental import pallas as pl
from jax.experimental.pallas import tpu as pltpu
from jax.sharding import PartitionSpec as P

C = 256
HEADS = 16
HEAD = 16
PATCH = 1024
TILE = 128
TILES = 8
PEERS = 16
META = 16
KEYS = 832
W_ROWS = 48
COLUMN = 8
PAIR = 2
LANES = 128
LIMIT = 40

norm_eps = 1e-05
mask_fill = 1000000000.0
LOG2E = 1.4426950408889634
BOUND2 = (4.0 * 40.0) ** 2

bf16 = jnp.bfloat16
f32 = jnp.float32
MIB = 2**20


def nn(a, b):
    return lax.dot_general(a, b, (((1,), (0,)), ((), ())), preferred_element_type=f32)


def nt(a, b):
    return lax.dot_general(a, b, (((1,), (1,)), ((), ())), preferred_element_type=f32)


def tn(a, b):
    return lax.dot_general(a, b, (((0,), (0,)), ((), ())), preferred_element_type=f32)


SMEM = pl.BlockSpec(memory_space=pltpu.SMEM)
WHOLE = pl.BlockSpec(memory_space=pltpu.VMEM)
FAR = pl.BlockSpec(memory_space=pltpu.HBM)


def far(shape, dtype):
    return pltpu.HBM(shape, dtype)


def pin(array):
    return pltpu.with_memory_space_constraint(array, pltpu.HBM)


def call(body, out_shape, in_specs, out_specs, scratch=(), name=None, cost=None, limit=16):
    return pl.pallas_call(
        body,
        out_shape=out_shape,
        in_specs=in_specs,
        out_specs=out_specs,
        scratch_shapes=list(scratch),
        name=name,
        cost_estimate=cost,
        compiler_params=pltpu.CompilerParams(vmem_limit_bytes=limit * MIB),
    )


def struct(shape, dtype):
    return jax.ShapeDtypeStruct(shape, dtype)


def pack_kernel(dest, cot, send, sems):
    moves = [
        pltpu.make_async_copy(cot.at[pl.ds(tile * TILE, TILE), :], send.at[dest[tile] >> 3], sems.at[tile])
        for tile in range(TILES)
    ]
    for move in moves:
        move.start()
    for move in moves:
        move.wait()


def edge_columns(block):
    edge = lax.broadcasted_iota(jnp.int32, (64, PATCH), 0)
    cell = lax.broadcasted_iota(jnp.int32, (64, PATCH), 1)
    wanted = jnp.where(edge < 32, edge * 32, (edge - 32) * 32 + 31)
    return nn((cell == wanted).astype(f32).astype(bf16), block).astype(bf16)


def mask_kernel(feat, occ, masked, first, final, low, high):
    live = occ[...].astype(f32)
    wide = jnp.concatenate([live, jnp.zeros((32, TILE - 32), f32)], axis=1)
    columns = jnp.concatenate([wide, jnp.zeros((TILE - 32, TILE), f32)], axis=0).T
    for line in range(32):
        rows = slice(line * 32, line * 32 + 32)
        kept = jnp.where(columns[:32, line : line + 1] > 0.0, feat[rows, :].astype(f32), 0.0)
        masked[rows, :] = kept.astype(bf16)
    first[...] = masked[:32, :]
    final[...] = masked[PATCH - 32 :, :]
    sides = edge_columns(masked[...])
    low[...] = sides[:32]
    high[...] = sides[32:]


def tap_dot(a, b, flip):
    return nt(a, b) if flip else nn(a, b)


def inside_taps(flip, block, weight, shifts):
    edge = jnp.zeros((32, C), f32)
    whole = jnp.concatenate([edge, block, edge], axis=0)
    total = whole.shape[0]
    col = lax.broadcasted_iota(jnp.int32, (total, C), 0) & 31
    shifts[0] = jnp.where(col == 0, 0.0, pltpu.roll(whole, 1, 0)).astype(bf16)
    shifts[1] = whole.astype(bf16)
    shifts[2] = jnp.where(col == 31, 0.0, pltpu.roll(whole, total - 1, 0)).astype(bf16)
    conv = None
    for a in range(3):
        for b in range(3):
            x, y = (2 - a, 2 - b) if flip else (a, b)
            term = tap_dot(shifts[y, x * 32 : x * 32 + PATCH, :], weight[a * 3 + b], flip)
            conv = term if conv is None else conv + term
    return conv


def conv_inside_kernel(block, weight, out, conv, shifts, sem):
    conv[...] = inside_taps(False, block[...].astype(f32), weight, shifts)
    save = pltpu.make_async_copy(conv, out, sem.at[0])
    save.start()
    save.wait()


def add_border(flip, top, bottom, left, right, weight, total):
    line = jnp.zeros((1, C), f32)
    first, last = (2, 0) if flip else (0, 2)

    def side(cells, taps):
        summed = None
        for k, tap in enumerate(taps):
            shift = 2 - k if flip else k
            term = tap_dot(cells[shift : shift + 32].astype(bf16), weight[tap], flip)
            summed = term if summed is None else summed + term
        return summed

    for edge, row, a in ((top, 0, first), (bottom, 31, last)):
        padded = jnp.concatenate([line, edge[...].astype(f32), line], axis=0)
        rows = slice(row * 32, row * 32 + 32)
        total[rows, :] = total[rows, :] + side(padded, [a * 3 + b for b in range(3)])
    for edge, col, b in ((left, 0, first), (right, 31, last)):
        added = side(edge[...].astype(f32), [a * 3 + b for a in range(3)])
        for i in range(32):
            at = slice(i * 32 + col, i * 32 + col + 1)
            total[at, :] = total[at, :] + added[i : i + 1]


def occupancy_columns(occ):
    live = occ[...].astype(f32)
    square = jnp.concatenate([live, jnp.zeros((TILE - TILES, TILE), f32)], axis=0)
    return square.T


def forward_kernel(
    dest, conv, feat, top, bottom, left, right, occ, weight, gain,
    resid_out, send, total, resid, hidden, meta, sems,
):
    load = pltpu.make_async_copy(conv, total, sems.at[1 + 2 * TILES])
    load.start()
    live = occ[...].astype(f32)
    row = lax.broadcasted_iota(jnp.int32, (META, C), 0)
    meta[...] = jnp.zeros(meta.shape, f32).astype(bf16)
    for tile in range(TILES):
        line = jnp.concatenate([live[tile : tile + 1], jnp.zeros((1, C - TILE), f32)], axis=1)
        meta[dest[tile] >> 3] = jnp.where(row == 0, line, 1.0).astype(bf16)
    moves = [pltpu.make_async_copy(meta, send.at[:, pl.ds(TILE, META), :], sems.at[0])]
    moves[0].start()
    load.wait()
    add_border(False, top, bottom, left, right, weight, total)
    columns = occupancy_columns(occ)
    for tile in range(TILES):
        rows = slice(tile * TILE, (tile + 1) * TILE)
        residual = feat[rows, :].astype(f32) + total[rows, :] * columns[:, tile : tile + 1]
        resid[rows, :] = residual
        centre = jnp.mean(residual, axis=-1, keepdims=True)
        deviation = residual - centre
        variance = jnp.mean(deviation * deviation, axis=-1, keepdims=True)
        hidden[rows, :] = (deviation * lax.rsqrt(variance + norm_eps) * gain[...]).astype(bf16)
        at = pl.ds(tile * TILE, TILE)
        for k, (source, target) in enumerate((
            (hidden.at[at, :], send.at[dest[tile] >> 3, pl.ds(0, TILE), :]),
            (resid.at[at, :], resid_out.at[at, :]),
        )):
            moves.append(pltpu.make_async_copy(source, target, sems.at[1 + 2 * tile + k]))
            moves[-1].start()
    for move in moves:
        move.wait()


def plain_forward(h, q_t, kf_t, vf_t, bias, o_t):
    block = 256
    at = pl.ds(pl.multiple_of(h * HEAD, HEAD), HEAD)
    key, value = kf_t[at, :], vf_t[at, :]

    def one_block(c, carry):
        cols = pl.ds(pl.multiple_of(c * block, block), block)
        scores = tn(key, q_t[at, cols]) * 0.25 + bias
        powers = jnp.exp(scores - jnp.max(scores, axis=0, keepdims=True))
        low = (powers / jnp.sum(powers, axis=0, keepdims=True)).astype(bf16)
        o_t[at, cols] = nn(value, low)
        return carry

    lax.fori_loop(0, PATCH // block, one_block, 0)


def plain_backward(h, q_t, kf_t, vf_t, dm_t, bias, dqkv_t):
    block = 256
    start = pl.multiple_of(h * HEAD, HEAD)
    at = pl.ds(start, HEAD)
    key, value = kf_t[at, :], vf_t[at, :]

    def one_block(c, sums):
        d_keys, d_values = sums
        cols = pl.ds(pl.multiple_of(c * block, block), block)
        query, d_mixed = q_t[at, cols], dm_t[at, cols]
        scores = tn(key, query) * 0.25 + bias
        powers = jnp.exp(scores - jnp.max(scores, axis=0, keepdims=True))
        probs = powers / jnp.sum(powers, axis=0, keepdims=True)
        low = probs.astype(bf16)
        d_probs = tn(value, d_mixed)
        inner = jnp.sum(d_probs * probs, axis=0, keepdims=True)
        d_scores = (probs * (d_probs - inner) * 0.25).astype(bf16)
        dqkv_t[at, cols] = nn(key, d_scores).astype(bf16)
        return (d_keys + nt(query, d_scores), d_values + nt(d_mixed, low))

    zero = jnp.zeros((HEAD, PATCH), f32)
    d_keys, d_values = lax.fori_loop(0, PATCH // block, one_block, (zero, zero))
    dqkv_t[pl.ds(start + C, HEAD), :] = d_keys.astype(bf16)
    dqkv_t[pl.ds(start + 2 * C, HEAD), :] = d_values.astype(bf16)


def plain_operands(hidden, live, w_qkv_t, kf_t, vf_t, bias):
    kf_t[...] = nt(w_qkv_t[C : 2 * C, :], hidden[...]).astype(bf16)
    vf_t[...] = nt(w_qkv_t[2 * C :, :], hidden[...]).astype(bf16)
    square = jnp.concatenate([live[...], jnp.zeros((TILE - TILES, TILE), f32)], axis=0).T
    column = jnp.concatenate([square[:, t : t + 1] for t in range(TILES)], axis=0)
    bias[...] = (column - 1.0) * mask_fill


def copies(pairs, sems):
    started = [pltpu.make_async_copy(source, target, sems.at[i]) for i, (source, target) in enumerate(pairs)]
    return started


def compaction(place):
    row = jnp.concatenate([place[t : t + 1, :] for t in range(TILES)], axis=1)
    key_index = lax.broadcasted_iota(jnp.int32, (KEYS, PATCH), 0).astype(f32)
    return (key_index == row).astype(f32).astype(bf16)


def by_blocks(blocks, array, extra):
    for block in range(2):
        blocks[block, :, :LANES] = array[:, block * LANES : block * LANES + LANES]
        blocks[block, :, LANES:] = extra


def place_head(operand, h, rows):
    own = pl.multiple_of((h & 7) * HEAD, HEAD)
    before = pl.multiple_of(((h - PAIR) & 7) * HEAD, HEAD)
    operand[pl.ds(before, HEAD), :] = jnp.zeros(rows.shape, rows.dtype)
    operand[pl.ds(own, HEAD), :] = rows


def head_rows(h, offset=0):
    return pl.ds(pl.multiple_of(h * HEAD + offset, HEAD), HEAD)


def attend_kernel(
    src, h_recv, w_qkv, w_qkv_t, w_proj,
    att_send, probs, o_out, hidden_out, live, place, q_out, k_out, v_out, fits,
    attended, o_t, hidden, q_t, k_t, v_nat, v_t, k_blocks, queries, low_t, kf_t, vf_t, bias, sems, p_sems,
):
    lives = []
    for tile in range(TILES):
        rows = slice(tile * TILE, (tile + 1) * TILE)
        hidden[rows, :] = h_recv[src[tile], :TILE, :]
        lives.append(h_recv[src[tile], TILE:, :].astype(f32)[0:1, :TILE])
    alive = jnp.concatenate(lives, axis=0)
    live[...] = alive
    lane_a = lax.broadcasted_iota(jnp.int32, (TILE, TILE), 0)
    lane_b = lax.broadcasted_iota(jnp.int32, (TILE, TILE), 1)
    counts = nn(alive.astype(bf16), (lane_a <= lane_b).astype(f32).astype(bf16))
    totals = jnp.broadcast_to(counts[:, TILE - 1 :], (TILES, TILE))
    line_a = lax.broadcasted_iota(jnp.int32, (TILES, TILES), 0)
    line_b = lax.broadcasted_iota(jnp.int32, (TILES, TILES), 1)
    before = nn((line_b < line_a).astype(f32).astype(bf16), totals.astype(bf16))
    place[...] = jnp.where(alive > 0.5, counts + before - 1.0, -1.0)
    live_count = jnp.sum(alive)

    q_t[...] = nt(w_qkv_t[:C, :], hidden[...]).astype(bf16)
    keys_in = nn(compaction(place), hidden[...]).astype(bf16)
    k_t[...] = nt(w_qkv_t[C : 2 * C, :], keys_in).astype(bf16)
    v_t[...] = nt(w_qkv_t[2 * C :, :], keys_in).astype(bf16)
    v_nat[...] = nn(keys_in, w_qkv[:, 2 * C :]).astype(bf16)
    saves = copies([(hidden, hidden_out), (q_t, q_out), (k_t, k_out), (v_nat, v_out)], sems)
    for copy in saves:
        copy.start()
    q_square = jnp.square(q_t[...].astype(f32)).reshape(HEADS, HEAD, PATCH)
    k_square = jnp.square(k_t[...].astype(f32)).reshape(HEADS, HEAD, KEYS)
    q_top = jnp.max(jnp.sum(q_square, axis=1))
    k_top = jnp.max(jnp.sum(k_square, axis=1))
    good = (live_count >= 1.0) & (live_count <= float(KEYS)) & (q_top * k_top <= BOUND2)
    fits[0] = good.astype(jnp.int32)

    @pl.when(fits[0] == 1)
    def _():
        lane = lax.broadcasted_iota(jnp.int32, (KEYS, HEAD), 1)
        key = lax.broadcasted_iota(jnp.int32, (KEYS, HEAD), 0).astype(f32)
        empty = jnp.where((lane == 0) & (key >= live_count), -65536.0, 0.0).astype(bf16)
        by_blocks(k_blocks, nn(keys_in, w_qkv[:, C : 2 * C]).astype(bf16), empty)
        row = lax.broadcasted_iota(jnp.int32, (LANES + HEAD, PATCH), 0)
        for unit in range(PAIR):
            queries[unit] = (row == LANES).astype(f32).astype(bf16)

        def save_probs(slot, unit, h):
            return pltpu.make_async_copy(low_t.at[slot, unit], probs.at[h], p_sems.at[slot, unit])

        def heads(i, carry):
            slot = i & 1

            @pl.when(i > 1)
            def _():
                for unit in range(PAIR):
                    save_probs(slot, unit, (i - 2) * PAIR + unit).wait()

            for unit in range(PAIR):
                h = i * PAIR + unit
                place_head(queries.at[unit], h, q_t[head_rows(h), :])
                scores = nn(k_blocks[h >> 3], queries[unit])
                powers = jnp.exp2(scores * (0.25 * LOG2E))
                inverse = 1.0 / jnp.sum(powers, axis=0, keepdims=True)
                low = (powers * inverse).astype(bf16)
                low_t[slot, unit] = low
                o_t[head_rows(h), :] = nn(v_t[head_rows(h), :], low)
            for unit in range(PAIR):
                save_probs(slot, unit, i * PAIR + unit).start()
            return carry

        lax.fori_loop(0, HEADS // PAIR, heads, 0)
        for slot in range(2):
            for unit in range(PAIR):
                save_probs(slot, unit, HEADS - (2 - slot) * PAIR + unit).wait()

    @pl.when(fits[0] == 0)
    def _():
        plain_operands(hidden, live, w_qkv_t, kf_t, vf_t, bias)

        def one_head(h, carry):
            plain_forward(h, q_t, kf_t, vf_t, bias[...], o_t)
            return carry

        lax.fori_loop(0, HEADS, one_head, 0)

    save_o = pltpu.make_async_copy(o_t, o_out, sems.at[4])
    save_o.start()
    attended[...] = tn(o_t[...].astype(bf16), w_proj[...]).astype(bf16)
    sends = [
        pltpu.make_async_copy(
            attended.at[pl.ds(tile * TILE, TILE), :], att_send.at[src[tile]], sems.at[5 + tile]
        )
        for tile in range(TILES)
    ]
    for copy in sends:
        copy.start()
    for copy in saves + [save_o] + sends:
        copy.wait()


def attend_grad_kernel(
    src, fits, g_recv, w_qkv_t, w_proj, probs, o_far, hidden_far, live, place, q_far, k_far, v_far,
    dh_send,
    o_t, hidden, q_t, k_t, v_nat, cot, low_t, dm_t, dqkv_t, dkv_t, v_blocks, d_mixes, d_hidden, w_part, kf_t, vf_t, bias, sems, p_sems,
):
    def load_probs(slot, unit, h):
        return pltpu.make_async_copy(probs.at[h], low_t.at[slot, unit], p_sems.at[slot, unit])

    loads = [
        pltpu.make_async_copy(g_recv.at[src[tile]], cot.at[pl.ds(tile * TILE, TILE), :], sems.at[tile])
        for tile in range(TILES)
    ]
    saved = [
        pltpu.make_async_copy(source, target, sems.at[TILES + 1 + i])
        for i, (source, target) in enumerate(
            [(v_far, v_nat), (q_far, q_t), (k_far, k_t), (o_far, o_t), (hidden_far, hidden)]
        )
    ]
    for copy in loads + saved[:4]:
        copy.start()

    @pl.when(fits[0] == 1)
    def _():
        for unit in range(PAIR):
            load_probs(0, unit, unit).start()

    saved[4].start()
    for copy in loads:
        copy.wait()
    dm_t[...] = nt(w_proj[...], cot[...]).astype(bf16)
    for copy in saved:
        copy.wait()

    @pl.when(fits[0] == 1)
    def _():
        lane = lax.broadcasted_iota(jnp.int32, (KEYS, HEAD), 1)
        by_blocks(v_blocks, v_nat, (lane < 2).astype(f32).astype(bf16))
        for unit in range(PAIR):
            d_mixes[unit] = jnp.zeros((LANES + HEAD, PATCH), f32).astype(bf16)
        rows = lax.broadcasted_iota(jnp.int32, (HEAD, PATCH), 0)

        def heads(i, carry):
            slot = i & 1

            @pl.when(i < HEADS // PAIR - 1)
            def _():
                for unit in range(PAIR):
                    load_probs(1 - slot, unit, (i + 1) * PAIR + unit).start()

            for unit in range(PAIR):
                load_probs(slot, unit, i * PAIR + unit).wait()
            for unit in range(PAIR):
                h = i * PAIR + unit
                at = head_rows(h)
                d_mixed, query = dm_t[at, :], q_t[at, :]
                inner = jnp.sum(d_mixed.astype(f32) * o_t[at, :], axis=0, keepdims=True)
                high = inner.astype(bf16).astype(f32)
                place_head(d_mixes.at[unit], h, d_mixed)
                d_mixes[unit, LANES:, :] = jnp.where(
                    rows == 0, -high, jnp.where(rows == 1, high - inner, 0.0)
                ).astype(bf16)
                centred = nn(v_blocks[h >> 3], d_mixes[unit])
                low = low_t[slot, unit]
                d_scores = (low.astype(f32) * centred).astype(bf16)
                dqkv_t[at, :] = (nn(k_t[at, :], d_scores) * 0.25).astype(bf16)
                dkv_t[at, :] = (nt(query, d_scores) * 0.25).astype(bf16)
                dkv_t[head_rows(h, C), :] = nt(d_mixed, low).astype(bf16)
            return carry

        lax.fori_loop(0, HEADS // PAIR, heads, 0)
        dqkv_t[C:, :] = nn(dkv_t[...], compaction(place)).astype(bf16)

    @pl.when(fits[0] == 0)
    def _():
        plain_operands(hidden, live, w_qkv_t, kf_t, vf_t, bias)

        def one_head(h, carry):
            plain_backward(h, q_t, kf_t, vf_t, dm_t, bias[...], dqkv_t)
            return carry

        lax.fori_loop(0, HEADS, one_head, 0)

    d_hidden[...] = tn(dqkv_t[...], w_qkv_t[...]).astype(bf16)
    sends = [
        pltpu.make_async_copy(
            d_hidden.at[pl.ds(tile * TILE, TILE), :], dh_send.at[src[tile], pl.ds(0, TILE), :], sems.at[tile]
        )
        for tile in range(TILES)
    ]
    for copy in sends:
        copy.start()
    w_grad = nt(hidden[...].T, dqkv_t[...]).astype(bf16)
    for peer in range(PEERS):
        for part in range(3):
            w_part[peer, part * 16 : part * 16 + 16, :] = w_grad[
                peer * 16 : peer * 16 + 16, part * C : part * C + C
            ]
    send_w = pltpu.make_async_copy(w_part, dh_send.at[:, pl.ds(TILE, W_ROWS), :], sems.at[TILES])
    send_w.start()
    for copy in sends + [send_w]:
        copy.wait()


def fold_kernel(back, w_send):
    w_sum = back[0, TILE:, :].astype(f32)
    for peer in range(1, PEERS):
        w_sum = w_sum + back[peer, TILE:, :].astype(f32)
    for place in range(COLUMN):
        for part in range(3):
            w_send[place, :, part * C : part * C + C] = w_sum[part * 16 : part * 16 + 16]


def residual_grad_kernel(
    dest, back, resid_far, cot_far, occ, gain, grad_far, masked_far, first, final, low, high,
    resid, cot, masked, sems,
):
    loads = []
    for tile in range(TILES):
        at = pl.ds(tile * TILE, TILE)
        loads.append([
            pltpu.make_async_copy(resid_far.at[at, :], resid.at[at, :], sems.at[2 * tile]),
            pltpu.make_async_copy(cot_far.at[at, :], cot.at[at, :], sems.at[2 * tile + 1]),
        ])
        for load in loads[tile]:
            load.start()
    columns = occupancy_columns(occ)
    moves = []
    for tile in range(TILES):
        for load in loads[tile]:
            load.wait()
        rows = slice(tile * TILE, (tile + 1) * TILE)
        residual = resid[rows, :]
        centre = jnp.mean(residual, axis=-1, keepdims=True)
        deviation = residual - centre
        variance = jnp.mean(deviation * deviation, axis=-1, keepdims=True)
        inv_std = lax.rsqrt(variance + norm_eps)
        normal = deviation * inv_std
        scaled = back[dest[tile] >> 3, :TILE, :].astype(f32) * gain[...]
        grad = cot[rows, :].astype(f32) + inv_std * (
            scaled
            - jnp.mean(scaled, axis=-1, keepdims=True)
            - normal * jnp.mean(scaled * normal, axis=-1, keepdims=True)
        )
        resid[rows, :] = grad
        masked[rows, :] = jnp.where(columns[:, tile : tile + 1] > 0.0, grad, 0.0).astype(bf16)
        at = pl.ds(tile * TILE, TILE)
        saves = [
            pltpu.make_async_copy(resid.at[at, :], grad_far.at[at, :], sems.at[2 * tile]),
            pltpu.make_async_copy(masked.at[at, :], masked_far.at[at, :], sems.at[2 * tile + 1]),
        ]
        for save in saves:
            save.start()
        moves += saves
    first[...] = masked[:32, :]
    final[...] = masked[PATCH - 32 :, :]
    sides = edge_columns(masked[...])
    low[...] = sides[:32]
    high[...] = sides[32:]
    for move in moves:
        move.wait()


def inside_grad_kernel(grad_far, masked_far, occ, weight, inside, grad, masked, shifts, sems):
    loads = [
        pltpu.make_async_copy(masked_far, masked, sems.at[0]),
        pltpu.make_async_copy(grad_far, grad, sems.at[1]),
    ]
    for load in loads:
        load.start()
    loads[0].wait()
    conv = inside_taps(True, masked[...].astype(f32), weight, shifts)
    columns = occupancy_columns(occ)
    loads[1].wait()
    moves = []
    for tile in range(TILES):
        rows = slice(tile * TILE, (tile + 1) * TILE)
        grad[rows, :] = grad[rows, :] + conv[rows] * columns[:, tile : tile + 1]
        at = pl.ds(tile * TILE, TILE)
        moves.append(pltpu.make_async_copy(grad.at[at, :], inside.at[at, :], sems.at[tile]))
        moves[-1].start()
    for move in moves:
        move.wait()


def conv_grad_kernel(inside, top, bottom, left, right, occ, weight, out, part, total, sem):
    load = pltpu.make_async_copy(inside, part, sem.at[0])
    load.start()
    total[...] = jnp.zeros((PATCH, C), f32)
    add_border(True, top, bottom, left, right, weight, total)
    columns = occupancy_columns(occ)
    load.wait()
    for tile in range(TILES):
        rows = slice(tile * TILE, (tile + 1) * TILE)
        out[rows, :] = (part[rows, :] + total[rows, :] * columns[:, tile : tile + 1]).astype(bf16)


def output_kernel(dest, back, resid, out):
    for tile in range(TILES):
        rows = slice(tile * TILE, (tile + 1) * TILE)
        out[rows, :] = (resid[rows, :] + back[dest[tile] >> 3].astype(f32)).astype(bf16)


def exchange(low_edge, high_edge, axis):
    count = lax.axis_size(axis)
    forward = [(i, i + 1) for i in range(count - 1)]
    backward = [(target, source) for source, target in forward]
    return lax.ppermute(high_edge, axis, forward), lax.ppermute(low_edge, axis, backward)


def halo(first, final, low, high):
    top, bottom = exchange(first, final, "gx")
    low = jnp.concatenate([top[:1], low, bottom[:1]], axis=0)
    high = jnp.concatenate([top[31:], high, bottom[31:]], axis=0)
    left, right = exchange(low, high, "gy")
    return top, bottom, left, right


def conv_inside(block, weight):
    return call(
        conv_inside_kernel, far((PATCH, C), f32), [WHOLE] * 2, FAR,
        [pltpu.VMEM((PATCH, C), f32), pltpu.VMEM((3, PATCH + 64, C), bf16), pltpu.SemaphoreType.DMA((1,))],
        name="conv_inside",
        cost=pl.CostEstimate(flops=1200 * 10**6, bytes_accessed=4 * 10**6, transcendentals=0),
    )(block, weight)


def after(array, other):
    return lax.optimization_barrier((array, other))[0]


def swap(array, axis="gx"):
    return lax.all_to_all(array, axis, split_axis=0, concat_axis=0, tiled=True)


PLAIN = [pltpu.VMEM((C, PATCH), bf16), pltpu.VMEM((C, PATCH), bf16), pltpu.VMEM((PATCH, 1), f32)]
BLOCKS = pltpu.VMEM((2, KEYS, LANES + HEAD), bf16)
OPERAND = pltpu.VMEM((PAIR, LANES + HEAD, PATCH), bf16)


def attend(src, h_recv, w_qkv, w_qkv_t, w_proj):
    saved = [((PATCH, C), bf16), ((C, PATCH), bf16), ((C, KEYS), bf16), ((KEYS, C), bf16)]
    return pl.pallas_call(
        attend_kernel,
        out_shape=[
            far((PEERS, TILE, C), bf16), far((HEADS, KEYS, PATCH), bf16), far((C, PATCH), f32),
            far(*saved[0]), struct((TILES, TILE), f32), struct((TILES, TILE), f32),
            far(*saved[1]), far(*saved[2]), far(*saved[3]), struct((1,), jnp.int32),
        ],
        in_specs=[SMEM] + [WHOLE] * 4,
        out_specs=[FAR, FAR, FAR, FAR, WHOLE, WHOLE, FAR, FAR, FAR, SMEM],
        scratch_shapes=[pltpu.VMEM((PATCH, C), bf16), pltpu.VMEM((C, PATCH), f32)]
        + [pltpu.VMEM(*one) for one in saved]
        + [pltpu.VMEM((C, KEYS), bf16), BLOCKS, OPERAND, pltpu.VMEM((2, PAIR, KEYS, PATCH), bf16)]
        + PLAIN + [pltpu.SemaphoreType.DMA((13,)), pltpu.SemaphoreType.DMA((2, PAIR))],
        name="attend",
        cost_estimate=pl.CostEstimate(flops=12 * 10**9, bytes_accessed=32 * 10**6, transcendentals=14 * 10**6),
        compiler_params=pltpu.CompilerParams(vmem_limit_bytes=LIMIT * MIB),
    )(src, h_recv, w_qkv, w_qkv_t, w_proj)


def attend_grad(src, fits, g_recv, w_qkv_t, w_proj, probs, o_t, hidden, live, place, q_t, k_t, v_nat):
    return pl.pallas_call(
        attend_grad_kernel,
        out_shape=far((PEERS, TILE + W_ROWS, C), bf16),
        in_specs=[SMEM, SMEM, FAR, WHOLE, WHOLE, FAR, FAR, FAR, WHOLE, WHOLE, FAR, FAR, FAR],
        out_specs=FAR,
        scratch_shapes=[
            pltpu.VMEM((C, PATCH), f32), pltpu.VMEM((PATCH, C), bf16), pltpu.VMEM((C, PATCH), bf16),
            pltpu.VMEM((C, KEYS), bf16), pltpu.VMEM((KEYS, C), bf16),
            pltpu.VMEM((PATCH, C), bf16), pltpu.VMEM((2, PAIR, KEYS, PATCH), bf16),
            pltpu.VMEM((C, PATCH), bf16), pltpu.VMEM((3 * C, PATCH), bf16), pltpu.VMEM((2 * C, KEYS), bf16),
            BLOCKS, OPERAND, pltpu.VMEM((PATCH, C), bf16), pltpu.VMEM((PEERS, W_ROWS, C), bf16),
        ] + PLAIN + [pltpu.SemaphoreType.DMA((TILES + 6,)), pltpu.SemaphoreType.DMA((2, PAIR))],
        name="attend_grad",
        cost_estimate=pl.CostEstimate(flops=24 * 10**9, bytes_accessed=32 * 10**6, transcendentals=0),
        compiler_params=pltpu.CompilerParams(vmem_limit_bytes=LIMIT * MIB),
    )(
        src, fits, pin(g_recv), w_qkv_t, w_proj, pin(probs), pin(o_t), pin(hidden), live, place,
        pin(q_t), pin(k_t), pin(v_nat),
    )


def local(features, occupied, conv_weight, norm_gain, w_qkv, w_proj, tile_dest, cotangent):
    size_x, size_y, feat_width = features.shape
    cells = size_x * size_y
    dest = tile_dest.reshape(TILES)
    occ = occupied.reshape(TILES, TILE)
    gain = norm_gain.reshape(1, C)
    feat = features.reshape(cells, C)
    cot = cotangent.reshape(cells, C)
    rows_f32 = struct((cells, C), f32)
    rows_bf16 = struct((cells, C), bf16)
    buckets = struct((PEERS, TILE, C), bf16)
    total = pltpu.VMEM((cells, C), f32)

    border = struct((32, C), bf16)
    masked, *edges = call(
        mask_kernel, [rows_bf16] + [border] * 4, [WHOLE] * 2, [WHOLE] * 5, name="mask"
    )(feat, occupied)
    edges = halo(*edges)
    conv = conv_inside(masked, conv_weight)
    resid, h_send = call(
        forward_kernel, [far((cells, C), f32), far((PEERS, TILE + META, C), bf16)],
        [SMEM, FAR] + [WHOLE] * 8, [FAR, FAR],
        [
            total, total, pltpu.VMEM((cells, C), bf16), pltpu.VMEM((PEERS, META, C), bf16),
            pltpu.SemaphoreType.DMA((2 + 2 * TILES,)),
        ],
        name="forward",
    )(dest, pin(conv), feat, *edges, occ, conv_weight, gain)
    h_recv = swap(h_send)
    flags = h_recv[:, TILE + 1, 0].astype(f32)
    order = jnp.arange(TILES, dtype=f32)
    peers = jnp.arange(PEERS, dtype=jnp.int32)
    ranks = jnp.sum(jnp.where(peers[None, :] < peers[:, None], flags[None, :], 0.0), axis=1)
    chosen = (ranks[None, :] == order[:, None]) & (flags[None, :] > 0.5)
    src = jnp.sum(jnp.where(chosen, peers[None, :], 0), axis=1)

    g_send = call(
        pack_kernel, far((PEERS, TILE, C), bf16), [SMEM, WHOLE], FAR, [pltpu.SemaphoreType.DMA((TILES,))], name="pack"
    )(dest, cot)
    g_send, h_recv = lax.optimization_barrier((g_send, h_recv))
    g_recv = swap(g_send)
    w_qkv_t = w_qkv.T
    att_send, probs, o_t, hidden, live, place, q_t, k_t, v_aug, fits = attend(src, h_recv, w_qkv, w_qkv_t, w_proj)
    att_back = swap(att_send)
    dh_send = attend_grad(src, fits, g_recv, w_qkv_t, w_proj, probs, o_t, hidden, live, place, q_t, k_t, v_aug)
    dh_send, att_back = lax.optimization_barrier((dh_send, att_back))
    dh_back = swap(dh_send)
    w_send = call(
        fold_kernel, far((COLUMN, 16, 3 * C), f32), [WHOLE], WHOLE, name="fold"
    )(dh_back)
    w_recv = swap(w_send, "gy")
    grad, grad_masked, *edges = call(
        residual_grad_kernel,
        [far((cells, C), f32), far((cells, C), bf16), border, border, border, border],
        [SMEM, WHOLE, FAR, FAR, WHOLE, WHOLE], [FAR] * 2 + [WHOLE] * 4,
        [
            total, pltpu.VMEM((cells, C), bf16), pltpu.VMEM((cells, C), bf16),
            pltpu.SemaphoreType.DMA((2 * TILES,)),
        ],
        name="residual_grad",
    )(dest, dh_back, pin(resid), pin(cot), occ, gain)
    grad_edges = halo(*edges)
    inside = call(
        inside_grad_kernel, far((cells, C), f32), [FAR, FAR, WHOLE, WHOLE], FAR,
        [
            total, pltpu.VMEM((cells, C), bf16), pltpu.VMEM((3, PATCH + 64, C), bf16),
            pltpu.SemaphoreType.DMA((TILES,)),
        ],
        name="inside_grad",
        cost=pl.CostEstimate(flops=1200 * 10**6, bytes_accessed=4 * 10**6, transcendentals=0),
    )(pin(grad), pin(grad_masked), occ, conv_weight)
    w_recv = after(w_recv, grad_edges[0])
    w_sum = (jnp.sum(w_recv, axis=0) / math.sqrt(131072)).astype(bf16)
    d_features = call(
        conv_grad_kernel, rows_bf16, [FAR] + [WHOLE] * 6, WHOLE,
        [total, total, pltpu.SemaphoreType.DMA((1,))], name="conv_grad",
    )(pin(inside), *grad_edges, occ, conv_weight)
    block_output = call(
        output_kernel, rows_bf16, [SMEM, WHOLE, WHOLE], WHOLE, name="output"
    )(dest, att_back, resid)
    w_grad = swap(jnp.broadcast_to(w_sum[None], (PEERS, 16, 3 * C))).reshape(C, 3 * C).astype(f32)
    shape = (size_x, size_y, feat_width)
    return (block_output.reshape(shape), d_features.reshape(shape), w_grad)


def solution(mesh):
    in_specs = (
        P("gx", "gy", None),
        P("gx", "gy"),
        P(),
        P(),
        P(),
        P(),
        P("gx", "gy"),
        P("gx", "gy", None),
    )
    out_specs = (P("gx", "gy", None), P("gx", "gy", None), P())
    return jax.shard_map(local, mesh=mesh, in_specs=in_specs, out_specs=out_specs, check_vma=False)
```

```python
import functools
import math

import jax
import jax.numpy as jnp
from jax import lax
from jax.experimental import pallas as pl
from jax.experimental.pallas import tpu as pltpu
from jax.sharding import PartitionSpec as P

C = 256
HEADS = 16
HEAD = 16
PATCH = 1024
TILE = 128
TILES = 8
PEERS = 16
META = 16
KEYS = 832
W_ROWS = 48
COLUMN = 8
PAIR = 2
LANES = 64
SHARE = LANES // HEAD
LIMIT = 40

norm_eps = 1e-05
mask_fill = 1000000000.0
LOG2E = 1.4426950408889634
BOUND2 = (4.0 * 40.0) ** 2

bf16 = jnp.bfloat16
f32 = jnp.float32
MIB = 2**20


def nn(a, b):
    return lax.dot_general(a, b, (((1,), (0,)), ((), ())), preferred_element_type=f32)


def nt(a, b):
    return lax.dot_general(a, b, (((1,), (1,)), ((), ())), preferred_element_type=f32)


def tn(a, b):
    return lax.dot_general(a, b, (((0,), (0,)), ((), ())), preferred_element_type=f32)


SMEM = pl.BlockSpec(memory_space=pltpu.SMEM)
WHOLE = pl.BlockSpec(memory_space=pltpu.VMEM)
FAR = pl.BlockSpec(memory_space=pltpu.HBM)


def far(shape, dtype):
    return pltpu.HBM(shape, dtype)


def pin(array):
    return pltpu.with_memory_space_constraint(array, pltpu.HBM)


def call(body, out_shape, in_specs, out_specs, scratch=(), name=None, cost=None, limit=16):
    return pl.pallas_call(
        body,
        out_shape=out_shape,
        in_specs=in_specs,
        out_specs=out_specs,
        scratch_shapes=list(scratch),
        name=name,
        cost_estimate=cost,
        compiler_params=pltpu.CompilerParams(vmem_limit_bytes=limit * MIB),
    )


def struct(shape, dtype):
    return jax.ShapeDtypeStruct(shape, dtype)


def pack_kernel(dest, cot, send, sems):
    moves = [
        pltpu.make_async_copy(cot.at[pl.ds(tile * TILE, TILE), :], send.at[dest[tile] >> 3], sems.at[tile])
        for tile in range(TILES)
    ]
    for move in moves:
        move.start()
    for move in moves:
        move.wait()


def edge_columns(block):
    edge = lax.broadcasted_iota(jnp.int32, (64, PATCH), 0)
    cell = lax.broadcasted_iota(jnp.int32, (64, PATCH), 1)
    wanted = jnp.where(edge < 32, edge * 32, (edge - 32) * 32 + 31)
    return nn((cell == wanted).astype(f32).astype(bf16), block).astype(bf16)


def mask_kernel(feat, occ, masked, first, final, low, high):
    live = occ[...].astype(f32)
    wide = jnp.concatenate([live, jnp.zeros((32, TILE - 32), f32)], axis=1)
    columns = jnp.concatenate([wide, jnp.zeros((TILE - 32, TILE), f32)], axis=0).T
    for line in range(32):
        rows = slice(line * 32, line * 32 + 32)
        kept = jnp.where(columns[:32, line : line + 1] > 0.0, feat[rows, :].astype(f32), 0.0)
        masked[rows, :] = kept.astype(bf16)
    first[...] = masked[:32, :]
    final[...] = masked[PATCH - 32 :, :]
    sides = edge_columns(masked[...])
    low[...] = sides[:32]
    high[...] = sides[32:]


def tap_dot(a, b, flip):
    return nt(a, b) if flip else nn(a, b)


def inside_taps(flip, block, weight, shifts):
    edge = jnp.zeros((32, C), f32)
    whole = jnp.concatenate([edge, block, edge], axis=0)
    total = whole.shape[0]
    col = lax.broadcasted_iota(jnp.int32, (total, C), 0) & 31
    shifts[0] = jnp.where(col == 0, 0.0, pltpu.roll(whole, 1, 0)).astype(bf16)
    shifts[1] = whole.astype(bf16)
    shifts[2] = jnp.where(col == 31, 0.0, pltpu.roll(whole, total - 1, 0)).astype(bf16)
    conv = None
    for a in range(3):
        for b in range(3):
            x, y = (2 - a, 2 - b) if flip else (a, b)
            term = tap_dot(shifts[y, x * 32 : x * 32 + PATCH, :], weight[a * 3 + b], flip)
            conv = term if conv is None else conv + term
    return conv


def conv_inside_kernel(block, weight, out, conv, shifts, sem):
    conv[...] = inside_taps(False, block[...].astype(f32), weight, shifts)
    save = pltpu.make_async_copy(conv, out, sem.at[0])
    save.start()
    save.wait()


def add_border(flip, top, bottom, left, right, weight, total):
    line = jnp.zeros((1, C), f32)
    first, last = (2, 0) if flip else (0, 2)

    def side(cells, taps):
        summed = None
        for k, tap in enumerate(taps):
            shift = 2 - k if flip else k
            term = tap_dot(cells[shift : shift + 32].astype(bf16), weight[tap], flip)
            summed = term if summed is None else summed + term
        return summed

    for edge, row, a in ((top, 0, first), (bottom, 31, last)):
        padded = jnp.concatenate([line, edge[...].astype(f32), line], axis=0)
        rows = slice(row * 32, row * 32 + 32)
        total[rows, :] = total[rows, :] + side(padded, [a * 3 + b for b in range(3)])
    for edge, col, b in ((left, 0, first), (right, 31, last)):
        added = side(edge[...].astype(f32), [a * 3 + b for a in range(3)])
        for i in range(32):
            at = slice(i * 32 + col, i * 32 + col + 1)
            total[at, :] = total[at, :] + added[i : i + 1]


def occupancy_columns(occ):
    live = occ[...].astype(f32)
    square = jnp.concatenate([live, jnp.zeros((TILE - TILES, TILE), f32)], axis=0)
    return square.T


def forward_kernel(
    dest, conv, feat, top, bottom, left, right, occ, weight, gain,
    resid_out, send, total, resid, hidden, meta, sems,
):
    load = pltpu.make_async_copy(conv, total, sems.at[1 + 2 * TILES])
    load.start()
    live = occ[...].astype(f32)
    row = lax.broadcasted_iota(jnp.int32, (META, C), 0)
    meta[...] = jnp.zeros(meta.shape, f32).astype(bf16)
    for tile in range(TILES):
        line = jnp.concatenate([live[tile : tile + 1], jnp.zeros((1, C - TILE), f32)], axis=1)
        meta[dest[tile] >> 3] = jnp.where(row == 0, line, 1.0).astype(bf16)
    moves = [pltpu.make_async_copy(meta, send.at[:, pl.ds(TILE, META), :], sems.at[0])]
    moves[0].start()
    load.wait()
    add_border(False, top, bottom, left, right, weight, total)
    columns = occupancy_columns(occ)
    for tile in range(TILES):
        rows = slice(tile * TILE, (tile + 1) * TILE)
        residual = feat[rows, :].astype(f32) + total[rows, :] * columns[:, tile : tile + 1]
        resid[rows, :] = residual
        centre = jnp.mean(residual, axis=-1, keepdims=True)
        deviation = residual - centre
        variance = jnp.mean(deviation * deviation, axis=-1, keepdims=True)
        hidden[rows, :] = (deviation * lax.rsqrt(variance + norm_eps) * gain[...]).astype(bf16)
        at = pl.ds(tile * TILE, TILE)
        for k, (source, target) in enumerate((
            (hidden.at[at, :], send.at[dest[tile] >> 3, pl.ds(0, TILE), :]),
            (resid.at[at, :], resid_out.at[at, :]),
        )):
            moves.append(pltpu.make_async_copy(source, target, sems.at[1 + 2 * tile + k]))
            moves[-1].start()
    for move in moves:
        move.wait()


def plain_forward(h, q_t, kf_t, vf_t, bias, o_t):
    block = 256
    at = pl.ds(pl.multiple_of(h * HEAD, HEAD), HEAD)
    key, value = kf_t[at, :], vf_t[at, :]

    def one_block(c, carry):
        cols = pl.ds(pl.multiple_of(c * block, block), block)
        scores = tn(key, q_t[at, cols]) * 0.25 + bias
        powers = jnp.exp(scores - jnp.max(scores, axis=0, keepdims=True))
        low = (powers / jnp.sum(powers, axis=0, keepdims=True)).astype(bf16)
        o_t[at, cols] = nn(value, low)
        return carry

    lax.fori_loop(0, PATCH // block, one_block, 0)


def plain_backward(h, q_t, kf_t, vf_t, dm_t, bias, dqkv_t):
    block = 256
    start = pl.multiple_of(h * HEAD, HEAD)
    at = pl.ds(start, HEAD)
    key, value = kf_t[at, :], vf_t[at, :]

    def one_block(c, sums):
        d_keys, d_values = sums
        cols = pl.ds(pl.multiple_of(c * block, block), block)
        query, d_mixed = q_t[at, cols], dm_t[at, cols]
        scores = tn(key, query) * 0.25 + bias
        powers = jnp.exp(scores - jnp.max(scores, axis=0, keepdims=True))
        probs = powers / jnp.sum(powers, axis=0, keepdims=True)
        low = probs.astype(bf16)
        d_probs = tn(value, d_mixed)
        inner = jnp.sum(d_probs * probs, axis=0, keepdims=True)
        d_scores = (probs * (d_probs - inner) * 0.25).astype(bf16)
        dqkv_t[at, cols] = nn(key, d_scores).astype(bf16)
        return (d_keys + nt(query, d_scores), d_values + nt(d_mixed, low))

    zero = jnp.zeros((HEAD, PATCH), f32)
    d_keys, d_values = lax.fori_loop(0, PATCH // block, one_block, (zero, zero))
    dqkv_t[pl.ds(start + C, HEAD), :] = d_keys.astype(bf16)
    dqkv_t[pl.ds(start + 2 * C, HEAD), :] = d_values.astype(bf16)


def plain_operands(hidden, live, w_qkv_t, kf_t, vf_t, bias):
    kf_t[...] = nt(w_qkv_t[C : 2 * C, :], hidden[...]).astype(bf16)
    vf_t[...] = nt(w_qkv_t[2 * C :, :], hidden[...]).astype(bf16)
    square = jnp.concatenate([live[...], jnp.zeros((TILE - TILES, TILE), f32)], axis=0).T
    column = jnp.concatenate([square[:, t : t + 1] for t in range(TILES)], axis=0)
    bias[...] = (column - 1.0) * mask_fill


def copies(pairs, sems):
    started = [pltpu.make_async_copy(source, target, sems.at[i]) for i, (source, target) in enumerate(pairs)]
    return started


def compaction(place):
    row = jnp.concatenate([place[t : t + 1, :] for t in range(TILES)], axis=1)
    key_index = lax.broadcasted_iota(jnp.int32, (KEYS, PATCH), 0).astype(f32)
    return (key_index == row).astype(f32).astype(bf16)


def by_blocks(blocks, array, extra):
    for block in range(C // LANES):
        blocks[block, :, :LANES] = array[:, block * LANES : block * LANES + LANES]
        blocks[block, :, LANES:] = extra


def place_head(operand, h, rows):
    own = pl.multiple_of((h & (SHARE - 1)) * HEAD, HEAD)
    before = pl.multiple_of(((h - PAIR) & (SHARE - 1)) * HEAD, HEAD)
    operand[pl.ds(before, HEAD), :] = jnp.zeros(rows.shape, rows.dtype)
    operand[pl.ds(own, HEAD), :] = rows


def head_rows(h, offset=0):
    return pl.ds(pl.multiple_of(h * HEAD + offset, HEAD), HEAD)


def attend_kernel(
    src, h_recv, w_qkv, w_qkv_t, w_proj,
    att_send, probs, o_out, hidden_out, live, place, q_out, k_out, v_out, fits,
    attended, o_t, hidden, q_t, k_t, v_nat, v_t, k_blocks, queries, low_t, kf_t, vf_t, bias, sems, p_sems,
):
    lives = []
    for tile in range(TILES):
        rows = slice(tile * TILE, (tile + 1) * TILE)
        hidden[rows, :] = h_recv[src[tile], :TILE, :]
        lives.append(h_recv[src[tile], TILE:, :].astype(f32)[0:1, :TILE])
    alive = jnp.concatenate(lives, axis=0)
    live[...] = alive
    lane_a = lax.broadcasted_iota(jnp.int32, (TILE, TILE), 0)
    lane_b = lax.broadcasted_iota(jnp.int32, (TILE, TILE), 1)
    counts = nn(alive.astype(bf16), (lane_a <= lane_b).astype(f32).astype(bf16))
    totals = jnp.broadcast_to(counts[:, TILE - 1 :], (TILES, TILE))
    line_a = lax.broadcasted_iota(jnp.int32, (TILES, TILES), 0)
    line_b = lax.broadcasted_iota(jnp.int32, (TILES, TILES), 1)
    before = nn((line_b < line_a).astype(f32).astype(bf16), totals.astype(bf16))
    place[...] = jnp.where(alive > 0.5, counts + before - 1.0, -1.0)
    live_count = jnp.sum(alive)

    q_t[...] = nt(w_qkv_t[:C, :], hidden[...]).astype(bf16)
    keys_in = nn(compaction(place), hidden[...]).astype(bf16)
    k_t[...] = nt(w_qkv_t[C : 2 * C, :], keys_in).astype(bf16)
    v_t[...] = nt(w_qkv_t[2 * C :, :], keys_in).astype(bf16)
    v_nat[...] = nn(keys_in, w_qkv[:, 2 * C :]).astype(bf16)
    saves = copies([(hidden, hidden_out), (q_t, q_out), (k_t, k_out), (v_nat, v_out)], sems)
    for copy in saves:
        copy.start()
    q_square = jnp.square(q_t[...].astype(f32)).reshape(HEADS, HEAD, PATCH)
    k_square = jnp.square(k_t[...].astype(f32)).reshape(HEADS, HEAD, KEYS)
    q_top = jnp.max(jnp.sum(q_square, axis=1))
    k_top = jnp.max(jnp.sum(k_square, axis=1))
    good = (live_count >= 1.0) & (live_count <= float(KEYS)) & (q_top * k_top <= BOUND2)
    fits[0] = good.astype(jnp.int32)

    def save_probs(slot, unit, h):
        return pltpu.make_async_copy(low_t.at[slot, unit], probs.at[h], p_sems.at[slot, unit])

    @pl.when(fits[0] == 1)
    def _():
        lane = lax.broadcasted_iota(jnp.int32, (KEYS, HEAD), 1)
        key = lax.broadcasted_iota(jnp.int32, (KEYS, HEAD), 0).astype(f32)
        empty = jnp.where((lane == 0) & (key >= live_count), -65536.0, 0.0).astype(bf16)
        by_blocks(k_blocks, nn(keys_in, w_qkv[:, C : 2 * C]).astype(bf16), empty)
        row = lax.broadcasted_iota(jnp.int32, (LANES + HEAD, PATCH), 0)
        for unit in range(PAIR):
            queries[unit] = (row == LANES).astype(f32).astype(bf16)

        def heads(i, carry):
            slot = i & 1

            @pl.when(i > 1)
            def _():
                for unit in range(PAIR):
                    save_probs(slot, unit, (i - 2) * PAIR + unit).wait()

            for unit in range(PAIR):
                h = i * PAIR + unit
                place_head(queries.at[unit], h, q_t[head_rows(h), :])
                scores = nn(k_blocks[h // SHARE], queries[unit])
                powers = jnp.exp2(scores * (0.25 * LOG2E))
                inverse = 1.0 / jnp.sum(powers, axis=0, keepdims=True)
                low = (powers * inverse).astype(bf16)
                low_t[slot, unit] = low
                if unit:
                    o_t[head_rows(h - 1), :] = nn(v_t[head_rows(h - 1), :], held)
                held = low
            o_t[head_rows(h), :] = nn(v_t[head_rows(h), :], held)
            for unit in range(PAIR):
                save_probs(slot, unit, i * PAIR + unit).start()
                at = head_rows(i * PAIR + unit)
                pltpu.make_async_copy(o_t.at[at, :], o_out.at[at, :], sems.at[4]).start()
            return carry

        lax.fori_loop(0, HEADS // PAIR, heads, 0)

    @pl.when(fits[0] == 0)
    def _():
        plain_operands(hidden, live, w_qkv_t, kf_t, vf_t, bias)

        def one_head(h, carry):
            plain_forward(h, q_t, kf_t, vf_t, bias[...], o_t)
            return carry

        lax.fori_loop(0, HEADS, one_head, 0)
        pltpu.make_async_copy(o_t, o_out, sems.at[4]).start()

    sends = []
    half = PATCH // 2
    for part in range(2):
        rows = slice(part * half, part * half + half)
        attended[rows, :] = tn(o_t[:, rows].astype(bf16), w_proj[...]).astype(bf16)
        for tile in range(part * TILES // 2, (part + 1) * TILES // 2):
            sends.append(
                pltpu.make_async_copy(
                    attended.at[pl.ds(tile * TILE, TILE), :], att_send.at[src[tile]], sems.at[5 + tile]
                )
            )
            sends[-1].start()
    for copy in saves + [pltpu.make_async_copy(o_t, o_out, sems.at[4])] + sends:
        copy.wait()

    @pl.when(fits[0] == 1)
    def _():
        for slot in range(2):
            for unit in range(PAIR):
                save_probs(slot, unit, HEADS - (2 - slot) * PAIR + unit).wait()


def attend_grad_kernel(
    src, fits, g_recv, w_qkv_t, w_proj, probs, o_far, hidden_far, live, place, q_far, k_far, v_far,
    dh_send,
    perm, o_t, hidden, q_t, k_t, v_nat, cot, low_t, dm_t, dqkv_t, dkv_t, v_blocks, d_mixes, d_hidden, w_part, kf_t, vf_t, bias, sems, p_sems,
):
    def load_probs(slot, unit, h):
        return pltpu.make_async_copy(probs.at[h], low_t.at[slot, unit], p_sems.at[slot, unit])

    loads = [
        pltpu.make_async_copy(g_recv.at[src[tile]], cot.at[pl.ds(tile * TILE, TILE), :], sems.at[tile])
        for tile in range(TILES)
    ]
    saved = [
        pltpu.make_async_copy(source, target, sems.at[TILES + 1 + i])
        for i, (source, target) in enumerate(
            [(v_far, v_nat), (q_far, q_t), (k_far, k_t), (o_far, o_t), (hidden_far, hidden)]
        )
    ]
    for copy in loads + saved[:4]:
        copy.start()

    @pl.when(fits[0] == 1)
    def _():
        for unit in range(PAIR):
            load_probs(0, unit, unit).start()

    saved[4].start()
    perm[...] = compaction(place)
    for copy in loads:
        copy.wait()
    dm_t[...] = nt(w_proj[...], cot[...]).astype(bf16)
    for copy in saved:
        copy.wait()

    @pl.when(fits[0] == 1)
    def _():
        lane = lax.broadcasted_iota(jnp.int32, (KEYS, HEAD), 1)
        by_blocks(v_blocks, v_nat, (lane < 2).astype(f32).astype(bf16))
        for unit in range(PAIR):
            d_mixes[unit] = jnp.zeros((LANES + HEAD, PATCH), f32).astype(bf16)
        rows = lax.broadcasted_iota(jnp.int32, (HEAD, PATCH), 0)

        def heads(i, carry):
            slot = i & 1

            @pl.when(i < HEADS // PAIR - 1)
            def _():
                for unit in range(PAIR):
                    load_probs(1 - slot, unit, (i + 1) * PAIR + unit).start()

            for unit in range(PAIR):
                load_probs(slot, unit, i * PAIR + unit).wait()
            for unit in range(PAIR):
                h = i * PAIR + unit
                at = head_rows(h)
                d_mixed, query = dm_t[at, :], q_t[at, :]
                inner = jnp.sum(d_mixed.astype(f32) * o_t[at, :], axis=0, keepdims=True)
                high = inner.astype(bf16).astype(f32)
                place_head(d_mixes.at[unit], h, d_mixed)
                d_mixes[unit, LANES:, :] = jnp.where(
                    rows == 0, -high, jnp.where(rows == 1, high - inner, 0.0)
                ).astype(bf16)
                low = low_t[slot, unit]
                dkv_t[head_rows(h, C), :] = nt(d_mixed, low).astype(bf16)
                centred = nn(v_blocks[h // SHARE], d_mixes[unit])
                d_scores = (low.astype(f32) * centred).astype(bf16)
                dkv_t[at, :] = (nt(query, d_scores) * 0.25).astype(bf16)
                dqkv_t[at, :] = (nn(k_t[at, :], d_scores) * 0.25).astype(bf16)
            return carry

        lax.fori_loop(0, HEADS // PAIR, heads, 0)
        dqkv_t[C:, :] = nn(dkv_t[...], perm[...]).astype(bf16)

    @pl.when(fits[0] == 0)
    def _():
        plain_operands(hidden, live, w_qkv_t, kf_t, vf_t, bias)

        def one_head(h, carry):
            plain_backward(h, q_t, kf_t, vf_t, dm_t, bias[...], dqkv_t)
            return carry

        lax.fori_loop(0, HEADS, one_head, 0)

    w_grad = nt(hidden[...].T, dqkv_t[...]).astype(bf16)
    for peer in range(PEERS):
        for part in range(3):
            w_part[peer, part * 16 : part * 16 + 16, :] = w_grad[
                peer * 16 : peer * 16 + 16, part * C : part * C + C
            ]
    send_w = pltpu.make_async_copy(w_part, dh_send.at[:, pl.ds(TILE, W_ROWS), :], sems.at[TILES])
    send_w.start()
    sends = [send_w]
    half = PATCH // 2
    for part in range(2):
        rows = slice(part * half, part * half + half)
        d_hidden[rows, :] = tn(dqkv_t[:, rows], w_qkv_t[...]).astype(bf16)
        for tile in range(part * TILES // 2, (part + 1) * TILES // 2):
            sends.append(
                pltpu.make_async_copy(
                    d_hidden.at[pl.ds(tile * TILE, TILE), :], dh_send.at[src[tile], pl.ds(0, TILE), :], sems.at[tile]
                )
            )
            sends[-1].start()
    for copy in sends:
        copy.wait()


def fold_kernel(back, w_send):
    w_sum = back[0, TILE:, :].astype(f32)
    for peer in range(1, PEERS):
        w_sum = w_sum + back[peer, TILE:, :].astype(f32)
    for place in range(COLUMN):
        for part in range(3):
            w_send[place, :, part * C : part * C + C] = w_sum[part * 16 : part * 16 + 16]


def residual_grad_kernel(
    dest, back, resid_far, cot_far, occ, gain, grad_far, first, final, low, high,
    resid, cot, masked, sems,
):
    loads = []
    for tile in range(TILES):
        at = pl.ds(tile * TILE, TILE)
        loads.append([
            pltpu.make_async_copy(resid_far.at[at, :], resid.at[at, :], sems.at[2 * tile]),
            pltpu.make_async_copy(cot_far.at[at, :], cot.at[at, :], sems.at[2 * tile + 1]),
        ])
        for load in loads[tile]:
            load.start()
    columns = occupancy_columns(occ)
    moves = []
    for tile in range(TILES):
        for load in loads[tile]:
            load.wait()
        rows = slice(tile * TILE, (tile + 1) * TILE)
        residual = resid[rows, :]
        centre = jnp.mean(residual, axis=-1, keepdims=True)
        deviation = residual - centre
        variance = jnp.mean(deviation * deviation, axis=-1, keepdims=True)
        inv_std = lax.rsqrt(variance + norm_eps)
        normal = deviation * inv_std
        scaled = back[dest[tile] >> 3, :TILE, :].astype(f32) * gain[...]
        grad = cot[rows, :].astype(f32) + inv_std * (
            scaled
            - jnp.mean(scaled, axis=-1, keepdims=True)
            - normal * jnp.mean(scaled * normal, axis=-1, keepdims=True)
        )
        resid[rows, :] = grad
        masked[rows, :] = jnp.where(columns[:, tile : tile + 1] > 0.0, grad, 0.0).astype(bf16)
        at = pl.ds(tile * TILE, TILE)
        moves.append(pltpu.make_async_copy(resid.at[at, :], grad_far.at[at, :], sems.at[2 * tile]))
        moves[-1].start()
    first[...] = masked[:32, :]
    final[...] = masked[PATCH - 32 :, :]
    sides = edge_columns(masked[...])
    low[...] = sides[:32]
    high[...] = sides[32:]
    for move in moves:
        move.wait()


def inside_grad_kernel(grad_far, occ, weight, inside, grad, masked, shifts, sems):
    loads = [
        pltpu.make_async_copy(grad_far.at[pl.ds(tile * TILE, TILE), :], grad.at[pl.ds(tile * TILE, TILE), :], sems.at[tile])
        for tile in range(TILES)
    ]
    for load in loads:
        load.start()
    columns = occupancy_columns(occ)
    for tile in range(TILES):
        loads[tile].wait()
        rows = slice(tile * TILE, (tile + 1) * TILE)
        masked[rows, :] = jnp.where(columns[:, tile : tile + 1] > 0.0, grad[rows, :], 0.0)
    conv = inside_taps(True, masked[...], weight, shifts)
    moves = []
    for tile in range(TILES):
        rows = slice(tile * TILE, (tile + 1) * TILE)
        grad[rows, :] = grad[rows, :] + conv[rows] * columns[:, tile : tile + 1]
        at = pl.ds(tile * TILE, TILE)
        moves.append(pltpu.make_async_copy(grad.at[at, :], inside.at[at, :], sems.at[tile]))
        moves[-1].start()
    for move in moves:
        move.wait()


def conv_grad_kernel(inside, top, bottom, left, right, occ, weight, out, part, total, sem):
    load = pltpu.make_async_copy(inside, part, sem.at[0])
    load.start()
    total[...] = jnp.zeros((PATCH, C), f32)
    add_border(True, top, bottom, left, right, weight, total)
    columns = occupancy_columns(occ)
    load.wait()
    for tile in range(TILES):
        rows = slice(tile * TILE, (tile + 1) * TILE)
        out[rows, :] = (part[rows, :] + total[rows, :] * columns[:, tile : tile + 1]).astype(bf16)


def output_kernel(dest, back, resid, out):
    for tile in range(TILES):
        rows = slice(tile * TILE, (tile + 1) * TILE)
        out[rows, :] = (resid[rows, :] + back[dest[tile] >> 3].astype(f32)).astype(bf16)


def exchange(low_edge, high_edge, axis):
    count = lax.axis_size(axis)
    forward = [(i, i + 1) for i in range(count - 1)]
    backward = [(target, source) for source, target in forward]
    return lax.ppermute(high_edge, axis, forward), lax.ppermute(low_edge, axis, backward)


def halo(first, final, low, high):
    top, bottom = exchange(first, final, "gx")
    low = jnp.concatenate([top[:1], low, bottom[:1]], axis=0)
    high = jnp.concatenate([top[31:], high, bottom[31:]], axis=0)
    left, right = exchange(low, high, "gy")
    return top, bottom, left, right


def conv_inside(block, weight):
    return call(
        conv_inside_kernel, far((PATCH, C), f32), [WHOLE] * 2, FAR,
        [pltpu.VMEM((PATCH, C), f32), pltpu.VMEM((3, PATCH + 64, C), bf16), pltpu.SemaphoreType.DMA((1,))],
        name="conv_inside",
        cost=pl.CostEstimate(flops=1200 * 10**6, bytes_accessed=4 * 10**6, transcendentals=0),
    )(block, weight)


def after(array, *others):
    return lax.optimization_barrier((array, *others))[0]


def swap(array, axis="gx"):
    return lax.all_to_all(array, axis, split_axis=0, concat_axis=0, tiled=True)


PLAIN = [pltpu.VMEM((C, PATCH), bf16), pltpu.VMEM((C, PATCH), bf16), pltpu.VMEM((PATCH, 1), f32)]
BLOCKS = pltpu.VMEM((C // LANES, KEYS, LANES + HEAD), bf16)
OPERAND = pltpu.VMEM((PAIR, LANES + HEAD, PATCH), bf16)


def attend(src, h_recv, w_qkv, w_qkv_t, w_proj):
    saved = [((PATCH, C), bf16), ((C, PATCH), bf16), ((C, KEYS), bf16), ((KEYS, C), bf16)]
    return pl.pallas_call(
        attend_kernel,
        out_shape=[
            far((PEERS, TILE, C), bf16), far((HEADS, KEYS, PATCH), bf16), far((C, PATCH), f32),
            far(*saved[0]), struct((TILES, TILE), f32), struct((TILES, TILE), f32),
            far(*saved[1]), far(*saved[2]), far(*saved[3]), struct((1,), jnp.int32),
        ],
        in_specs=[SMEM] + [WHOLE] * 4,
        out_specs=[FAR, FAR, FAR, FAR, WHOLE, WHOLE, FAR, FAR, FAR, SMEM],
        scratch_shapes=[pltpu.VMEM((PATCH, C), bf16), pltpu.VMEM((C, PATCH), f32)]
        + [pltpu.VMEM(*one) for one in saved]
        + [pltpu.VMEM((C, KEYS), bf16), BLOCKS, OPERAND, pltpu.VMEM((2, PAIR, KEYS, PATCH), bf16)]
        + PLAIN + [pltpu.SemaphoreType.DMA((13,)), pltpu.SemaphoreType.DMA((2, PAIR))],
        name="attend",
        cost_estimate=pl.CostEstimate(flops=12 * 10**9, bytes_accessed=32 * 10**6, transcendentals=14 * 10**6),
        compiler_params=pltpu.CompilerParams(vmem_limit_bytes=LIMIT * MIB),
    )(src, h_recv, w_qkv, w_qkv_t, w_proj)


def attend_grad(src, fits, g_recv, w_qkv_t, w_proj, probs, o_t, hidden, live, place, q_t, k_t, v_nat):
    return pl.pallas_call(
        attend_grad_kernel,
        out_shape=far((PEERS, TILE + W_ROWS, C), bf16),
        in_specs=[SMEM, SMEM, FAR, WHOLE, WHOLE, FAR, FAR, FAR, WHOLE, WHOLE, FAR, FAR, FAR],
        out_specs=FAR,
        scratch_shapes=[
            pltpu.VMEM((KEYS, PATCH), bf16),
            pltpu.VMEM((C, PATCH), f32), pltpu.VMEM((PATCH, C), bf16), pltpu.VMEM((C, PATCH), bf16),
            pltpu.VMEM((C, KEYS), bf16), pltpu.VMEM((KEYS, C), bf16),
            pltpu.VMEM((PATCH, C), bf16), pltpu.VMEM((2, PAIR, KEYS, PATCH), bf16),
            pltpu.VMEM((C, PATCH), bf16), pltpu.VMEM((3 * C, PATCH), bf16), pltpu.VMEM((2 * C, KEYS), bf16),
            BLOCKS, OPERAND, pltpu.VMEM((PATCH, C), bf16), pltpu.VMEM((PEERS, W_ROWS, C), bf16),
        ] + PLAIN + [pltpu.SemaphoreType.DMA((TILES + 6,)), pltpu.SemaphoreType.DMA((2, PAIR))],
        name="attend_grad",
        cost_estimate=pl.CostEstimate(flops=24 * 10**9, bytes_accessed=32 * 10**6, transcendentals=0),
        compiler_params=pltpu.CompilerParams(vmem_limit_bytes=LIMIT * MIB),
    )(
        src, fits, pin(g_recv), w_qkv_t, w_proj, pin(probs), pin(o_t), pin(hidden), live, place,
        pin(q_t), pin(k_t), pin(v_nat),
    )


def local(features, occupied, conv_weight, norm_gain, w_qkv, w_proj, tile_dest, cotangent):
    size_x, size_y, feat_width = features.shape
    cells = size_x * size_y
    dest = tile_dest.reshape(TILES)
    occ = occupied.reshape(TILES, TILE)
    gain = norm_gain.reshape(1, C)
    feat = features.reshape(cells, C)
    cot = cotangent.reshape(cells, C)
    rows_f32 = struct((cells, C), f32)
    rows_bf16 = struct((cells, C), bf16)
    buckets = struct((PEERS, TILE, C), bf16)
    total = pltpu.VMEM((cells, C), f32)

    border = struct((32, C), bf16)
    masked, *edges = call(
        mask_kernel, [rows_bf16] + [border] * 4, [WHOLE] * 2, [WHOLE] * 5, name="mask"
    )(feat, occupied)
    edges = halo(*edges)
    conv = conv_inside(masked, conv_weight)
    resid, h_send = call(
        forward_kernel, [far((cells, C), f32), far((PEERS, TILE + META, C), bf16)],
        [SMEM, FAR] + [WHOLE] * 8, [FAR, FAR],
        [
            total, total, pltpu.VMEM((cells, C), bf16), pltpu.VMEM((PEERS, META, C), bf16),
            pltpu.SemaphoreType.DMA((2 + 2 * TILES,)),
        ],
        name="forward",
    )(dest, pin(conv), feat, *edges, occ, conv_weight, gain)
    h_recv = swap(h_send)
    flags = h_recv[:, TILE + 1, 0].astype(f32)
    order = jnp.arange(TILES, dtype=f32)
    peers = jnp.arange(PEERS, dtype=jnp.int32)
    ranks = jnp.sum(jnp.where(peers[None, :] < peers[:, None], flags[None, :], 0.0), axis=1)
    chosen = (ranks[None, :] == order[:, None]) & (flags[None, :] > 0.5)
    src = jnp.sum(jnp.where(chosen, peers[None, :], 0), axis=1)

    g_send = call(
        pack_kernel, far((PEERS, TILE, C), bf16), [SMEM, WHOLE], FAR, [pltpu.SemaphoreType.DMA((TILES,))], name="pack"
    )(dest, cot)
    g_send, h_recv = lax.optimization_barrier((g_send, h_recv))
    g_recv = swap(g_send)
    w_qkv_t = w_qkv.T
    att_send, probs, o_t, hidden, live, place, q_t, k_t, v_aug, fits = attend(src, h_recv, w_qkv, w_qkv_t, w_proj)
    att_back = swap(att_send)
    dh_send = attend_grad(src, fits, g_recv, w_qkv_t, w_proj, probs, o_t, hidden, live, place, q_t, k_t, v_aug)
    dh_send, att_back = lax.optimization_barrier((dh_send, att_back))
    dh_back = swap(dh_send)
    w_send = call(
        fold_kernel, far((COLUMN, 16, 3 * C), f32), [WHOLE], WHOLE, name="fold"
    )(dh_back)
    w_recv = swap(w_send, "gy")
    grad, *edges = call(
        residual_grad_kernel,
        [far((cells, C), f32), border, border, border, border],
        [SMEM, WHOLE, FAR, FAR, WHOLE, WHOLE], [FAR] + [WHOLE] * 4,
        [
            total, pltpu.VMEM((cells, C), bf16), pltpu.VMEM((cells, C), bf16),
            pltpu.SemaphoreType.DMA((2 * TILES,)),
        ],
        name="residual_grad",
    )(dest, dh_back, pin(resid), pin(cot), occ, gain)
    grad_edges = halo(*edges)
    inside = call(
        inside_grad_kernel, far((cells, C), f32), [FAR, WHOLE, WHOLE], FAR,
        [total, total, pltpu.VMEM((3, PATCH + 64, C), bf16), pltpu.SemaphoreType.DMA((TILES,))],
        name="inside_grad",
        cost=pl.CostEstimate(flops=1200 * 10**6, bytes_accessed=4 * 10**6, transcendentals=0),
    )(pin(grad), occ, conv_weight)
    w_recv = after(w_recv, grad_edges[0])
    w_sum = (jnp.sum(w_recv, axis=0) / math.sqrt(131072)).astype(bf16)
    d_features = call(
        conv_grad_kernel, rows_bf16, [FAR] + [WHOLE] * 6, WHOLE,
        [total, total, pltpu.SemaphoreType.DMA((1,))], name="conv_grad",
    )(pin(inside), *grad_edges, occ, conv_weight)
    block_output = call(
        output_kernel, rows_bf16, [SMEM, WHOLE, WHOLE], WHOLE, name="output"
    )(dest, att_back, resid)
    w_grad = swap(jnp.broadcast_to(w_sum[None], (PEERS, 16, 3 * C))).reshape(C, 3 * C).astype(f32)
    shape = (size_x, size_y, feat_width)
    return (block_output.reshape(shape), d_features.reshape(shape), w_grad)


def solution(mesh):
    in_specs = (
        P("gx", "gy", None),
        P("gx", "gy"),
        P(),
        P(),
        P(),
        P(),
        P("gx", "gy"),
        P("gx", "gy", None),
    )
    out_specs = (P("gx", "gy", None), P("gx", "gy", None), P())
    return jax.shard_map(local, mesh=mesh, in_specs=in_specs, out_specs=out_specs, check_vma=False)
```

```python
import functools
import math

import jax
import jax.numpy as jnp
from jax import lax
from jax.experimental import pallas as pl
from jax.experimental.pallas import tpu as pltpu
from jax.sharding import PartitionSpec as P

C = 256
HEADS = 16
HEAD = 16
PATCH = 1024
TILE = 128
TILES = 8
PEERS = 16
META = 16
KEYS = 832
W_ROWS = 48
COLUMN = 8
PAIR = 2
LANES = 64
SHARE = LANES // HEAD
LIMIT = 40

norm_eps = 1e-05
mask_fill = 1000000000.0
LOG2E = 1.4426950408889634
BOUND2 = (4.0 * 80.0) ** 2

bf16 = jnp.bfloat16
f32 = jnp.float32
MIB = 2**20


def nn(a, b):
    return lax.dot_general(a, b, (((1,), (0,)), ((), ())), preferred_element_type=f32)


def nt(a, b):
    return lax.dot_general(a, b, (((1,), (1,)), ((), ())), preferred_element_type=f32)


def tn(a, b):
    return lax.dot_general(a, b, (((0,), (0,)), ((), ())), preferred_element_type=f32)


SMEM = pl.BlockSpec(memory_space=pltpu.SMEM)
WHOLE = pl.BlockSpec(memory_space=pltpu.VMEM)
FAR = pl.BlockSpec(memory_space=pltpu.HBM)


def far(shape, dtype):
    return pltpu.HBM(shape, dtype)


def pin(array):
    return pltpu.with_memory_space_constraint(array, pltpu.HBM)


def call(body, out_shape, in_specs, out_specs, scratch=(), name=None, cost=None, limit=16):
    return pl.pallas_call(
        body,
        out_shape=out_shape,
        in_specs=in_specs,
        out_specs=out_specs,
        scratch_shapes=list(scratch),
        name=name,
        cost_estimate=cost,
        compiler_params=pltpu.CompilerParams(vmem_limit_bytes=limit * MIB),
    )


def struct(shape, dtype):
    return jax.ShapeDtypeStruct(shape, dtype)


def pack_kernel(dest, cot, send, sems):
    moves = [
        pltpu.make_async_copy(cot.at[pl.ds(tile * TILE, TILE), :], send.at[dest[tile] >> 3], sems.at[tile])
        for tile in range(TILES)
    ]
    for move in moves:
        move.start()
    for move in moves:
        move.wait()


def edge_columns(block):
    edge = lax.broadcasted_iota(jnp.int32, (64, PATCH), 0)
    cell = lax.broadcasted_iota(jnp.int32, (64, PATCH), 1)
    wanted = jnp.where(edge < 32, edge * 32, (edge - 32) * 32 + 31)
    return nn((cell == wanted).astype(f32).astype(bf16), block).astype(bf16)


def mask_kernel(feat_far, occ_far, masked, first, final, low, high, feat, occ, sems):
    parts = 4
    size = PATCH // parts
    loads = [pltpu.make_async_copy(occ_far, occ, sems.at[parts])] + [
        pltpu.make_async_copy(feat_far.at[pl.ds(k * size, size), :], feat.at[pl.ds(k * size, size), :], sems.at[k])
        for k in range(parts)
    ]
    for load in loads:
        load.start()
    loads[0].wait()
    live = occ[...].astype(f32)
    wide = jnp.concatenate([live, jnp.zeros((32, TILE - 32), f32)], axis=1)
    columns = jnp.concatenate([wide, jnp.zeros((TILE - 32, TILE), f32)], axis=0).T
    for line in range(32):
        if line * 32 % size == 0:
            loads[1 + line * 32 // size].wait()
        rows = slice(line * 32, line * 32 + 32)
        kept = jnp.where(columns[:32, line : line + 1] > 0.0, feat[rows, :].astype(f32), 0.0)
        masked[rows, :] = kept.astype(bf16)
    first[...] = masked[:32, :]
    final[...] = masked[PATCH - 32 :, :]
    sides = edge_columns(masked[...])
    low[...] = sides[:32]
    high[...] = sides[32:]


def tap_dot(a, b, flip):
    return nt(a, b) if flip else nn(a, b)


def inside_taps(flip, block, weight, shifts):
    edge = jnp.zeros((32, C), f32)
    whole = jnp.concatenate([edge, block, edge], axis=0)
    total = whole.shape[0]
    col = lax.broadcasted_iota(jnp.int32, (total, C), 0) & 31
    shifts[0] = jnp.where(col == 0, 0.0, pltpu.roll(whole, 1, 0)).astype(bf16)
    shifts[1] = whole.astype(bf16)
    shifts[2] = jnp.where(col == 31, 0.0, pltpu.roll(whole, total - 1, 0)).astype(bf16)
    conv = None
    for a in range(3):
        for b in range(3):
            x, y = (2 - a, 2 - b) if flip else (a, b)
            term = tap_dot(shifts[y, x * 32 : x * 32 + PATCH, :], weight[a * 3 + b], flip)
            conv = term if conv is None else conv + term
    return conv


def conv_inside_kernel(block, weight, out, conv, shifts, sem):
    conv[...] = inside_taps(False, block[...].astype(f32), weight, shifts)
    save = pltpu.make_async_copy(conv, out, sem.at[0])
    save.start()
    save.wait()


def border_sums(flip, top, bottom, left, right, weight):
    line = jnp.zeros((1, C), f32)
    first, last = (2, 0) if flip else (0, 2)

    def side(cells, taps):
        summed = None
        for k, tap in enumerate(taps):
            shift = 2 - k if flip else k
            term = tap_dot(cells[shift : shift + 32].astype(bf16), weight[tap], flip)
            summed = term if summed is None else summed + term
        return summed

    rows = []
    for edge, a in ((top, first), (bottom, last)):
        padded = jnp.concatenate([line, edge[...].astype(f32), line], axis=0)
        rows.append(side(padded, [a * 3 + b for b in range(3)]))
    columns = []
    for edge, b in ((left, first), (right, last)):
        columns.append(side(edge[...].astype(f32), [a * 3 + b for a in range(3)]))
    return rows, columns


def add_border(sums, total):
    rows, columns = sums
    for added, line in zip(rows, (0, 31)):
        at = slice(line * 32, line * 32 + 32)
        total[at, :] = total[at, :] + added
    for added, col in zip(columns, (0, 31)):
        for i in range(32):
            at = slice(i * 32 + col, i * 32 + col + 1)
            total[at, :] = total[at, :] + added[i : i + 1]


def occupancy_columns(occ):
    live = occ[...].astype(f32)
    square = jnp.concatenate([live, jnp.zeros((TILE - TILES, TILE), f32)], axis=0)
    return square.T


def forward_kernel(
    dest, conv, feat, top, bottom, left, right, occ, weight, gain,
    resid_out, send, total, resid, hidden, meta, sems,
):
    load = pltpu.make_async_copy(conv, total, sems.at[1 + 2 * TILES])
    load.start()
    live = occ[...].astype(f32)
    row = lax.broadcasted_iota(jnp.int32, (META, C), 0)
    meta[...] = jnp.zeros(meta.shape, f32).astype(bf16)
    for tile in range(TILES):
        line = jnp.concatenate([live[tile : tile + 1], jnp.zeros((1, C - TILE), f32)], axis=1)
        meta[dest[tile] >> 3] = jnp.where(row == 0, line, 1.0).astype(bf16)
    moves = [pltpu.make_async_copy(meta, send.at[:, pl.ds(TILE, META), :], sems.at[0])]
    moves[0].start()
    sums = border_sums(False, top, bottom, left, right, weight)
    columns = occupancy_columns(occ)
    load.wait()
    add_border(sums, total)
    for tile in range(TILES):
        rows = slice(tile * TILE, (tile + 1) * TILE)
        residual = feat[rows, :].astype(f32) + total[rows, :] * columns[:, tile : tile + 1]
        resid[rows, :] = residual
        centre = jnp.mean(residual, axis=-1, keepdims=True)
        deviation = residual - centre
        variance = jnp.mean(deviation * deviation, axis=-1, keepdims=True)
        hidden[rows, :] = (deviation * lax.rsqrt(variance + norm_eps) * gain[...]).astype(bf16)
        at = pl.ds(tile * TILE, TILE)
        for k, (source, target) in enumerate((
            (hidden.at[at, :], send.at[dest[tile] >> 3, pl.ds(0, TILE), :]),
            (resid.at[at, :], resid_out.at[at, :]),
        )):
            moves.append(pltpu.make_async_copy(source, target, sems.at[1 + 2 * tile + k]))
            moves[-1].start()
    for move in moves:
        move.wait()


def plain_forward(h, q_t, kf_t, vf_t, bias, o_t):
    block = 256
    at = pl.ds(pl.multiple_of(h * HEAD, HEAD), HEAD)
    key, value = kf_t[at, :], vf_t[at, :]

    def one_block(c, carry):
        cols = pl.ds(pl.multiple_of(c * block, block), block)
        scores = tn(key, q_t[at, cols]) * 0.25 + bias
        powers = jnp.exp(scores - jnp.max(scores, axis=0, keepdims=True))
        low = (powers / jnp.sum(powers, axis=0, keepdims=True)).astype(bf16)
        o_t[at, cols] = nn(value, low)
        return carry

    lax.fori_loop(0, PATCH // block, one_block, 0)


def plain_backward(h, q_t, kf_t, vf_t, dm_t, bias, dqkv_t):
    block = 256
    start = pl.multiple_of(h * HEAD, HEAD)
    at = pl.ds(start, HEAD)
    key, value = kf_t[at, :], vf_t[at, :]

    def one_block(c, sums):
        d_keys, d_values = sums
        cols = pl.ds(pl.multiple_of(c * block, block), block)
        query, d_mixed = q_t[at, cols], dm_t[at, cols]
        scores = tn(key, query) * 0.25 + bias
        powers = jnp.exp(scores - jnp.max(scores, axis=0, keepdims=True))
        probs = powers / jnp.sum(powers, axis=0, keepdims=True)
        low = probs.astype(bf16)
        d_probs = tn(value, d_mixed)
        inner = jnp.sum(d_probs * probs, axis=0, keepdims=True)
        d_scores = (probs * (d_probs - inner) * 0.25).astype(bf16)
        dqkv_t[at, cols] = nn(key, d_scores).astype(bf16)
        return (d_keys + nt(query, d_scores), d_values + nt(d_mixed, low))

    zero = jnp.zeros((HEAD, PATCH), f32)
    d_keys, d_values = lax.fori_loop(0, PATCH // block, one_block, (zero, zero))
    dqkv_t[pl.ds(start + C, HEAD), :] = d_keys.astype(bf16)
    dqkv_t[pl.ds(start + 2 * C, HEAD), :] = d_values.astype(bf16)


def plain_operands(hidden, live, w_qkv_t, kf_t, vf_t, bias):
    kf_t[...] = nt(w_qkv_t[C : 2 * C, :], hidden[...]).astype(bf16)
    vf_t[...] = nt(w_qkv_t[2 * C :, :], hidden[...]).astype(bf16)
    square = jnp.concatenate([live[...], jnp.zeros((TILE - TILES, TILE), f32)], axis=0).T
    column = jnp.concatenate([square[:, t : t + 1] for t in range(TILES)], axis=0)
    bias[...] = (column - 1.0) * mask_fill


def copies(pairs, sems):
    started = [pltpu.make_async_copy(source, target, sems.at[i]) for i, (source, target) in enumerate(pairs)]
    return started


def compaction(place):
    row = jnp.concatenate([place[t : t + 1, :] for t in range(TILES)], axis=1)
    key_index = lax.broadcasted_iota(jnp.int32, (KEYS, PATCH), 0).astype(f32)
    return (key_index == row).astype(f32).astype(bf16)


def by_blocks(blocks, array, extra):
    for block in range(C // LANES):
        blocks[block, :, :LANES] = array[:, block * LANES : block * LANES + LANES]
        blocks[block, :, LANES:] = extra


def place_head(operand, h, rows):
    own = pl.multiple_of((h & (SHARE - 1)) * HEAD, HEAD)
    before = pl.multiple_of(((h - PAIR) & (SHARE - 1)) * HEAD, HEAD)
    operand[pl.ds(before, HEAD), :] = jnp.zeros(rows.shape, rows.dtype)
    operand[pl.ds(own, HEAD), :] = rows


def head_rows(h, offset=0):
    return pl.ds(pl.multiple_of(h * HEAD + offset, HEAD), HEAD)


def attend_kernel(
    src, h_recv, w_qkv, w_qkv_t, w_proj,
    att_send, probs, o_out, hidden_out, live, place, q_out, k_out, v_out, fits,
    attended, o_t, hidden, q_t, k_t, v_nat, v_t, k_blocks, queries, low_t, kf_t, vf_t, bias, sems, p_sems,
):
    lives = []
    for tile in range(TILES):
        rows = slice(tile * TILE, (tile + 1) * TILE)
        hidden[rows, :] = h_recv[src[tile], :TILE, :]
        lives.append(h_recv[src[tile], TILE:, :].astype(f32)[0:1, :TILE])
    alive = jnp.concatenate(lives, axis=0)
    live[...] = alive
    lane_a = lax.broadcasted_iota(jnp.int32, (TILE, TILE), 0)
    lane_b = lax.broadcasted_iota(jnp.int32, (TILE, TILE), 1)
    counts = nn(alive.astype(bf16), (lane_a <= lane_b).astype(f32).astype(bf16))
    totals = jnp.broadcast_to(counts[:, TILE - 1 :], (TILES, TILE))
    line_a = lax.broadcasted_iota(jnp.int32, (TILES, TILES), 0)
    line_b = lax.broadcasted_iota(jnp.int32, (TILES, TILES), 1)
    before = nn((line_b < line_a).astype(f32).astype(bf16), totals.astype(bf16))
    place[...] = jnp.where(alive > 0.5, counts + before - 1.0, -1.0)
    live_count = jnp.sum(alive)

    q_t[...] = nt(w_qkv_t[:C, :], hidden[...]).astype(bf16)
    keys_in = nn(compaction(place), hidden[...]).astype(bf16)
    k_t[...] = nt(w_qkv_t[C : 2 * C, :], keys_in).astype(bf16)
    v_t[...] = nt(w_qkv_t[2 * C :, :], keys_in).astype(bf16)
    v_nat[...] = nn(keys_in, w_qkv[:, 2 * C :]).astype(bf16)
    saves = copies([(hidden, hidden_out), (q_t, q_out), (k_t, k_out), (v_nat, v_out)], sems)
    for copy in saves:
        copy.start()
    q_square = jnp.square(q_t[...].astype(f32)).reshape(HEADS, HEAD, PATCH)
    k_square = jnp.square(k_t[...].astype(f32)).reshape(HEADS, HEAD, KEYS)
    q_top = jnp.max(jnp.sum(q_square, axis=1))
    k_top = jnp.max(jnp.sum(k_square, axis=1))
    good = (live_count >= 1.0) & (live_count <= float(KEYS)) & (q_top * k_top <= BOUND2)
    fits[0] = good.astype(jnp.int32)

    def save_probs(slot, unit, h):
        return pltpu.make_async_copy(low_t.at[slot, unit], probs.at[h], p_sems.at[slot, unit])

    @pl.when(fits[0] == 1)
    def _():
        lane = lax.broadcasted_iota(jnp.int32, (KEYS, HEAD), 1)
        key = lax.broadcasted_iota(jnp.int32, (KEYS, HEAD), 0).astype(f32)
        empty = jnp.where((lane == 0) & (key >= live_count), -65536.0, 0.0).astype(bf16)
        by_blocks(k_blocks, nn(keys_in, w_qkv[:, C : 2 * C]).astype(bf16), empty)
        row = lax.broadcasted_iota(jnp.int32, (LANES + HEAD, PATCH), 0)
        for unit in range(PAIR):
            queries[unit] = (row == LANES).astype(f32).astype(bf16)

        def heads(i, carry):
            slot = i & 1

            @pl.when(i > 1)
            def _():
                for unit in range(PAIR):
                    save_probs(slot, unit, (i - 2) * PAIR + unit).wait()

            for unit in range(PAIR):
                h = i * PAIR + unit
                place_head(queries.at[unit], h, q_t[head_rows(h), :])
                scores = nn(k_blocks[h // SHARE], queries[unit])
                powers = jnp.exp2(scores * (0.25 * LOG2E))
                inverse = 1.0 / jnp.sum(powers, axis=0, keepdims=True)
                low = (powers * inverse).astype(bf16)
                low_t[slot, unit] = low
                if unit:
                    o_t[head_rows(h - 1), :] = nn(v_t[head_rows(h - 1), :], held)
                held = low
            o_t[head_rows(h), :] = nn(v_t[head_rows(h), :], held)
            for unit in range(PAIR):
                save_probs(slot, unit, i * PAIR + unit).start()
                at = head_rows(i * PAIR + unit)
                pltpu.make_async_copy(o_t.at[at, :], o_out.at[at, :], sems.at[4]).start()
            return carry

        lax.fori_loop(0, HEADS // PAIR, heads, 0)

    @pl.when(fits[0] == 0)
    def _():
        plain_operands(hidden, live, w_qkv_t, kf_t, vf_t, bias)

        def one_head(h, carry):
            plain_forward(h, q_t, kf_t, vf_t, bias[...], o_t)
            return carry

        lax.fori_loop(0, HEADS, one_head, 0)
        pltpu.make_async_copy(o_t, o_out, sems.at[4]).start()

    sends = []
    half = PATCH // 2
    for part in range(2):
        rows = slice(part * half, part * half + half)
        attended[rows, :] = tn(o_t[:, rows].astype(bf16), w_proj[...]).astype(bf16)
        for tile in range(part * TILES // 2, (part + 1) * TILES // 2):
            sends.append(
                pltpu.make_async_copy(
                    attended.at[pl.ds(tile * TILE, TILE), :], att_send.at[src[tile]], sems.at[5 + tile]
                )
            )
            sends[-1].start()
    for copy in saves + [pltpu.make_async_copy(o_t, o_out, sems.at[4])] + sends:
        copy.wait()

    @pl.when(fits[0] == 1)
    def _():
        for slot in range(2):
            for unit in range(PAIR):
                save_probs(slot, unit, HEADS - (2 - slot) * PAIR + unit).wait()


def attend_grad_kernel(
    src, fits, g_recv, w_qkv_t, w_proj, probs, o_far, hidden_far, live, place, q_far, k_far, v_far,
    dh_send,
    perm, o_t, hidden, q_t, k_t, v_nat, cot, low_t, dm_t, dqkv_t, dkv_t, v_blocks, d_mixes, d_hidden, w_part, kf_t, vf_t, bias, sems, p_sems,
):
    def load_probs(slot, unit, h):
        return pltpu.make_async_copy(probs.at[h], low_t.at[slot, unit], p_sems.at[slot, unit])

    loads = [
        pltpu.make_async_copy(g_recv.at[src[tile]], cot.at[pl.ds(tile * TILE, TILE), :], sems.at[tile])
        for tile in range(TILES)
    ]
    saved = [
        pltpu.make_async_copy(source, target, sems.at[TILES + 1 + i])
        for i, (source, target) in enumerate(
            [(v_far, v_nat), (q_far, q_t), (k_far, k_t), (o_far, o_t), (hidden_far, hidden)]
        )
    ]
    for copy in loads + saved[:4]:
        copy.start()

    @pl.when(fits[0] == 1)
    def _():
        for unit in range(PAIR):
            load_probs(0, unit, unit).start()

    saved[4].start()
    perm[...] = compaction(place)
    for copy in loads:
        copy.wait()
    dm_t[...] = nt(w_proj[...], cot[...]).astype(bf16)
    for copy in saved:
        copy.wait()

    @pl.when(fits[0] == 1)
    def _():
        lane = lax.broadcasted_iota(jnp.int32, (KEYS, HEAD), 1)
        by_blocks(v_blocks, v_nat, (lane < 2).astype(f32).astype(bf16))
        for unit in range(PAIR):
            d_mixes[unit] = jnp.zeros((LANES + HEAD, PATCH), f32).astype(bf16)
        rows = lax.broadcasted_iota(jnp.int32, (HEAD, PATCH), 0)

        def heads(i, carry):
            slot = i & 1

            @pl.when(i < HEADS // PAIR - 1)
            def _():
                for unit in range(PAIR):
                    load_probs(1 - slot, unit, (i + 1) * PAIR + unit).start()

            for unit in range(PAIR):
                load_probs(slot, unit, i * PAIR + unit).wait()
            for unit in range(PAIR):
                h = i * PAIR + unit
                at = head_rows(h)
                d_mixed, query = dm_t[at, :], q_t[at, :]
                inner = jnp.sum(d_mixed.astype(f32) * o_t[at, :], axis=0, keepdims=True)
                high = inner.astype(bf16).astype(f32)
                place_head(d_mixes.at[unit], h, d_mixed)
                d_mixes[unit, LANES:, :] = jnp.where(
                    rows == 0, -high, jnp.where(rows == 1, high - inner, 0.0)
                ).astype(bf16)
                low = low_t[slot, unit]
                dkv_t[head_rows(h, C), :] = nt(d_mixed, low).astype(bf16)
                centred = nn(v_blocks[h // SHARE], d_mixes[unit])
                d_scores = (low.astype(f32) * centred).astype(bf16)
                dkv_t[at, :] = (nt(query, d_scores) * 0.25).astype(bf16)
                dqkv_t[at, :] = (nn(k_t[at, :], d_scores) * 0.25).astype(bf16)
            return carry

        lax.fori_loop(0, HEADS // PAIR, heads, 0)
        dqkv_t[C:, :] = nn(dkv_t[...], perm[...]).astype(bf16)

    @pl.when(fits[0] == 0)
    def _():
        plain_operands(hidden, live, w_qkv_t, kf_t, vf_t, bias)

        def one_head(h, carry):
            plain_backward(h, q_t, kf_t, vf_t, dm_t, bias[...], dqkv_t)
            return carry

        lax.fori_loop(0, HEADS, one_head, 0)

    w_grad = nt(hidden[...].T, dqkv_t[...]).astype(bf16)
    for peer in range(PEERS):
        for part in range(3):
            w_part[peer, part * 16 : part * 16 + 16, :] = w_grad[
                peer * 16 : peer * 16 + 16, part * C : part * C + C
            ]
    send_w = pltpu.make_async_copy(w_part, dh_send.at[:, pl.ds(TILE, W_ROWS), :], sems.at[TILES])
    send_w.start()
    sends = [send_w]
    half = PATCH // 2
    for part in range(2):
        rows = slice(part * half, part * half + half)
        d_hidden[rows, :] = tn(dqkv_t[:, rows], w_qkv_t[...]).astype(bf16)
        for tile in range(part * TILES // 2, (part + 1) * TILES // 2):
            sends.append(
                pltpu.make_async_copy(
                    d_hidden.at[pl.ds(tile * TILE, TILE), :], dh_send.at[src[tile], pl.ds(0, TILE), :], sems.at[tile]
                )
            )
            sends[-1].start()
    for copy in sends:
        copy.wait()


def fold_kernel(back, w_send):
    w_sum = back[0, TILE:, :].astype(f32)
    for peer in range(1, PEERS):
        w_sum = w_sum + back[peer, TILE:, :].astype(f32)
    for place in range(COLUMN):
        for part in range(3):
            w_send[place, :, part * C : part * C + C] = w_sum[part * 16 : part * 16 + 16]


def residual_grad_kernel(
    dest, back, resid_far, cot_far, occ, gain, grad_far, first, final, low, high,
    resid, cot, masked, sems,
):
    loads = []
    for tile in range(TILES):
        at = pl.ds(tile * TILE, TILE)
        loads.append([
            pltpu.make_async_copy(resid_far.at[at, :], resid.at[at, :], sems.at[2 * tile]),
            pltpu.make_async_copy(cot_far.at[at, :], cot.at[at, :], sems.at[2 * tile + 1]),
        ])
        for load in loads[tile]:
            load.start()
    columns = occupancy_columns(occ)
    moves = []
    for tile in range(TILES):
        for load in loads[tile]:
            load.wait()
        rows = slice(tile * TILE, (tile + 1) * TILE)
        residual = resid[rows, :]
        centre = jnp.mean(residual, axis=-1, keepdims=True)
        deviation = residual - centre
        variance = jnp.mean(deviation * deviation, axis=-1, keepdims=True)
        inv_std = lax.rsqrt(variance + norm_eps)
        normal = deviation * inv_std
        scaled = back[dest[tile] >> 3, :TILE, :].astype(f32) * gain[...]
        grad = cot[rows, :].astype(f32) + inv_std * (
            scaled
            - jnp.mean(scaled, axis=-1, keepdims=True)
            - normal * jnp.mean(scaled * normal, axis=-1, keepdims=True)
        )
        resid[rows, :] = grad
        masked[rows, :] = jnp.where(columns[:, tile : tile + 1] > 0.0, grad, 0.0).astype(bf16)
        at = pl.ds(tile * TILE, TILE)
        moves.append(pltpu.make_async_copy(resid.at[at, :], grad_far.at[at, :], sems.at[2 * tile]))
        moves[-1].start()
    first[...] = masked[:32, :]
    final[...] = masked[PATCH - 32 :, :]
    sides = edge_columns(masked[...])
    low[...] = sides[:32]
    high[...] = sides[32:]
    for move in moves:
        move.wait()


def inside_grad_kernel(grad_far, occ, weight, inside, grad, masked, shifts, sems):
    loads = [
        pltpu.make_async_copy(grad_far.at[pl.ds(tile * TILE, TILE), :], grad.at[pl.ds(tile * TILE, TILE), :], sems.at[tile])
        for tile in range(TILES)
    ]
    for load in loads:
        load.start()
    columns = occupancy_columns(occ)
    for tile in range(TILES):
        loads[tile].wait()
        rows = slice(tile * TILE, (tile + 1) * TILE)
        masked[rows, :] = jnp.where(columns[:, tile : tile + 1] > 0.0, grad[rows, :], 0.0)
    conv = inside_taps(True, masked[...], weight, shifts)
    moves = []
    for tile in range(TILES):
        rows = slice(tile * TILE, (tile + 1) * TILE)
        grad[rows, :] = grad[rows, :] + conv[rows] * columns[:, tile : tile + 1]
        at = pl.ds(tile * TILE, TILE)
        moves.append(pltpu.make_async_copy(grad.at[at, :], inside.at[at, :], sems.at[tile]))
        moves[-1].start()
    for move in moves:
        move.wait()


def conv_grad_kernel(inside, top, bottom, left, right, occ, weight, out, part, total, sem):
    load = pltpu.make_async_copy(inside, part, sem.at[0])
    load.start()
    total[...] = jnp.zeros((PATCH, C), f32)
    add_border(border_sums(True, top, bottom, left, right, weight), total)
    columns = occupancy_columns(occ)
    load.wait()
    for tile in range(TILES):
        rows = slice(tile * TILE, (tile + 1) * TILE)
        out[rows, :] = (part[rows, :] + total[rows, :] * columns[:, tile : tile + 1]).astype(bf16)


def output_kernel(dest, back, resid, out):
    for tile in range(TILES):
        rows = slice(tile * TILE, (tile + 1) * TILE)
        out[rows, :] = (resid[rows, :] + back[dest[tile] >> 3].astype(f32)).astype(bf16)


def exchange(low_edge, high_edge, axis):
    count = lax.axis_size(axis)
    forward = [(i, i + 1) for i in range(count - 1)]
    backward = [(target, source) for source, target in forward]
    return lax.ppermute(high_edge, axis, forward), lax.ppermute(low_edge, axis, backward)


def halo(first, final, low, high):
    top, bottom = exchange(first, final, "gx")
    low = jnp.concatenate([top[:1], low, bottom[:1]], axis=0)
    high = jnp.concatenate([top[31:], high, bottom[31:]], axis=0)
    left, right = exchange(low, high, "gy")
    return top, bottom, left, right


def conv_inside(block, weight):
    return call(
        conv_inside_kernel, far((PATCH, C), f32), [WHOLE] * 2, FAR,
        [pltpu.VMEM((PATCH, C), f32), pltpu.VMEM((3, PATCH + 64, C), bf16), pltpu.SemaphoreType.DMA((1,))],
        name="conv_inside",
        cost=pl.CostEstimate(flops=1200 * 10**6, bytes_accessed=4 * 10**6, transcendentals=0),
    )(block, weight)


def after(array, *others):
    return lax.optimization_barrier((array, *others))[0]


def swap(array, axis="gx"):
    return lax.all_to_all(array, axis, split_axis=0, concat_axis=0, tiled=True)


PLAIN = [pltpu.VMEM((C, PATCH), bf16), pltpu.VMEM((C, PATCH), bf16), pltpu.VMEM((PATCH, 1), f32)]
BLOCKS = pltpu.VMEM((C // LANES, KEYS, LANES + HEAD), bf16)
OPERAND = pltpu.VMEM((PAIR, LANES + HEAD, PATCH), bf16)


def attend(src, h_recv, w_qkv, w_qkv_t, w_proj):
    saved = [((PATCH, C), bf16), ((C, PATCH), bf16), ((C, KEYS), bf16), ((KEYS, C), bf16)]
    return pl.pallas_call(
        attend_kernel,
        out_shape=[
            far((PEERS, TILE, C), bf16), far((HEADS, KEYS, PATCH), bf16), far((C, PATCH), f32),
            far(*saved[0]), struct((TILES, TILE), f32), struct((TILES, TILE), f32),
            far(*saved[1]), far(*saved[2]), far(*saved[3]), struct((1,), jnp.int32),
        ],
        in_specs=[SMEM] + [WHOLE] * 4,
        out_specs=[FAR, FAR, FAR, FAR, WHOLE, WHOLE, FAR, FAR, FAR, SMEM],
        scratch_shapes=[pltpu.VMEM((PATCH, C), bf16), pltpu.VMEM((C, PATCH), f32)]
        + [pltpu.VMEM(*one) for one in saved]
        + [pltpu.VMEM((C, KEYS), bf16), BLOCKS, OPERAND, pltpu.VMEM((2, PAIR, KEYS, PATCH), bf16)]
        + PLAIN + [pltpu.SemaphoreType.DMA((13,)), pltpu.SemaphoreType.DMA((2, PAIR))],
        name="attend",
        cost_estimate=pl.CostEstimate(flops=12 * 10**9, bytes_accessed=32 * 10**6, transcendentals=14 * 10**6),
        compiler_params=pltpu.CompilerParams(vmem_limit_bytes=LIMIT * MIB),
    )(src, h_recv, w_qkv, w_qkv_t, w_proj)


def attend_grad(src, fits, g_recv, w_qkv_t, w_proj, probs, o_t, hidden, live, place, q_t, k_t, v_nat):
    return pl.pallas_call(
        attend_grad_kernel,
        out_shape=far((PEERS, TILE + W_ROWS, C), bf16),
        in_specs=[SMEM, SMEM, FAR, WHOLE, WHOLE, FAR, FAR, FAR, WHOLE, WHOLE, FAR, FAR, FAR],
        out_specs=FAR,
        scratch_shapes=[
            pltpu.VMEM((KEYS, PATCH), bf16),
            pltpu.VMEM((C, PATCH), f32), pltpu.VMEM((PATCH, C), bf16), pltpu.VMEM((C, PATCH), bf16),
            pltpu.VMEM((C, KEYS), bf16), pltpu.VMEM((KEYS, C), bf16),
            pltpu.VMEM((PATCH, C), bf16), pltpu.VMEM((2, PAIR, KEYS, PATCH), bf16),
            pltpu.VMEM((C, PATCH), bf16), pltpu.VMEM((3 * C, PATCH), bf16), pltpu.VMEM((2 * C, KEYS), bf16),
            BLOCKS, OPERAND, pltpu.VMEM((PATCH, C), bf16), pltpu.VMEM((PEERS, W_ROWS, C), bf16),
        ] + PLAIN + [pltpu.SemaphoreType.DMA((TILES + 6,)), pltpu.SemaphoreType.DMA((2, PAIR))],
        name="attend_grad",
        cost_estimate=pl.CostEstimate(flops=24 * 10**9, bytes_accessed=32 * 10**6, transcendentals=0),
        compiler_params=pltpu.CompilerParams(vmem_limit_bytes=LIMIT * MIB),
    )(
        src, fits, pin(g_recv), w_qkv_t, w_proj, pin(probs), pin(o_t), pin(hidden), live, place,
        pin(q_t), pin(k_t), pin(v_nat),
    )


def local(features, occupied, conv_weight, norm_gain, w_qkv, w_proj, tile_dest, cotangent):
    size_x, size_y, feat_width = features.shape
    cells = size_x * size_y
    dest = tile_dest.reshape(TILES)
    occ = occupied.reshape(TILES, TILE)
    gain = norm_gain.reshape(1, C)
    feat = features.reshape(cells, C)
    cot = cotangent.reshape(cells, C)
    rows_f32 = struct((cells, C), f32)
    rows_bf16 = struct((cells, C), bf16)
    buckets = struct((PEERS, TILE, C), bf16)
    total = pltpu.VMEM((cells, C), f32)

    border = struct((32, C), bf16)
    masked, *edges = call(
        mask_kernel, [rows_bf16] + [border] * 4, [FAR] * 2, [WHOLE] * 5,
        [pltpu.VMEM((cells, C), bf16), pltpu.VMEM((32, 32), jnp.int32), pltpu.SemaphoreType.DMA((5,))],
        name="mask",
    )(pin(feat), pin(occupied))
    edges = halo(*edges)
    conv = conv_inside(masked, conv_weight)
    resid, h_send = call(
        forward_kernel, [far((cells, C), f32), far((PEERS, TILE + META, C), bf16)],
        [SMEM, FAR] + [WHOLE] * 8, [FAR, FAR],
        [
            total, total, pltpu.VMEM((cells, C), bf16), pltpu.VMEM((PEERS, META, C), bf16),
            pltpu.SemaphoreType.DMA((2 + 2 * TILES,)),
        ],
        name="forward",
    )(dest, pin(conv), feat, *edges, occ, conv_weight, gain)
    h_recv = swap(h_send)
    flags = h_recv[:, TILE + 1, 0].astype(f32)
    order = jnp.arange(TILES, dtype=f32)
    peers = jnp.arange(PEERS, dtype=jnp.int32)
    ranks = jnp.sum(jnp.where(peers[None, :] < peers[:, None], flags[None, :], 0.0), axis=1)
    chosen = (ranks[None, :] == order[:, None]) & (flags[None, :] > 0.5)
    src = jnp.sum(jnp.where(chosen, peers[None, :], 0), axis=1)

    g_send = call(
        pack_kernel, far((PEERS, TILE, C), bf16), [SMEM, WHOLE], FAR, [pltpu.SemaphoreType.DMA((TILES,))], name="pack"
    )(dest, cot)
    g_send, h_recv = lax.optimization_barrier((g_send, h_recv))
    g_recv = swap(g_send)
    w_qkv_t = w_qkv.T
    att_send, probs, o_t, hidden, live, place, q_t, k_t, v_aug, fits = attend(src, h_recv, w_qkv, w_qkv_t, w_proj)
    att_back = swap(att_send)
    dh_send = attend_grad(src, fits, g_recv, w_qkv_t, w_proj, probs, o_t, hidden, live, place, q_t, k_t, v_aug)
    block_output = call(
        output_kernel, rows_bf16, [SMEM, WHOLE, WHOLE], WHOLE, name="output"
    )(dest, after(att_back, dh_send), resid)
    dh_send = after(dh_send, block_output)
    dh_back = swap(dh_send)
    w_send = call(
        fold_kernel, far((COLUMN, 16, 3 * C), f32), [WHOLE], WHOLE, name="fold"
    )(dh_back)
    w_recv = swap(w_send, "gy")
    grad, *edges = call(
        residual_grad_kernel,
        [far((cells, C), f32), border, border, border, border],
        [SMEM, WHOLE, FAR, FAR, WHOLE, WHOLE], [FAR] + [WHOLE] * 4,
        [
            total, pltpu.VMEM((cells, C), bf16), pltpu.VMEM((cells, C), bf16),
            pltpu.SemaphoreType.DMA((2 * TILES,)),
        ],
        name="residual_grad",
    )(dest, dh_back, pin(resid), pin(cot), occ, gain)
    grad_edges = halo(*edges)
    inside = call(
        inside_grad_kernel, far((cells, C), f32), [FAR, WHOLE, WHOLE], FAR,
        [total, total, pltpu.VMEM((3, PATCH + 64, C), bf16), pltpu.SemaphoreType.DMA((TILES,))],
        name="inside_grad",
        cost=pl.CostEstimate(flops=1200 * 10**6, bytes_accessed=4 * 10**6, transcendentals=0),
    )(pin(grad), occ, conv_weight)
    w_recv = after(w_recv, grad_edges[0])
    w_sum = (jnp.sum(w_recv, axis=0) / math.sqrt(131072)).astype(bf16)
    d_features = call(
        conv_grad_kernel, rows_bf16, [FAR] + [WHOLE] * 6, WHOLE,
        [total, total, pltpu.SemaphoreType.DMA((1,))], name="conv_grad",
    )(pin(inside), *grad_edges, occ, conv_weight)
    w_grad = swap(jnp.broadcast_to(w_sum[None], (PEERS, 16, 3 * C))).reshape(C, 3 * C).astype(f32)
    shape = (size_x, size_y, feat_width)
    return (block_output.reshape(shape), d_features.reshape(shape), w_grad)


def solution(mesh):
    in_specs = (
        P("gx", "gy", None),
        P("gx", "gy"),
        P(),
        P(),
        P(),
        P(),
        P("gx", "gy"),
        P("gx", "gy", None),
    )
    out_specs = (P("gx", "gy", None), P("gx", "gy", None), P())
    return jax.shard_map(local, mesh=mesh, in_specs=in_specs, out_specs=out_specs, check_vma=False)
```

```python
import functools
import math

import jax
import jax.numpy as jnp
from jax import lax
from jax.experimental import pallas as pl
from jax.experimental.pallas import tpu as pltpu
from jax.sharding import PartitionSpec as P

C = 256
HEADS = 16
HEAD = 16
PATCH = 1024
TILE = 128
TILES = 8
PEERS = 16
META = 16
KEYS = 832
W_ROWS = 48
COLUMN = 8
PAIR = 2
LANES = 64
SHARE = LANES // HEAD
LIMIT = 40

norm_eps = 1e-05
mask_fill = 1000000000.0
LOG2E = 1.4426950408889634
BOUND2 = (4.0 * 80.0) ** 2

bf16 = jnp.bfloat16
f32 = jnp.float32
MIB = 2**20


def nn(a, b):
    return lax.dot_general(a, b, (((1,), (0,)), ((), ())), preferred_element_type=f32)


def nt(a, b):
    return lax.dot_general(a, b, (((1,), (1,)), ((), ())), preferred_element_type=f32)


def tn(a, b):
    return lax.dot_general(a, b, (((0,), (0,)), ((), ())), preferred_element_type=f32)


SMEM = pl.BlockSpec(memory_space=pltpu.SMEM)
WHOLE = pl.BlockSpec(memory_space=pltpu.VMEM)
FAR = pl.BlockSpec(memory_space=pltpu.HBM)


def far(shape, dtype):
    return pltpu.HBM(shape, dtype)


def pin(array):
    return pltpu.with_memory_space_constraint(array, pltpu.HBM)


def call(body, out_shape, in_specs, out_specs, scratch=(), name=None, cost=None, limit=16):
    return pl.pallas_call(
        body,
        out_shape=out_shape,
        in_specs=in_specs,
        out_specs=out_specs,
        scratch_shapes=list(scratch),
        name=name,
        cost_estimate=cost,
        compiler_params=pltpu.CompilerParams(vmem_limit_bytes=limit * MIB),
    )


def struct(shape, dtype):
    return jax.ShapeDtypeStruct(shape, dtype)


def pack_kernel(dest, cot, send, sems):
    moves = [
        pltpu.make_async_copy(cot.at[pl.ds(tile * TILE, TILE), :], send.at[dest[tile] >> 3], sems.at[tile])
        for tile in range(TILES)
    ]
    for move in moves:
        move.start()
    for move in moves:
        move.wait()


def edge_columns(block):
    edge = lax.broadcasted_iota(jnp.int32, (64, PATCH), 0)
    cell = lax.broadcasted_iota(jnp.int32, (64, PATCH), 1)
    wanted = jnp.where(edge < 32, edge * 32, (edge - 32) * 32 + 31)
    return nn((cell == wanted).astype(f32).astype(bf16), block).astype(bf16)


def mask_kernel(feat_far, occ_far, masked, first, final, low, high, feat, occ, sems):
    parts = 4
    size = PATCH // parts
    loads = [pltpu.make_async_copy(occ_far, occ, sems.at[parts])] + [
        pltpu.make_async_copy(feat_far.at[pl.ds(k * size, size), :], feat.at[pl.ds(k * size, size), :], sems.at[k])
        for k in range(parts)
    ]
    for load in loads:
        load.start()
    loads[0].wait()
    live = occ[...].astype(f32)
    wide = jnp.concatenate([live, jnp.zeros((32, TILE - 32), f32)], axis=1)
    columns = jnp.concatenate([wide, jnp.zeros((TILE - 32, TILE), f32)], axis=0).T
    for line in range(32):
        if line * 32 % size == 0:
            loads[1 + line * 32 // size].wait()
        rows = slice(line * 32, line * 32 + 32)
        kept = jnp.where(columns[:32, line : line + 1] > 0.0, feat[rows, :].astype(f32), 0.0)
        masked[rows, :] = kept.astype(bf16)
    first[...] = masked[:32, :]
    final[...] = masked[PATCH - 32 :, :]
    sides = edge_columns(masked[...])
    low[...] = sides[:32]
    high[...] = sides[32:]


def tap_dot(a, b, flip):
    return nt(a, b) if flip else nn(a, b)


def inside_taps(flip, block, weight, shifts):
    edge = jnp.zeros((32, C), f32)
    whole = jnp.concatenate([edge, block, edge], axis=0)
    total = whole.shape[0]
    col = lax.broadcasted_iota(jnp.int32, (total, C), 0) & 31
    shifts[0] = jnp.where(col == 0, 0.0, pltpu.roll(whole, 1, 0)).astype(bf16)
    shifts[1] = whole.astype(bf16)
    shifts[2] = jnp.where(col == 31, 0.0, pltpu.roll(whole, total - 1, 0)).astype(bf16)
    conv = None
    for a in range(3):
        for b in range(3):
            x, y = (2 - a, 2 - b) if flip else (a, b)
            term = tap_dot(shifts[y, x * 32 : x * 32 + PATCH, :], weight[a * 3 + b], flip)
            conv = term if conv is None else conv + term
    return conv


def conv_inside_kernel(block, weight, out, conv, shifts, sem):
    conv[...] = inside_taps(False, block[...].astype(f32), weight, shifts)
    save = pltpu.make_async_copy(conv, out, sem.at[0])
    save.start()
    save.wait()


def border_sums(flip, top, bottom, left, right, weight):
    line = jnp.zeros((1, C), f32)
    first, last = (2, 0) if flip else (0, 2)

    def side(cells, taps):
        summed = None
        for k, tap in enumerate(taps):
            shift = 2 - k if flip else k
            term = tap_dot(cells[shift : shift + 32].astype(bf16), weight[tap], flip)
            summed = term if summed is None else summed + term
        return summed

    rows = []
    for edge, a in ((top, first), (bottom, last)):
        padded = jnp.concatenate([line, edge[...].astype(f32), line], axis=0)
        rows.append(side(padded, [a * 3 + b for b in range(3)]))
    columns = []
    for edge, b in ((left, first), (right, last)):
        columns.append(side(edge[...].astype(f32), [a * 3 + b for a in range(3)]))
    return rows, columns


def add_border(sums, total):
    rows, columns = sums
    for added, line in zip(rows, (0, 31)):
        at = slice(line * 32, line * 32 + 32)
        total[at, :] = total[at, :] + added
    for added, col in zip(columns, (0, 31)):
        for i in range(32):
            at = slice(i * 32 + col, i * 32 + col + 1)
            total[at, :] = total[at, :] + added[i : i + 1]


def occupancy_columns(occ):
    live = occ[...].astype(f32)
    square = jnp.concatenate([live, jnp.zeros((TILE - TILES, TILE), f32)], axis=0)
    return square.T


def forward_kernel(
    dest, conv, feat, top, bottom, left, right, occ, weight, gain,
    resid_out, send, total, resid, hidden, meta, sems,
):
    load = pltpu.make_async_copy(conv, total, sems.at[1 + 2 * TILES])
    load.start()
    live = occ[...].astype(f32)
    row = lax.broadcasted_iota(jnp.int32, (META, C), 0)
    meta[...] = jnp.zeros(meta.shape, f32).astype(bf16)
    for tile in range(TILES):
        line = jnp.concatenate([live[tile : tile + 1], jnp.zeros((1, C - TILE), f32)], axis=1)
        meta[dest[tile] >> 3] = jnp.where(row == 0, line, 1.0).astype(bf16)
    moves = [pltpu.make_async_copy(meta, send.at[:, pl.ds(TILE, META), :], sems.at[0])]
    moves[0].start()
    sums = border_sums(False, top, bottom, left, right, weight)
    columns = occupancy_columns(occ)
    load.wait()
    add_border(sums, total)
    for tile in range(TILES):
        rows = slice(tile * TILE, (tile + 1) * TILE)
        residual = feat[rows, :].astype(f32) + total[rows, :] * columns[:, tile : tile + 1]
        resid[rows, :] = residual
        centre = jnp.mean(residual, axis=-1, keepdims=True)
        deviation = residual - centre
        variance = jnp.mean(deviation * deviation, axis=-1, keepdims=True)
        hidden[rows, :] = (deviation * lax.rsqrt(variance + norm_eps) * gain[...]).astype(bf16)
        at = pl.ds(tile * TILE, TILE)
        for k, (source, target) in enumerate((
            (hidden.at[at, :], send.at[dest[tile] >> 3, pl.ds(0, TILE), :]),
            (resid.at[at, :], resid_out.at[at, :]),
        )):
            moves.append(pltpu.make_async_copy(source, target, sems.at[1 + 2 * tile + k]))
            moves[-1].start()
    for move in moves:
        move.wait()


def plain_forward(h, q_t, kf_t, vf_t, bias, o_t):
    block = 256
    at = pl.ds(pl.multiple_of(h * HEAD, HEAD), HEAD)
    key, value = kf_t[at, :], vf_t[at, :]

    def one_block(c, carry):
        cols = pl.ds(pl.multiple_of(c * block, block), block)
        scores = tn(key, q_t[at, cols]) * 0.25 + bias
        powers = jnp.exp(scores - jnp.max(scores, axis=0, keepdims=True))
        low = (powers / jnp.sum(powers, axis=0, keepdims=True)).astype(bf16)
        o_t[at, cols] = nn(value, low)
        return carry

    lax.fori_loop(0, PATCH // block, one_block, 0)


def plain_backward(h, q_t, kf_t, vf_t, dm_t, bias, dqkv_t):
    block = 256
    start = pl.multiple_of(h * HEAD, HEAD)
    at = pl.ds(start, HEAD)
    key, value = kf_t[at, :], vf_t[at, :]

    def one_block(c, sums):
        d_keys, d_values = sums
        cols = pl.ds(pl.multiple_of(c * block, block), block)
        query, d_mixed = q_t[at, cols], dm_t[at, cols]
        scores = tn(key, query) * 0.25 + bias
        powers = jnp.exp(scores - jnp.max(scores, axis=0, keepdims=True))
        probs = powers / jnp.sum(powers, axis=0, keepdims=True)
        low = probs.astype(bf16)
        d_probs = tn(value, d_mixed)
        inner = jnp.sum(d_probs * probs, axis=0, keepdims=True)
        d_scores = (probs * (d_probs - inner) * 0.25).astype(bf16)
        dqkv_t[at, cols] = nn(key, d_scores).astype(bf16)
        return (d_keys + nt(query, d_scores), d_values + nt(d_mixed, low))

    zero = jnp.zeros((HEAD, PATCH), f32)
    d_keys, d_values = lax.fori_loop(0, PATCH // block, one_block, (zero, zero))
    dqkv_t[pl.ds(start + C, HEAD), :] = d_keys.astype(bf16)
    dqkv_t[pl.ds(start + 2 * C, HEAD), :] = d_values.astype(bf16)


def plain_operands(hidden, live, w_qkv_t, kf_t, vf_t, bias):
    kf_t[...] = nt(w_qkv_t[C : 2 * C, :], hidden[...]).astype(bf16)
    vf_t[...] = nt(w_qkv_t[2 * C :, :], hidden[...]).astype(bf16)
    square = jnp.concatenate([live[...], jnp.zeros((TILE - TILES, TILE), f32)], axis=0).T
    column = jnp.concatenate([square[:, t : t + 1] for t in range(TILES)], axis=0)
    bias[...] = (column - 1.0) * mask_fill


def copies(pairs, sems):
    started = [pltpu.make_async_copy(source, target, sems.at[i]) for i, (source, target) in enumerate(pairs)]
    return started


def compaction(place):
    row = jnp.concatenate([place[t : t + 1, :] for t in range(TILES)], axis=1)
    key_index = lax.broadcasted_iota(jnp.int32, (KEYS, PATCH), 0).astype(f32)
    return (key_index == row).astype(f32).astype(bf16)


def by_blocks(blocks, array, extra):
    for block in range(C // LANES):
        blocks[block, :, :LANES] = array[:, block * LANES : block * LANES + LANES]
        blocks[block, :, LANES:] = extra


def place_head(operand, h, rows):
    own = pl.multiple_of((h & (SHARE - 1)) * HEAD, HEAD)
    before = pl.multiple_of(((h - PAIR) & (SHARE - 1)) * HEAD, HEAD)
    operand[pl.ds(before, HEAD), :] = jnp.zeros(rows.shape, rows.dtype)
    operand[pl.ds(own, HEAD), :] = rows


def head_rows(h, offset=0):
    return pl.ds(pl.multiple_of(h * HEAD + offset, HEAD), HEAD)


def attend_kernel(
    src, h_recv, w_qkv, w_qkv_t, w_proj,
    att_send, probs, o_out, hidden_out, live, place, q_out, k_out, v_out, fits,
    attended, o_t, hidden, q_t, k_t, v_nat, v_t, k_blocks, queries, low_t, kf_t, vf_t, bias, sems, p_sems,
):
    lives = []
    for tile in range(TILES):
        rows = slice(tile * TILE, (tile + 1) * TILE)
        hidden[rows, :] = h_recv[src[tile], :TILE, :]
        lives.append(h_recv[src[tile], TILE:, :].astype(f32)[0:1, :TILE])
    alive = jnp.concatenate(lives, axis=0)
    live[...] = alive
    lane_a = lax.broadcasted_iota(jnp.int32, (TILE, TILE), 0)
    lane_b = lax.broadcasted_iota(jnp.int32, (TILE, TILE), 1)
    counts = nn(alive.astype(bf16), (lane_a <= lane_b).astype(f32).astype(bf16))
    totals = jnp.broadcast_to(counts[:, TILE - 1 :], (TILES, TILE))
    line_a = lax.broadcasted_iota(jnp.int32, (TILES, TILES), 0)
    line_b = lax.broadcasted_iota(jnp.int32, (TILES, TILES), 1)
    before = nn((line_b < line_a).astype(f32).astype(bf16), totals.astype(bf16))
    place[...] = jnp.where(alive > 0.5, counts + before - 1.0, -1.0)
    live_count = jnp.sum(alive)

    q_t[...] = nt(w_qkv_t[:C, :], hidden[...]).astype(bf16)
    keys_in = nn(compaction(place), hidden[...]).astype(bf16)
    k_t[...] = nt(w_qkv_t[C : 2 * C, :], keys_in).astype(bf16)
    v_t[...] = nt(w_qkv_t[2 * C :, :], keys_in).astype(bf16)
    v_nat[...] = nn(keys_in, w_qkv[:, 2 * C :]).astype(bf16)
    saves = copies([(hidden, hidden_out), (q_t, q_out), (k_t, k_out), (v_nat, v_out)], sems)
    for copy in saves:
        copy.start()
    q_square = jnp.square(q_t[...].astype(f32)).reshape(HEADS, HEAD, PATCH)
    k_square = jnp.square(k_t[...].astype(f32)).reshape(HEADS, HEAD, KEYS)
    q_top = jnp.max(jnp.sum(q_square, axis=1))
    k_top = jnp.max(jnp.sum(k_square, axis=1))
    good = (live_count >= 1.0) & (live_count <= float(KEYS)) & (q_top * k_top <= BOUND2)
    fits[0] = good.astype(jnp.int32)

    def save_probs(slot, unit, h):
        return pltpu.make_async_copy(low_t.at[slot, unit], probs.at[h], p_sems.at[slot, unit])

    @pl.when(fits[0] == 1)
    def _():
        lane = lax.broadcasted_iota(jnp.int32, (KEYS, HEAD), 1)
        key = lax.broadcasted_iota(jnp.int32, (KEYS, HEAD), 0).astype(f32)
        empty = jnp.where((lane == 0) & (key >= live_count), -65536.0, 0.0).astype(bf16)
        by_blocks(k_blocks, nn(keys_in, w_qkv[:, C : 2 * C]).astype(bf16), empty)
        row = lax.broadcasted_iota(jnp.int32, (LANES + HEAD, PATCH), 0)
        for unit in range(PAIR):
            queries[unit] = (row == LANES).astype(f32).astype(bf16)

        def heads(i, carry):
            slot = i & 1

            @pl.when(i > 1)
            def _():
                for unit in range(PAIR):
                    save_probs(slot, unit, (i - 2) * PAIR + unit).wait()

            for unit in range(PAIR):
                h = i * PAIR + unit
                place_head(queries.at[unit], h, q_t[head_rows(h), :])
                scores = nn(k_blocks[h // SHARE], queries[unit])
                powers = jnp.exp2(scores * (0.25 * LOG2E))
                inverse = 1.0 / jnp.sum(powers, axis=0, keepdims=True)
                low = (powers * inverse).astype(bf16)
                low_t[slot, unit] = low
                if unit:
                    o_t[head_rows(h - 1), :] = nn(v_t[head_rows(h - 1), :], held)
                held = low
            o_t[head_rows(h), :] = nn(v_t[head_rows(h), :], held)
            for unit in range(PAIR):
                save_probs(slot, unit, i * PAIR + unit).start()
                at = head_rows(i * PAIR + unit)
                pltpu.make_async_copy(o_t.at[at, :], o_out.at[at, :], sems.at[4]).start()
            return carry

        lax.fori_loop(0, HEADS // PAIR, heads, 0)

    @pl.when(fits[0] == 0)
    def _():
        plain_operands(hidden, live, w_qkv_t, kf_t, vf_t, bias)

        def one_head(h, carry):
            plain_forward(h, q_t, kf_t, vf_t, bias[...], o_t)
            return carry

        lax.fori_loop(0, HEADS, one_head, 0)
        pltpu.make_async_copy(o_t, o_out, sems.at[4]).start()

    sends = []
    half = PATCH // 2
    for part in range(2):
        rows = slice(part * half, part * half + half)
        attended[rows, :] = tn(o_t[:, rows].astype(bf16), w_proj[...]).astype(bf16)
        for tile in range(part * TILES // 2, (part + 1) * TILES // 2):
            sends.append(
                pltpu.make_async_copy(
                    attended.at[pl.ds(tile * TILE, TILE), :], att_send.at[src[tile]], sems.at[5 + tile]
                )
            )
            sends[-1].start()
    for copy in saves + [pltpu.make_async_copy(o_t, o_out, sems.at[4])] + sends:
        copy.wait()

    @pl.when(fits[0] == 1)
    def _():
        for slot in range(2):
            for unit in range(PAIR):
                save_probs(slot, unit, HEADS - (2 - slot) * PAIR + unit).wait()


def attend_grad_kernel(
    src, fits, g_recv, w_qkv_t, w_proj, probs, o_far, hidden_far, live, place, q_far, k_far, v_far,
    dh_send,
    perm, o_t, hidden, q_t, k_t, v_nat, cot, low_t, dm_t, dqkv_t, dkv_t, v_blocks, d_mixes, d_hidden, w_part, kf_t, vf_t, bias, sems, p_sems,
):
    def load_probs(slot, unit, h):
        return pltpu.make_async_copy(probs.at[h], low_t.at[slot, unit], p_sems.at[slot, unit])

    loads = [
        pltpu.make_async_copy(g_recv.at[src[tile]], cot.at[pl.ds(tile * TILE, TILE), :], sems.at[tile])
        for tile in range(TILES)
    ]
    saved = [
        pltpu.make_async_copy(source, target, sems.at[TILES + 1 + i])
        for i, (source, target) in enumerate(
            [(v_far, v_nat), (q_far, q_t), (k_far, k_t), (o_far, o_t), (hidden_far, hidden)]
        )
    ]
    for copy in loads + saved[:4]:
        copy.start()

    @pl.when(fits[0] == 1)
    def _():
        for unit in range(PAIR):
            load_probs(0, unit, unit).start()

    saved[4].start()
    perm[...] = compaction(place)
    saved[0].wait()
    lane = lax.broadcasted_iota(jnp.int32, (KEYS, HEAD), 1)
    by_blocks(v_blocks, v_nat, (lane < 2).astype(f32).astype(bf16))
    for copy in loads:
        copy.wait()
    dm_t[...] = nt(w_proj[...], cot[...]).astype(bf16)
    for copy in saved[1:]:
        copy.wait()

    @pl.when(fits[0] == 1)
    def _():
        for unit in range(PAIR):
            d_mixes[unit] = jnp.zeros((LANES + HEAD, PATCH), f32).astype(bf16)
        rows = lax.broadcasted_iota(jnp.int32, (HEAD, PATCH), 0)

        def heads(i, carry):
            slot = i & 1

            @pl.when(i < HEADS // PAIR - 1)
            def _():
                for unit in range(PAIR):
                    load_probs(1 - slot, unit, (i + 1) * PAIR + unit).start()

            for unit in range(PAIR):
                load_probs(slot, unit, i * PAIR + unit).wait()
            for unit in range(PAIR):
                h = i * PAIR + unit
                at = head_rows(h)
                d_mixed, query = dm_t[at, :], q_t[at, :]
                inner = jnp.sum(d_mixed.astype(f32) * o_t[at, :], axis=0, keepdims=True)
                high = inner.astype(bf16).astype(f32)
                place_head(d_mixes.at[unit], h, d_mixed)
                d_mixes[unit, LANES:, :] = jnp.where(
                    rows == 0, -high, jnp.where(rows == 1, high - inner, 0.0)
                ).astype(bf16)
                low = low_t[slot, unit]
                dkv_t[head_rows(h, C), :] = nt(d_mixed, low).astype(bf16)
                centred = nn(v_blocks[h // SHARE], d_mixes[unit])
                d_scores = (low.astype(f32) * centred).astype(bf16)
                dkv_t[at, :] = (nt(query, d_scores) * 0.25).astype(bf16)
                dqkv_t[at, :] = (nn(k_t[at, :], d_scores) * 0.25).astype(bf16)
            return carry

        lax.fori_loop(0, HEADS // PAIR, heads, 0)
        dqkv_t[C:, :] = nn(dkv_t[...], perm[...]).astype(bf16)

    @pl.when(fits[0] == 0)
    def _():
        plain_operands(hidden, live, w_qkv_t, kf_t, vf_t, bias)

        def one_head(h, carry):
            plain_backward(h, q_t, kf_t, vf_t, dm_t, bias[...], dqkv_t)
            return carry

        lax.fori_loop(0, HEADS, one_head, 0)

    w_grad = nt(hidden[...].T, dqkv_t[...]).astype(bf16)
    for peer in range(PEERS):
        for part in range(3):
            w_part[peer, part * 16 : part * 16 + 16, :] = w_grad[
                peer * 16 : peer * 16 + 16, part * C : part * C + C
            ]
    send_w = pltpu.make_async_copy(w_part, dh_send.at[:, pl.ds(TILE, W_ROWS), :], sems.at[TILES])
    send_w.start()
    sends = [send_w]
    half = PATCH // 2
    for part in range(2):
        rows = slice(part * half, part * half + half)
        d_hidden[rows, :] = tn(dqkv_t[:, rows], w_qkv_t[...]).astype(bf16)
        for tile in range(part * TILES // 2, (part + 1) * TILES // 2):
            sends.append(
                pltpu.make_async_copy(
                    d_hidden.at[pl.ds(tile * TILE, TILE), :], dh_send.at[src[tile], pl.ds(0, TILE), :], sems.at[tile]
                )
            )
            sends[-1].start()
    for copy in sends:
        copy.wait()


def fold_kernel(back, w_send):
    w_sum = back[0, TILE:, :].astype(f32)
    for peer in range(1, PEERS):
        w_sum = w_sum + back[peer, TILE:, :].astype(f32)
    for place in range(COLUMN):
        for part in range(3):
            w_send[place, :, part * C : part * C + C] = w_sum[part * 16 : part * 16 + 16]


def residual_grad_kernel(
    dest, back, resid_far, cot_far, occ, gain, grad_far, first, final, low, high,
    resid, cot, masked, sems,
):
    loads = []
    for tile in range(TILES):
        at = pl.ds(tile * TILE, TILE)
        loads.append([
            pltpu.make_async_copy(resid_far.at[at, :], resid.at[at, :], sems.at[2 * tile]),
            pltpu.make_async_copy(cot_far.at[at, :], cot.at[at, :], sems.at[2 * tile + 1]),
        ])
        for load in loads[tile]:
            load.start()
    columns = occupancy_columns(occ)
    moves = []
    for tile in range(TILES):
        for load in loads[tile]:
            load.wait()
        rows = slice(tile * TILE, (tile + 1) * TILE)
        residual = resid[rows, :]
        centre = jnp.mean(residual, axis=-1, keepdims=True)
        deviation = residual - centre
        variance = jnp.mean(deviation * deviation, axis=-1, keepdims=True)
        inv_std = lax.rsqrt(variance + norm_eps)
        normal = deviation * inv_std
        scaled = back[dest[tile] >> 3, :TILE, :].astype(f32) * gain[...]
        grad = cot[rows, :].astype(f32) + inv_std * (
            scaled
            - jnp.mean(scaled, axis=-1, keepdims=True)
            - normal * jnp.mean(scaled * normal, axis=-1, keepdims=True)
        )
        resid[rows, :] = grad
        masked[rows, :] = jnp.where(columns[:, tile : tile + 1] > 0.0, grad, 0.0).astype(bf16)
        at = pl.ds(tile * TILE, TILE)
        moves.append(pltpu.make_async_copy(resid.at[at, :], grad_far.at[at, :], sems.at[2 * tile]))
        moves[-1].start()
    first[...] = masked[:32, :]
    final[...] = masked[PATCH - 32 :, :]
    sides = edge_columns(masked[...])
    low[...] = sides[:32]
    high[...] = sides[32:]
    for move in moves:
        move.wait()


def inside_grad_kernel(grad_far, occ, weight, inside, grad, masked, shifts, sems):
    loads = [
        pltpu.make_async_copy(grad_far.at[pl.ds(tile * TILE, TILE), :], grad.at[pl.ds(tile * TILE, TILE), :], sems.at[tile])
        for tile in range(TILES)
    ]
    for load in loads:
        load.start()
    columns = occupancy_columns(occ)
    for tile in range(TILES):
        loads[tile].wait()
        rows = slice(tile * TILE, (tile + 1) * TILE)
        masked[rows, :] = jnp.where(columns[:, tile : tile + 1] > 0.0, grad[rows, :], 0.0)
    conv = inside_taps(True, masked[...], weight, shifts)
    moves = []
    for tile in range(TILES):
        rows = slice(tile * TILE, (tile + 1) * TILE)
        grad[rows, :] = grad[rows, :] + conv[rows] * columns[:, tile : tile + 1]
        at = pl.ds(tile * TILE, TILE)
        moves.append(pltpu.make_async_copy(grad.at[at, :], inside.at[at, :], sems.at[tile]))
        moves[-1].start()
    for move in moves:
        move.wait()


def conv_grad_kernel(inside, top, bottom, left, right, occ, weight, out, total, sem):
    load = pltpu.make_async_copy(inside, total, sem.at[0])
    load.start()
    rows, columns = border_sums(True, top, bottom, left, right, weight)
    live = occ[...].astype(f32)
    wide = jnp.concatenate([live, jnp.zeros((32, TILE - 32), f32)], axis=1)
    lines = jnp.concatenate([wide, jnp.zeros((TILE - 32, TILE), f32)], axis=0).T
    rows = [added * lines[:32, line : line + 1] for added, line in zip(rows, (0, 31))]
    columns = [added * live[:, col : col + 1] for added, col in zip(columns, (0, 31))]
    load.wait()
    add_border((rows, columns), total)
    out[...] = total[...].astype(bf16)


def output_kernel(dest, back, resid, out):
    for tile in range(TILES):
        rows = slice(tile * TILE, (tile + 1) * TILE)
        out[rows, :] = (resid[rows, :] + back[dest[tile] >> 3].astype(f32)).astype(bf16)


def exchange(low_edge, high_edge, axis):
    count = lax.axis_size(axis)
    forward = [(i, i + 1) for i in range(count - 1)]
    backward = [(target, source) for source, target in forward]
    return lax.ppermute(high_edge, axis, forward), lax.ppermute(low_edge, axis, backward)


def halo(first, final, low, high):
    top, bottom = exchange(first, final, "gx")
    low = jnp.concatenate([top[:1], low, bottom[:1]], axis=0)
    high = jnp.concatenate([top[31:], high, bottom[31:]], axis=0)
    left, right = exchange(low, high, "gy")
    return top, bottom, left, right


def conv_inside(block, weight):
    return call(
        conv_inside_kernel, far((PATCH, C), f32), [WHOLE] * 2, FAR,
        [pltpu.VMEM((PATCH, C), f32), pltpu.VMEM((3, PATCH + 64, C), bf16), pltpu.SemaphoreType.DMA((1,))],
        name="conv_inside",
        cost=pl.CostEstimate(flops=1200 * 10**6, bytes_accessed=4 * 10**6, transcendentals=0),
    )(block, weight)


def after(array, *others):
    return lax.optimization_barrier((array, *others))[0]


def swap(array, axis="gx"):
    return lax.all_to_all(array, axis, split_axis=0, concat_axis=0, tiled=True)


PLAIN = [pltpu.VMEM((C, PATCH), bf16), pltpu.VMEM((C, PATCH), bf16), pltpu.VMEM((PATCH, 1), f32)]
BLOCKS = pltpu.VMEM((C // LANES, KEYS, LANES + HEAD), bf16)
OPERAND = pltpu.VMEM((PAIR, LANES + HEAD, PATCH), bf16)


def attend(src, h_recv, w_qkv, w_qkv_t, w_proj):
    saved = [((PATCH, C), bf16), ((C, PATCH), bf16), ((C, KEYS), bf16), ((KEYS, C), bf16)]
    return pl.pallas_call(
        attend_kernel,
        out_shape=[
            far((PEERS, TILE, C), bf16), far((HEADS, KEYS, PATCH), bf16), far((C, PATCH), f32),
            far(*saved[0]), struct((TILES, TILE), f32), struct((TILES, TILE), f32),
            far(*saved[1]), far(*saved[2]), far(*saved[3]), struct((1,), jnp.int32),
        ],
        in_specs=[SMEM] + [WHOLE] * 4,
        out_specs=[FAR, FAR, FAR, FAR, WHOLE, WHOLE, FAR, FAR, FAR, SMEM],
        scratch_shapes=[pltpu.VMEM((PATCH, C), bf16), pltpu.VMEM((C, PATCH), f32)]
        + [pltpu.VMEM(*one) for one in saved]
        + [pltpu.VMEM((C, KEYS), bf16), BLOCKS, OPERAND, pltpu.VMEM((2, PAIR, KEYS, PATCH), bf16)]
        + PLAIN + [pltpu.SemaphoreType.DMA((13,)), pltpu.SemaphoreType.DMA((2, PAIR))],
        name="attend",
        cost_estimate=pl.CostEstimate(flops=12 * 10**9, bytes_accessed=32 * 10**6, transcendentals=14 * 10**6),
        compiler_params=pltpu.CompilerParams(vmem_limit_bytes=LIMIT * MIB),
    )(src, h_recv, w_qkv, w_qkv_t, w_proj)


def attend_grad(src, fits, g_recv, w_qkv_t, w_proj, probs, o_t, hidden, live, place, q_t, k_t, v_nat):
    return pl.pallas_call(
        attend_grad_kernel,
        out_shape=far((PEERS, TILE + W_ROWS, C), bf16),
        in_specs=[SMEM, SMEM, FAR, WHOLE, WHOLE, FAR, FAR, FAR, WHOLE, WHOLE, FAR, FAR, FAR],
        out_specs=FAR,
        scratch_shapes=[
            pltpu.VMEM((KEYS, PATCH), bf16),
            pltpu.VMEM((C, PATCH), f32), pltpu.VMEM((PATCH, C), bf16), pltpu.VMEM((C, PATCH), bf16),
            pltpu.VMEM((C, KEYS), bf16), pltpu.VMEM((KEYS, C), bf16),
            pltpu.VMEM((PATCH, C), bf16), pltpu.VMEM((2, PAIR, KEYS, PATCH), bf16),
            pltpu.VMEM((C, PATCH), bf16), pltpu.VMEM((3 * C, PATCH), bf16), pltpu.VMEM((2 * C, KEYS), bf16),
            BLOCKS, OPERAND, pltpu.VMEM((PATCH, C), bf16), pltpu.VMEM((PEERS, W_ROWS, C), bf16),
        ] + PLAIN + [pltpu.SemaphoreType.DMA((TILES + 6,)), pltpu.SemaphoreType.DMA((2, PAIR))],
        name="attend_grad",
        cost_estimate=pl.CostEstimate(flops=24 * 10**9, bytes_accessed=32 * 10**6, transcendentals=0),
        compiler_params=pltpu.CompilerParams(vmem_limit_bytes=LIMIT * MIB),
    )(
        src, fits, pin(g_recv), w_qkv_t, w_proj, pin(probs), pin(o_t), pin(hidden), live, place,
        pin(q_t), pin(k_t), pin(v_nat),
    )


def local(features, occupied, conv_weight, norm_gain, w_qkv, w_proj, tile_dest, cotangent):
    size_x, size_y, feat_width = features.shape
    cells = size_x * size_y
    dest = tile_dest.reshape(TILES)
    occ = occupied.reshape(TILES, TILE)
    gain = norm_gain.reshape(1, C)
    feat = features.reshape(cells, C)
    cot = cotangent.reshape(cells, C)
    rows_f32 = struct((cells, C), f32)
    rows_bf16 = struct((cells, C), bf16)
    buckets = struct((PEERS, TILE, C), bf16)
    total = pltpu.VMEM((cells, C), f32)

    border = struct((32, C), bf16)
    masked, *edges = call(
        mask_kernel, [rows_bf16] + [border] * 4, [FAR] * 2, [WHOLE] * 5,
        [pltpu.VMEM((cells, C), bf16), pltpu.VMEM((32, 32), jnp.int32), pltpu.SemaphoreType.DMA((5,))],
        name="mask",
    )(pin(feat), pin(occupied))
    edges = halo(*edges)
    conv = conv_inside(masked, conv_weight)
    resid, h_send = call(
        forward_kernel, [far((cells, C), f32), far((PEERS, TILE + META, C), bf16)],
        [SMEM, FAR] + [WHOLE] * 8, [FAR, FAR],
        [
            total, total, pltpu.VMEM((cells, C), bf16), pltpu.VMEM((PEERS, META, C), bf16),
            pltpu.SemaphoreType.DMA((2 + 2 * TILES,)),
        ],
        name="forward",
    )(dest, pin(conv), feat, *edges, occ, conv_weight, gain)
    h_recv = swap(h_send)
    flags = h_recv[:, TILE + 1, 0].astype(f32)
    order = jnp.arange(TILES, dtype=f32)
    peers = jnp.arange(PEERS, dtype=jnp.int32)
    ranks = jnp.sum(jnp.where(peers[None, :] < peers[:, None], flags[None, :], 0.0), axis=1)
    chosen = (ranks[None, :] == order[:, None]) & (flags[None, :] > 0.5)
    src = jnp.sum(jnp.where(chosen, peers[None, :], 0), axis=1)

    g_send = call(
        pack_kernel, far((PEERS, TILE, C), bf16), [SMEM, WHOLE], FAR, [pltpu.SemaphoreType.DMA((TILES,))], name="pack"
    )(dest, cot)
    g_send, h_recv = lax.optimization_barrier((g_send, h_recv))
    g_recv = swap(g_send)
    w_qkv_t = w_qkv.T
    att_send, probs, o_t, hidden, live, place, q_t, k_t, v_aug, fits = attend(src, h_recv, w_qkv, w_qkv_t, w_proj)
    att_back = swap(att_send)
    dh_send = attend_grad(src, fits, g_recv, w_qkv_t, w_proj, probs, o_t, hidden, live, place, q_t, k_t, v_aug)
    block_output = call(
        output_kernel, rows_bf16, [SMEM, WHOLE, WHOLE], WHOLE, name="output"
    )(dest, after(att_back, dh_send), resid)
    dh_send = after(dh_send, block_output)
    dh_back = swap(dh_send)
    w_send = call(
        fold_kernel, far((COLUMN, 16, 3 * C), f32), [WHOLE], WHOLE, name="fold"
    )(dh_back)
    w_recv = swap(w_send, "gy")
    grad, *edges = call(
        residual_grad_kernel,
        [far((cells, C), f32), border, border, border, border],
        [SMEM, WHOLE, FAR, FAR, WHOLE, WHOLE], [FAR] + [WHOLE] * 4,
        [
            total, pltpu.VMEM((cells, C), bf16), pltpu.VMEM((cells, C), bf16),
            pltpu.SemaphoreType.DMA((2 * TILES,)),
        ],
        name="residual_grad",
    )(dest, dh_back, pin(resid), pin(cot), occ, gain)
    grad_edges = halo(*edges)
    inside = call(
        inside_grad_kernel, far((cells, C), f32), [FAR, WHOLE, WHOLE], FAR,
        [total, total, pltpu.VMEM((3, PATCH + 64, C), bf16), pltpu.SemaphoreType.DMA((TILES,))],
        name="inside_grad",
        cost=pl.CostEstimate(flops=1200 * 10**6, bytes_accessed=4 * 10**6, transcendentals=0),
    )(pin(grad), occ, conv_weight)
    w_recv = after(w_recv, grad_edges[0])
    w_sum = (jnp.sum(w_recv, axis=0) / math.sqrt(131072)).astype(bf16)
    d_features = call(
        conv_grad_kernel, rows_bf16, [FAR] + [WHOLE] * 6, WHOLE,
        [total, pltpu.SemaphoreType.DMA((1,))], name="conv_grad",
    )(pin(inside), *grad_edges, occupied, conv_weight)
    w_grad = swap(jnp.broadcast_to(w_sum[None], (PEERS, 16, 3 * C))).reshape(C, 3 * C).astype(f32)
    shape = (size_x, size_y, feat_width)
    return (block_output.reshape(shape), d_features.reshape(shape), w_grad)


def solution(mesh):
    in_specs = (
        P("gx", "gy", None),
        P("gx", "gy"),
        P(),
        P(),
        P(),
        P(),
        P("gx", "gy"),
        P("gx", "gy", None),
    )
    out_specs = (P("gx", "gy", None), P("gx", "gy", None), P())
    return jax.shard_map(local, mesh=mesh, in_specs=in_specs, out_specs=out_specs, check_vma=False)
```

```python
import functools
import math

import jax
import jax.numpy as jnp
from jax import lax
from jax.experimental import pallas as pl
from jax.experimental.pallas import tpu as pltpu
from jax.sharding import PartitionSpec as P

C = 256
HEADS = 16
HEAD = 16
PATCH = 1024
TILE = 128
TILES = 8
PEERS = 16
META = 16
KEYS = 832
W_ROWS = 48
COLUMN = 8
PAIR = 2
LANES = 64
SHARE = LANES // HEAD
LIMIT = 40

norm_eps = 1e-05
mask_fill = 1000000000.0
LOG2E = 1.4426950408889634
BOUND2 = (4.0 * 80.0) ** 2

bf16 = jnp.bfloat16
f32 = jnp.float32
MIB = 2**20


def nn(a, b):
    return lax.dot_general(a, b, (((1,), (0,)), ((), ())), preferred_element_type=f32)


def nt(a, b):
    return lax.dot_general(a, b, (((1,), (1,)), ((), ())), preferred_element_type=f32)


def tn(a, b):
    return lax.dot_general(a, b, (((0,), (0,)), ((), ())), preferred_element_type=f32)


SMEM = pl.BlockSpec(memory_space=pltpu.SMEM)
WHOLE = pl.BlockSpec(memory_space=pltpu.VMEM)
FAR = pl.BlockSpec(memory_space=pltpu.HBM)


def far(shape, dtype):
    return pltpu.HBM(shape, dtype)


def pin(array):
    return pltpu.with_memory_space_constraint(array, pltpu.HBM)


def call(body, out_shape, in_specs, out_specs, scratch=(), name=None, cost=None, limit=16):
    return pl.pallas_call(
        body,
        out_shape=out_shape,
        in_specs=in_specs,
        out_specs=out_specs,
        scratch_shapes=list(scratch),
        name=name,
        cost_estimate=cost,
        compiler_params=pltpu.CompilerParams(vmem_limit_bytes=limit * MIB),
    )


def struct(shape, dtype):
    return jax.ShapeDtypeStruct(shape, dtype)


def pack_kernel(dest, cot, send, sems):
    moves = [
        pltpu.make_async_copy(cot.at[pl.ds(tile * TILE, TILE), :], send.at[dest[tile] >> 3], sems.at[tile])
        for tile in range(TILES)
    ]
    for move in moves:
        move.start()
    for move in moves:
        move.wait()


def edge_columns(block):
    edge = lax.broadcasted_iota(jnp.int32, (64, PATCH), 0)
    cell = lax.broadcasted_iota(jnp.int32, (64, PATCH), 1)
    wanted = jnp.where(edge < 32, edge * 32, (edge - 32) * 32 + 31)
    return nn((cell == wanted).astype(f32).astype(bf16), block).astype(bf16)


def mask_kernel(feat_far, occ_far, masked, first, final, low, high, feat, occ, sems):
    parts = 4
    size = PATCH // parts
    loads = [pltpu.make_async_copy(occ_far, occ, sems.at[parts])] + [
        pltpu.make_async_copy(feat_far.at[pl.ds(k * size, size), :], feat.at[pl.ds(k * size, size), :], sems.at[k])
        for k in range(parts)
    ]
    for load in loads:
        load.start()
    loads[0].wait()
    live = occ[...].astype(f32)
    wide = jnp.concatenate([live, jnp.zeros((32, TILE - 32), f32)], axis=1)
    columns = jnp.concatenate([wide, jnp.zeros((TILE - 32, TILE), f32)], axis=0).T
    for line in range(32):
        if line * 32 % size == 0:
            loads[1 + line * 32 // size].wait()
        rows = slice(line * 32, line * 32 + 32)
        kept = jnp.where(columns[:32, line : line + 1] > 0.0, feat[rows, :].astype(f32), 0.0)
        masked[rows, :] = kept.astype(bf16)
    first[...] = masked[:32, :]
    final[...] = masked[PATCH - 32 :, :]
    sides = edge_columns(masked[...])
    low[...] = sides[:32]
    high[...] = sides[32:]


def tap_dot(a, b, flip):
    return nt(a, b) if flip else nn(a, b)


def inside_taps(flip, block, weight, shifts):
    edge = jnp.zeros((32, C), f32)
    whole = jnp.concatenate([edge, block, edge], axis=0)
    total = whole.shape[0]
    col = lax.broadcasted_iota(jnp.int32, (total, C), 0) & 31
    shifts[0] = jnp.where(col == 0, 0.0, pltpu.roll(whole, 1, 0)).astype(bf16)
    shifts[1] = whole.astype(bf16)
    shifts[2] = jnp.where(col == 31, 0.0, pltpu.roll(whole, total - 1, 0)).astype(bf16)
    conv = None
    for a in range(3):
        for b in range(3):
            x, y = (2 - a, 2 - b) if flip else (a, b)
            term = tap_dot(shifts[y, x * 32 : x * 32 + PATCH, :], weight[a * 3 + b], flip)
            conv = term if conv is None else conv + term
    return conv


def conv_inside_kernel(block, weight, out, conv, shifts, sem):
    conv[...] = inside_taps(False, block[...].astype(f32), weight, shifts)
    save = pltpu.make_async_copy(conv, out, sem.at[0])
    save.start()
    save.wait()


def border_sums(flip, top, bottom, left, right, weight):
    line = jnp.zeros((1, C), f32)
    first, last = (2, 0) if flip else (0, 2)

    def side(cells, taps):
        summed = None
        for k, tap in enumerate(taps):
            shift = 2 - k if flip else k
            term = tap_dot(cells[shift : shift + 32].astype(bf16), weight[tap], flip)
            summed = term if summed is None else summed + term
        return summed

    rows = []
    for edge, a in ((top, first), (bottom, last)):
        padded = jnp.concatenate([line, edge[...].astype(f32), line], axis=0)
        rows.append(side(padded, [a * 3 + b for b in range(3)]))
    columns = []
    for edge, b in ((left, first), (right, last)):
        columns.append(side(edge[...].astype(f32), [a * 3 + b for a in range(3)]))
    return rows, columns


def add_border(sums, total):
    rows, columns = sums
    for added, line in zip(rows, (0, 31)):
        at = slice(line * 32, line * 32 + 32)
        total[at, :] = total[at, :] + added
    for added, col in zip(columns, (0, 31)):
        for i in range(32):
            at = slice(i * 32 + col, i * 32 + col + 1)
            total[at, :] = total[at, :] + added[i : i + 1]


def occupancy_columns(occ):
    live = occ[...].astype(f32)
    square = jnp.concatenate([live, jnp.zeros((TILE - TILES, TILE), f32)], axis=0)
    return square.T


def forward_kernel(
    dest, conv, feat, top, bottom, left, right, occ, weight, gain,
    resid_out, send, total, resid, hidden, meta, sems,
):
    load = pltpu.make_async_copy(conv, total, sems.at[1 + 2 * TILES])
    load.start()
    live = occ[...].astype(f32)
    row = lax.broadcasted_iota(jnp.int32, (META, C), 0)
    meta[...] = jnp.zeros(meta.shape, f32).astype(bf16)
    for tile in range(TILES):
        line = jnp.concatenate([live[tile : tile + 1], jnp.zeros((1, C - TILE), f32)], axis=1)
        meta[dest[tile] >> 3] = jnp.where(row == 0, line, 1.0).astype(bf16)
    moves = [pltpu.make_async_copy(meta, send.at[:, pl.ds(TILE, META), :], sems.at[0])]
    moves[0].start()
    sums = border_sums(False, top, bottom, left, right, weight)
    columns = occupancy_columns(occ)
    load.wait()
    add_border(sums, total)
    for tile in range(TILES):
        rows = slice(tile * TILE, (tile + 1) * TILE)
        residual = feat[rows, :].astype(f32) + total[rows, :] * columns[:, tile : tile + 1]
        resid[rows, :] = residual
        centre = jnp.mean(residual, axis=-1, keepdims=True)
        deviation = residual - centre
        variance = jnp.mean(deviation * deviation, axis=-1, keepdims=True)
        hidden[rows, :] = (deviation * lax.rsqrt(variance + norm_eps) * gain[...]).astype(bf16)
        at = pl.ds(tile * TILE, TILE)
        for k, (source, target) in enumerate((
            (hidden.at[at, :], send.at[dest[tile] >> 3, pl.ds(0, TILE), :]),
            (resid.at[at, :], resid_out.at[at, :]),
        )):
            moves.append(pltpu.make_async_copy(source, target, sems.at[1 + 2 * tile + k]))
            moves[-1].start()
    for move in moves:
        move.wait()


def plain_forward(h, q_t, kf_t, vf_t, bias, o_t):
    block = 256
    at = pl.ds(pl.multiple_of(h * HEAD, HEAD), HEAD)
    key, value = kf_t[at, :], vf_t[at, :]

    def one_block(c, carry):
        cols = pl.ds(pl.multiple_of(c * block, block), block)
        scores = tn(key, q_t[at, cols]) * 0.25 + bias
        powers = jnp.exp(scores - jnp.max(scores, axis=0, keepdims=True))
        low = (powers / jnp.sum(powers, axis=0, keepdims=True)).astype(bf16)
        o_t[at, cols] = nn(value, low)
        return carry

    lax.fori_loop(0, PATCH // block, one_block, 0)


def plain_backward(h, q_t, kf_t, vf_t, dm_t, bias, dqkv_t):
    block = 256
    start = pl.multiple_of(h * HEAD, HEAD)
    at = pl.ds(start, HEAD)
    key, value = kf_t[at, :], vf_t[at, :]

    def one_block(c, sums):
        d_keys, d_values = sums
        cols = pl.ds(pl.multiple_of(c * block, block), block)
        query, d_mixed = q_t[at, cols], dm_t[at, cols]
        scores = tn(key, query) * 0.25 + bias
        powers = jnp.exp(scores - jnp.max(scores, axis=0, keepdims=True))
        probs = powers / jnp.sum(powers, axis=0, keepdims=True)
        low = probs.astype(bf16)
        d_probs = tn(value, d_mixed)
        inner = jnp.sum(d_probs * probs, axis=0, keepdims=True)
        d_scores = (probs * (d_probs - inner) * 0.25).astype(bf16)
        dqkv_t[at, cols] = nn(key, d_scores).astype(bf16)
        return (d_keys + nt(query, d_scores), d_values + nt(d_mixed, low))

    zero = jnp.zeros((HEAD, PATCH), f32)
    d_keys, d_values = lax.fori_loop(0, PATCH // block, one_block, (zero, zero))
    dqkv_t[pl.ds(start + C, HEAD), :] = d_keys.astype(bf16)
    dqkv_t[pl.ds(start + 2 * C, HEAD), :] = d_values.astype(bf16)


def plain_operands(hidden, live, w_qkv_t, kf_t, vf_t, bias):
    kf_t[...] = nt(w_qkv_t[C : 2 * C, :], hidden[...]).astype(bf16)
    vf_t[...] = nt(w_qkv_t[2 * C :, :], hidden[...]).astype(bf16)
    square = jnp.concatenate([live[...], jnp.zeros((TILE - TILES, TILE), f32)], axis=0).T
    column = jnp.concatenate([square[:, t : t + 1] for t in range(TILES)], axis=0)
    bias[...] = (column - 1.0) * mask_fill


def copies(pairs, sems):
    started = [pltpu.make_async_copy(source, target, sems.at[i]) for i, (source, target) in enumerate(pairs)]
    return started


def compaction(place):
    row = jnp.concatenate([place[t : t + 1, :] for t in range(TILES)], axis=1)
    key_index = lax.broadcasted_iota(jnp.int32, (KEYS, PATCH), 0).astype(f32)
    return (key_index == row).astype(f32).astype(bf16)


def by_blocks(blocks, array, extra):
    for block in range(C // LANES):
        blocks[block, :, :LANES] = array[:, block * LANES : block * LANES + LANES]
        blocks[block, :, LANES:] = extra


def place_head(operand, h, rows):
    own = pl.multiple_of((h & (SHARE - 1)) * HEAD, HEAD)
    before = pl.multiple_of(((h - PAIR) & (SHARE - 1)) * HEAD, HEAD)
    operand[pl.ds(before, HEAD), :] = jnp.zeros(rows.shape, rows.dtype)
    operand[pl.ds(own, HEAD), :] = rows


def head_rows(h, offset=0):
    return pl.ds(pl.multiple_of(h * HEAD + offset, HEAD), HEAD)


def attend_kernel(
    src, h_recv, w_qkv, w_qkv_t, w_proj,
    att_send, probs, o_out, hidden_out, live, place, q_out, k_out, v_out, fits,
    attended, o_t, hidden, q_t, k_t, v_nat, v_t, k_blocks, queries, low_t, kf_t, vf_t, bias, sems, p_sems,
):
    lives = []
    for tile in range(TILES):
        rows = slice(tile * TILE, (tile + 1) * TILE)
        hidden[rows, :] = h_recv[src[tile], :TILE, :]
        lives.append(h_recv[src[tile], TILE:, :].astype(f32)[0:1, :TILE])
    alive = jnp.concatenate(lives, axis=0)
    live[...] = alive
    lane_a = lax.broadcasted_iota(jnp.int32, (TILE, TILE), 0)
    lane_b = lax.broadcasted_iota(jnp.int32, (TILE, TILE), 1)
    counts = nn(alive.astype(bf16), (lane_a <= lane_b).astype(f32).astype(bf16))
    totals = jnp.broadcast_to(counts[:, TILE - 1 :], (TILES, TILE))
    line_a = lax.broadcasted_iota(jnp.int32, (TILES, TILES), 0)
    line_b = lax.broadcasted_iota(jnp.int32, (TILES, TILES), 1)
    before = nn((line_b < line_a).astype(f32).astype(bf16), totals.astype(bf16))
    place[...] = jnp.where(alive > 0.5, counts + before - 1.0, -1.0)
    live_count = jnp.sum(alive)

    q_t[...] = nt(w_qkv_t[:C, :], hidden[...]).astype(bf16)
    keys_in = nn(compaction(place), hidden[...]).astype(bf16)
    k_t[...] = nt(w_qkv_t[C : 2 * C, :], keys_in).astype(bf16)
    v_t[...] = nt(w_qkv_t[2 * C :, :], keys_in).astype(bf16)
    v_nat[...] = nn(keys_in, w_qkv[:, 2 * C :]).astype(bf16)
    saves = copies([(hidden, hidden_out), (q_t, q_out), (k_t, k_out), (v_nat, v_out)], sems)
    for copy in saves:
        copy.start()
    q_square = jnp.square(q_t[...].astype(f32)).reshape(HEADS, HEAD, PATCH)
    k_square = jnp.square(k_t[...].astype(f32)).reshape(HEADS, HEAD, KEYS)
    q_top = jnp.max(jnp.sum(q_square, axis=1))
    k_top = jnp.max(jnp.sum(k_square, axis=1))
    good = (live_count >= 1.0) & (live_count <= float(KEYS)) & (q_top * k_top <= BOUND2)
    fits[0] = good.astype(jnp.int32)

    def save_probs(slot, unit, h):
        return pltpu.make_async_copy(low_t.at[slot, unit], probs.at[h], p_sems.at[slot, unit])

    @pl.when(fits[0] == 1)
    def _():
        lane = lax.broadcasted_iota(jnp.int32, (KEYS, HEAD), 1)
        key = lax.broadcasted_iota(jnp.int32, (KEYS, HEAD), 0).astype(f32)
        empty = jnp.where((lane == 0) & (key >= live_count), -65536.0, 0.0).astype(bf16)
        by_blocks(k_blocks, nn(keys_in, w_qkv[:, C : 2 * C]).astype(bf16), empty)
        row = lax.broadcasted_iota(jnp.int32, (LANES + HEAD, PATCH), 0)
        for unit in range(PAIR):
            queries[unit] = (row == LANES).astype(f32).astype(bf16)

        def heads(i, carry):
            slot = i & 1

            @pl.when(i > 1)
            def _():
                for unit in range(PAIR):
                    save_probs(slot, unit, (i - 2) * PAIR + unit).wait()

            for unit in range(PAIR):
                h = i * PAIR + unit
                place_head(queries.at[unit], h, q_t[head_rows(h), :])
                scores = nn(k_blocks[h // SHARE], queries[unit])
                powers = jnp.exp2(scores * (0.25 * LOG2E))
                inverse = 1.0 / jnp.sum(powers, axis=0, keepdims=True)
                low = (powers * inverse).astype(bf16)
                low_t[slot, unit] = low
                if unit:
                    o_t[head_rows(h - 1), :] = nn(v_t[head_rows(h - 1), :], held)
                held = low
            o_t[head_rows(h), :] = nn(v_t[head_rows(h), :], held)
            for unit in range(PAIR):
                save_probs(slot, unit, i * PAIR + unit).start()
                at = head_rows(i * PAIR + unit)
                pltpu.make_async_copy(o_t.at[at, :], o_out.at[at, :], sems.at[4]).start()
            return carry

        lax.fori_loop(0, HEADS // PAIR, heads, 0)

    @pl.when(fits[0] == 0)
    def _():
        plain_operands(hidden, live, w_qkv_t, kf_t, vf_t, bias)

        def one_head(h, carry):
            plain_forward(h, q_t, kf_t, vf_t, bias[...], o_t)
            return carry

        lax.fori_loop(0, HEADS, one_head, 0)
        pltpu.make_async_copy(o_t, o_out, sems.at[4]).start()

    sends = []
    half = PATCH // 2
    for part in range(2):
        rows = slice(part * half, part * half + half)
        attended[rows, :] = tn(o_t[:, rows].astype(bf16), w_proj[...]).astype(bf16)
        for tile in range(part * TILES // 2, (part + 1) * TILES // 2):
            sends.append(
                pltpu.make_async_copy(
                    attended.at[pl.ds(tile * TILE, TILE), :], att_send.at[src[tile]], sems.at[5 + tile]
                )
            )
            sends[-1].start()
    for copy in saves + [pltpu.make_async_copy(o_t, o_out, sems.at[4])] + sends:
        copy.wait()

    @pl.when(fits[0] == 1)
    def _():
        for slot in range(2):
            for unit in range(PAIR):
                save_probs(slot, unit, HEADS - (2 - slot) * PAIR + unit).wait()


def attend_grad_kernel(
    src, fits, g_recv, w_far, w_proj, probs, o_far, hidden_far, live, place, q_far, k_far, v_far,
    dh_send,
    w_qkv_t, perm, o_t, hidden, q_t, k_t, v_nat, cot, low_t, dm_t, dqkv_t, dkv_t, v_blocks, d_mixes, d_hidden, w_part, kf_t, vf_t, bias, sems, p_sems,
):
    def load_probs(slot, unit, h):
        return pltpu.make_async_copy(probs.at[h], low_t.at[slot, unit], p_sems.at[slot, unit])

    loads = [
        pltpu.make_async_copy(g_recv.at[src[tile]], cot.at[pl.ds(tile * TILE, TILE), :], sems.at[tile])
        for tile in range(TILES)
    ]
    saved = [
        pltpu.make_async_copy(source, target, sems.at[TILES + 1 + i])
        for i, (source, target) in enumerate(
            [(v_far, v_nat), (q_far, q_t), (k_far, k_t), (o_far, o_t), (hidden_far, hidden), (w_far, w_qkv_t)]
        )
    ]
    for copy in loads + saved[:4]:
        copy.start()

    @pl.when(fits[0] == 1)
    def _():
        for unit in range(PAIR):
            load_probs(0, unit, unit).start()

    saved[4].start()
    saved[5].start()
    perm[...] = compaction(place)
    saved[0].wait()
    lane = lax.broadcasted_iota(jnp.int32, (KEYS, HEAD), 1)
    by_blocks(v_blocks, v_nat, (lane < 2).astype(f32).astype(bf16))
    for copy in loads:
        copy.wait()
    dm_t[...] = nt(w_proj[...], cot[...]).astype(bf16)
    for copy in saved[1:]:
        copy.wait()

    @pl.when(fits[0] == 1)
    def _():
        for unit in range(PAIR):
            d_mixes[unit] = jnp.zeros((LANES + HEAD, PATCH), f32).astype(bf16)
        rows = lax.broadcasted_iota(jnp.int32, (HEAD, PATCH), 0)

        def heads(i, carry):
            slot = i & 1

            @pl.when(i < HEADS // PAIR - 1)
            def _():
                for unit in range(PAIR):
                    load_probs(1 - slot, unit, (i + 1) * PAIR + unit).start()

            for unit in range(PAIR):
                load_probs(slot, unit, i * PAIR + unit).wait()
            for unit in range(PAIR):
                h = i * PAIR + unit
                at = head_rows(h)
                d_mixed, query = dm_t[at, :], q_t[at, :]
                inner = jnp.sum(d_mixed.astype(f32) * o_t[at, :], axis=0, keepdims=True)
                high = inner.astype(bf16).astype(f32)
                place_head(d_mixes.at[unit], h, d_mixed)
                d_mixes[unit, LANES:, :] = jnp.where(
                    rows == 0, -high, jnp.where(rows == 1, high - inner, 0.0)
                ).astype(bf16)
                low = low_t[slot, unit]
                dkv_t[head_rows(h, C), :] = nt(d_mixed, low).astype(bf16)
                centred = nn(v_blocks[h // SHARE], d_mixes[unit])
                d_scores = (low.astype(f32) * centred).astype(bf16)
                dkv_t[at, :] = (nt(query, d_scores) * 0.25).astype(bf16)
                dqkv_t[at, :] = (nn(k_t[at, :], d_scores) * 0.25).astype(bf16)
            return carry

        lax.fori_loop(0, HEADS // PAIR, heads, 0)
        dqkv_t[C:, :] = nn(dkv_t[...], perm[...]).astype(bf16)

    @pl.when(fits[0] == 0)
    def _():
        plain_operands(hidden, live, w_qkv_t, kf_t, vf_t, bias)

        def one_head(h, carry):
            plain_backward(h, q_t, kf_t, vf_t, dm_t, bias[...], dqkv_t)
            return carry

        lax.fori_loop(0, HEADS, one_head, 0)

    w_grad = nt(hidden[...].T, dqkv_t[...]).astype(bf16)
    for peer in range(PEERS):
        for part in range(3):
            w_part[peer, part * 16 : part * 16 + 16, :] = w_grad[
                peer * 16 : peer * 16 + 16, part * C : part * C + C
            ]
    send_w = pltpu.make_async_copy(w_part, dh_send.at[:, pl.ds(TILE, W_ROWS), :], sems.at[TILES])
    send_w.start()
    sends = [send_w]
    half = PATCH // 2
    for part in range(2):
        rows = slice(part * half, part * half + half)
        d_hidden[rows, :] = tn(dqkv_t[:, rows], w_qkv_t[...]).astype(bf16)
        for tile in range(part * TILES // 2, (part + 1) * TILES // 2):
            sends.append(
                pltpu.make_async_copy(
                    d_hidden.at[pl.ds(tile * TILE, TILE), :], dh_send.at[src[tile], pl.ds(0, TILE), :], sems.at[tile]
                )
            )
            sends[-1].start()
    for copy in sends:
        copy.wait()


def fold_kernel(back, w_send):
    w_sum = back[0, TILE:, :].astype(f32)
    for peer in range(1, PEERS):
        w_sum = w_sum + back[peer, TILE:, :].astype(f32)
    for place in range(COLUMN):
        for part in range(3):
            w_send[place, :, part * C : part * C + C] = w_sum[part * 16 : part * 16 + 16]


def residual_grad_kernel(
    dest, back, resid_far, cot_far, occ, gain, grad_far, first, final, low, high,
    resid, cot, masked, sems,
):
    loads = []
    for tile in range(TILES):
        at = pl.ds(tile * TILE, TILE)
        loads.append([
            pltpu.make_async_copy(resid_far.at[at, :], resid.at[at, :], sems.at[2 * tile]),
            pltpu.make_async_copy(cot_far.at[at, :], cot.at[at, :], sems.at[2 * tile + 1]),
        ])
        for load in loads[tile]:
            load.start()
    columns = occupancy_columns(occ)
    moves = []
    for tile in range(TILES):
        for load in loads[tile]:
            load.wait()
        rows = slice(tile * TILE, (tile + 1) * TILE)
        residual = resid[rows, :]
        centre = jnp.mean(residual, axis=-1, keepdims=True)
        deviation = residual - centre
        variance = jnp.mean(deviation * deviation, axis=-1, keepdims=True)
        inv_std = lax.rsqrt(variance + norm_eps)
        normal = deviation * inv_std
        scaled = back[dest[tile] >> 3, :TILE, :].astype(f32) * gain[...]
        grad = cot[rows, :].astype(f32) + inv_std * (
            scaled
            - jnp.mean(scaled, axis=-1, keepdims=True)
            - normal * jnp.mean(scaled * normal, axis=-1, keepdims=True)
        )
        resid[rows, :] = grad
        masked[rows, :] = jnp.where(columns[:, tile : tile + 1] > 0.0, grad, 0.0).astype(bf16)
        at = pl.ds(tile * TILE, TILE)
        moves.append(pltpu.make_async_copy(resid.at[at, :], grad_far.at[at, :], sems.at[2 * tile]))
        moves[-1].start()
    first[...] = masked[:32, :]
    final[...] = masked[PATCH - 32 :, :]
    sides = edge_columns(masked[...])
    low[...] = sides[:32]
    high[...] = sides[32:]
    for move in moves:
        move.wait()


def inside_grad_kernel(grad_far, occ, weight, inside, grad, masked, shifts, sems):
    loads = [
        pltpu.make_async_copy(grad_far.at[pl.ds(tile * TILE, TILE), :], grad.at[pl.ds(tile * TILE, TILE), :], sems.at[tile])
        for tile in range(TILES)
    ]
    for load in loads:
        load.start()
    columns = occupancy_columns(occ)
    for tile in range(TILES):
        loads[tile].wait()
        rows = slice(tile * TILE, (tile + 1) * TILE)
        masked[rows, :] = jnp.where(columns[:, tile : tile + 1] > 0.0, grad[rows, :], 0.0)
    conv = inside_taps(True, masked[...], weight, shifts)
    moves = []
    for tile in range(TILES):
        rows = slice(tile * TILE, (tile + 1) * TILE)
        grad[rows, :] = grad[rows, :] + conv[rows] * columns[:, tile : tile + 1]
        at = pl.ds(tile * TILE, TILE)
        moves.append(pltpu.make_async_copy(grad.at[at, :], inside.at[at, :], sems.at[tile]))
        moves[-1].start()
    for move in moves:
        move.wait()


def conv_grad_kernel(inside, top, bottom, left, right, occ, weight, out, total, sem):
    load = pltpu.make_async_copy(inside, total, sem.at[0])
    load.start()
    rows, columns = border_sums(True, top, bottom, left, right, weight)
    live = occ[...].astype(f32)
    wide = jnp.concatenate([live, jnp.zeros((32, TILE - 32), f32)], axis=1)
    lines = jnp.concatenate([wide, jnp.zeros((TILE - 32, TILE), f32)], axis=0).T
    rows = [added * lines[:32, line : line + 1] for added, line in zip(rows, (0, 31))]
    columns = [added * live[:, col : col + 1] for added, col in zip(columns, (0, 31))]
    load.wait()
    add_border((rows, columns), total)
    out[...] = total[...].astype(bf16)


def output_kernel(dest, back, resid, out):
    for tile in range(TILES):
        rows = slice(tile * TILE, (tile + 1) * TILE)
        out[rows, :] = (resid[rows, :] + back[dest[tile] >> 3].astype(f32)).astype(bf16)


def exchange(low_edge, high_edge, axis):
    count = lax.axis_size(axis)
    forward = [(i, i + 1) for i in range(count - 1)]
    backward = [(target, source) for source, target in forward]
    return lax.ppermute(high_edge, axis, forward), lax.ppermute(low_edge, axis, backward)


def halo(first, final, low, high):
    top, bottom = exchange(first, final, "gx")
    low = jnp.concatenate([top[:1], low, bottom[:1]], axis=0)
    high = jnp.concatenate([top[31:], high, bottom[31:]], axis=0)
    left, right = exchange(low, high, "gy")
    return top, bottom, left, right


def conv_inside(block, weight):
    return call(
        conv_inside_kernel, far((PATCH, C), f32), [WHOLE] * 2, FAR,
        [pltpu.VMEM((PATCH, C), f32), pltpu.VMEM((3, PATCH + 64, C), bf16), pltpu.SemaphoreType.DMA((1,))],
        name="conv_inside",
        cost=pl.CostEstimate(flops=1200 * 10**6, bytes_accessed=4 * 10**6, transcendentals=0),
    )(block, weight)


def after(array, *others):
    return lax.optimization_barrier((array, *others))[0]


def swap(array, axis="gx"):
    return lax.all_to_all(array, axis, split_axis=0, concat_axis=0, tiled=True)


PLAIN = [pltpu.VMEM((C, PATCH), bf16), pltpu.VMEM((C, PATCH), bf16), pltpu.VMEM((PATCH, 1), f32)]
BLOCKS = pltpu.VMEM((C // LANES, KEYS, LANES + HEAD), bf16)
OPERAND = pltpu.VMEM((PAIR, LANES + HEAD, PATCH), bf16)


def attend(src, h_recv, w_qkv, w_qkv_t, w_proj):
    saved = [((PATCH, C), bf16), ((C, PATCH), bf16), ((C, KEYS), bf16), ((KEYS, C), bf16)]
    return pl.pallas_call(
        attend_kernel,
        out_shape=[
            far((PEERS, TILE, C), bf16), far((HEADS, KEYS, PATCH), bf16), far((C, PATCH), f32),
            far(*saved[0]), struct((TILES, TILE), f32), struct((TILES, TILE), f32),
            far(*saved[1]), far(*saved[2]), far(*saved[3]), struct((1,), jnp.int32),
        ],
        in_specs=[SMEM] + [WHOLE] * 4,
        out_specs=[FAR, FAR, FAR, FAR, WHOLE, WHOLE, FAR, FAR, FAR, SMEM],
        scratch_shapes=[pltpu.VMEM((PATCH, C), bf16), pltpu.VMEM((C, PATCH), f32)]
        + [pltpu.VMEM(*one) for one in saved]
        + [pltpu.VMEM((C, KEYS), bf16), BLOCKS, OPERAND, pltpu.VMEM((2, PAIR, KEYS, PATCH), bf16)]
        + PLAIN + [pltpu.SemaphoreType.DMA((13,)), pltpu.SemaphoreType.DMA((2, PAIR))],
        name="attend",
        cost_estimate=pl.CostEstimate(flops=12 * 10**9, bytes_accessed=32 * 10**6, transcendentals=14 * 10**6),
        compiler_params=pltpu.CompilerParams(vmem_limit_bytes=LIMIT * MIB),
    )(src, h_recv, w_qkv, w_qkv_t, w_proj)


def attend_grad(src, fits, g_recv, w_qkv_t, w_proj, probs, o_t, hidden, live, place, q_t, k_t, v_nat):
    return pl.pallas_call(
        attend_grad_kernel,
        out_shape=far((PEERS, TILE + W_ROWS, C), bf16),
        in_specs=[SMEM, SMEM, FAR, FAR, WHOLE, FAR, FAR, FAR, WHOLE, WHOLE, FAR, FAR, FAR],
        out_specs=FAR,
        scratch_shapes=[
            pltpu.VMEM((3 * C, C), bf16), pltpu.VMEM((KEYS, PATCH), bf16),
            pltpu.VMEM((C, PATCH), f32), pltpu.VMEM((PATCH, C), bf16), pltpu.VMEM((C, PATCH), bf16),
            pltpu.VMEM((C, KEYS), bf16), pltpu.VMEM((KEYS, C), bf16),
            pltpu.VMEM((PATCH, C), bf16), pltpu.VMEM((2, PAIR, KEYS, PATCH), bf16),
            pltpu.VMEM((C, PATCH), bf16), pltpu.VMEM((3 * C, PATCH), bf16), pltpu.VMEM((2 * C, KEYS), bf16),
            BLOCKS, OPERAND, pltpu.VMEM((PATCH, C), bf16), pltpu.VMEM((PEERS, W_ROWS, C), bf16),
        ] + PLAIN + [pltpu.SemaphoreType.DMA((TILES + 7,)), pltpu.SemaphoreType.DMA((2, PAIR))],
        name="attend_grad",
        cost_estimate=pl.CostEstimate(flops=24 * 10**9, bytes_accessed=32 * 10**6, transcendentals=0),
        compiler_params=pltpu.CompilerParams(vmem_limit_bytes=LIMIT * MIB),
    )(
        src, fits, pin(g_recv), pin(w_qkv_t), w_proj, pin(probs), pin(o_t), pin(hidden), live, place,
        pin(q_t), pin(k_t), pin(v_nat),
    )


def local(features, occupied, conv_weight, norm_gain, w_qkv, w_proj, tile_dest, cotangent):
    size_x, size_y, feat_width = features.shape
    cells = size_x * size_y
    dest = tile_dest.reshape(TILES)
    occ = occupied.reshape(TILES, TILE)
    gain = norm_gain.reshape(1, C)
    feat = features.reshape(cells, C)
    cot = cotangent.reshape(cells, C)
    rows_f32 = struct((cells, C), f32)
    rows_bf16 = struct((cells, C), bf16)
    buckets = struct((PEERS, TILE, C), bf16)
    total = pltpu.VMEM((cells, C), f32)

    border = struct((32, C), bf16)
    masked, *edges = call(
        mask_kernel, [rows_bf16] + [border] * 4, [FAR] * 2, [WHOLE] * 5,
        [pltpu.VMEM((cells, C), bf16), pltpu.VMEM((32, 32), jnp.int32), pltpu.SemaphoreType.DMA((5,))],
        name="mask",
    )(pin(feat), pin(occupied))
    edges = halo(*edges)
    conv = conv_inside(masked, conv_weight)
    resid, h_send = call(
        forward_kernel, [far((cells, C), f32), far((PEERS, TILE + META, C), bf16)],
        [SMEM, FAR] + [WHOLE] * 8, [FAR, FAR],
        [
            total, total, pltpu.VMEM((cells, C), bf16), pltpu.VMEM((PEERS, META, C), bf16),
            pltpu.SemaphoreType.DMA((2 + 2 * TILES,)),
        ],
        name="forward",
    )(dest, pin(conv), feat, *edges, occ, conv_weight, gain)
    h_recv = swap(h_send)
    flags = h_recv[:, TILE + 1, 0].astype(f32)
    order = jnp.arange(TILES, dtype=f32)
    peers = jnp.arange(PEERS, dtype=jnp.int32)
    ranks = jnp.sum(jnp.where(peers[None, :] < peers[:, None], flags[None, :], 0.0), axis=1)
    chosen = (ranks[None, :] == order[:, None]) & (flags[None, :] > 0.5)
    src = jnp.sum(jnp.where(chosen, peers[None, :], 0), axis=1)

    g_send = call(
        pack_kernel, far((PEERS, TILE, C), bf16), [SMEM, WHOLE], FAR, [pltpu.SemaphoreType.DMA((TILES,))], name="pack"
    )(dest, cot)
    g_send, h_recv = lax.optimization_barrier((g_send, h_recv))
    g_recv = swap(g_send)
    w_qkv_t = w_qkv.T
    att_send, probs, o_t, hidden, live, place, q_t, k_t, v_aug, fits = attend(src, h_recv, w_qkv, w_qkv_t, w_proj)
    att_back = swap(att_send)
    dh_send = attend_grad(src, fits, g_recv, w_qkv_t, w_proj, probs, o_t, hidden, live, place, q_t, k_t, v_aug)
    block_output = call(
        output_kernel, rows_bf16, [SMEM, WHOLE, WHOLE], WHOLE, name="output"
    )(dest, after(att_back, dh_send), resid)
    dh_send = after(dh_send, block_output)
    dh_back = swap(dh_send)
    w_send = call(
        fold_kernel, far((COLUMN, 16, 3 * C), f32), [WHOLE], WHOLE, name="fold"
    )(dh_back)
    w_recv = swap(w_send, "gy")
    grad, *edges = call(
        residual_grad_kernel,
        [far((cells, C), f32), border, border, border, border],
        [SMEM, WHOLE, FAR, FAR, WHOLE, WHOLE], [FAR] + [WHOLE] * 4,
        [
            total, pltpu.VMEM((cells, C), bf16), pltpu.VMEM((cells, C), bf16),
            pltpu.SemaphoreType.DMA((2 * TILES,)),
        ],
        name="residual_grad",
    )(dest, dh_back, pin(resid), pin(cot), occ, gain)
    grad_edges = halo(*edges)
    inside = call(
        inside_grad_kernel, far((cells, C), f32), [FAR, WHOLE, WHOLE], FAR,
        [total, total, pltpu.VMEM((3, PATCH + 64, C), bf16), pltpu.SemaphoreType.DMA((TILES,))],
        name="inside_grad",
        cost=pl.CostEstimate(flops=1200 * 10**6, bytes_accessed=4 * 10**6, transcendentals=0),
    )(pin(grad), occ, conv_weight)
    w_recv = after(w_recv, grad_edges[0])
    w_sum = (jnp.sum(w_recv, axis=0) / math.sqrt(131072)).astype(bf16)
    d_features = call(
        conv_grad_kernel, rows_bf16, [FAR] + [WHOLE] * 6, WHOLE,
        [total, pltpu.SemaphoreType.DMA((1,))], name="conv_grad",
    )(pin(inside), *grad_edges, occupied, conv_weight)
    w_grad = swap(jnp.broadcast_to(w_sum[None], (PEERS, 16, 3 * C))).reshape(C, 3 * C).astype(f32)
    shape = (size_x, size_y, feat_width)
    return (block_output.reshape(shape), d_features.reshape(shape), w_grad)


def solution(mesh):
    in_specs = (
        P("gx", "gy", None),
        P("gx", "gy"),
        P(),
        P(),
        P(),
        P(),
        P("gx", "gy"),
        P("gx", "gy", None),
    )
    out_specs = (P("gx", "gy", None), P("gx", "gy", None), P())
    return jax.shard_map(local, mesh=mesh, in_specs=in_specs, out_specs=out_specs, check_vma=False)
```
